128 devices in a mesh: row: 16 (over y_lo, x, core), col: 8 (over y_hi, z).
Axes of the slice: x: 4, y: 4 (y_hi: 2, y_lo: 2; y = y_hi * 2 + y_lo), z: 4, core: 2. Of those that a mesh axis runs over, the one named last changes fastest.
Arguments:
- gradient: float32 [5120, 9216], P('row', 'col'), may hold values from -0.015625 to 0.015625
- momentum: float32 [5120, 9216], P('row', 'col'), may hold values from -0.015625 to 0.015625
Outputs:
- new_momentum: float32 [5120, 9216], P('row', 'col')
- update: float32 [5120, 9216], P('row', 'col')
The draws below stay inside these ranges and needn't reach their ends.
All inputs are finite; a program needn't handle non-finite values.
Results may differ from the reference program's by a relative error of at most 0.013.
Values may be sent and summed in bfloat16 or wider, within the bound.
A program may use at most 128 MiB of HBM per device.

```python
import math
import jax
import jax.numpy as jnp
from jax import lax

FEATURES = 5120
HIDDEN_SIZE = 9216
N_COL = 8


def level_of(own_key, dims, shards, least, largest):
    factor_of, own = 1.0, jax.random.fold_in(own_key, 6)
    for dim, parts in shards:
        draws = jnp.exp(jax.random.uniform(jax.random.fold_in(own, dim), (parts,), jnp.float32, least / len(shards), largest / len(shards)))
        factor_of = factor_of * jnp.repeat(draws, dims[dim] // parts).reshape([-1 if axis == dim else 1 for axis in range(len(dims))])
    return factor_of


def gaussian(own_key, dims, spread, most, pieces=(), kind=jnp.bfloat16):
    drawn = jax.random.normal(own_key, dims, jnp.float32) * spread
    if len(pieces) > 0:
        drawn = level_of(own_key, dims, pieces, -0.22, 0.18) * drawn
    return jnp.clip(drawn, min=-most, max=most).astype(kind)


def setup_inputs(seed: int = 0) -> dict:
    keys = jax.random.split(jax.random.key(seed), 3)
    return {
        "gradient": gaussian(keys[0], (FEATURES, HIDDEN_SIZE), (18 * HIDDEN_SIZE) ** -0.5, 0.015625, ((0, 16), (1, 8)), jnp.float32),
        "momentum": gaussian(keys[1], (FEATURES, HIDDEN_SIZE), (18 * HIDDEN_SIZE) ** -0.5, 0.015625, ((0, 16), (1, 8)), jnp.float32),
    }


MOMENTUM_RATE = 0.95
COEF_A = 3.4445
COEF_B = -4.775
COEF_C = 2.0315

def reference(gradient, momentum):
    new_momentum = MOMENTUM_RATE * momentum + gradient
    nesterov = gradient + MOMENTUM_RATE * new_momentum
    lowered = nesterov.astype(jnp.bfloat16)
    block_width = HIDDEN_SIZE // N_COL
    gram = jnp.zeros((FEATURES, FEATURES), jnp.float32)
    for column_block in range(N_COL):
        block_part = lowered[:, column_block * block_width:(column_block + 1) * block_width]
        term = lax.dot_general(block_part, block_part, (((1,), (1,)), ((), ())), preferred_element_type=jnp.float32)
        term = lax.optimization_barrier(term.astype(jnp.bfloat16)).astype(jnp.float32)
        gram = gram + term
    gram_half = gram.astype(jnp.bfloat16)
    square = jnp.dot(gram_half, gram_half, preferred_element_type=jnp.float32)
    mixing = (COEF_B * gram + COEF_C * square).astype(jnp.bfloat16)
    product = jnp.dot(mixing, lowered, preferred_element_type=jnp.float32)
    update = math.sqrt(HIDDEN_SIZE) * (COEF_A * nesterov + product)
    return (new_momentum, update)
```

```python
import math

import jax
import jax.numpy as jnp
from jax import lax
from jax.experimental import pallas as pl
from jax.experimental.pallas import tpu as pltpu
from jax.sharding import PartitionSpec as P

HIDDEN_SIZE = 9216
MOMENTUM_RATE = 0.95
COEF_A = 3.4445
COEF_B = -4.775
COEF_C = 2.0315
SCALE = math.sqrt(HIDDEN_SIZE)

MESH = pl.DeviceIdType.MESH
ROWS = 320
COLS = 1152
HALF = ROWS // 2
CHIP = 2 * ROWS
PIECE = ROWS // 4
PLACES = {(0, 0): 0, (-1, 0): 1, (1, 0): 2, (2, 0): 3, (0, 1): 4, (-1, 1): 5, (1, 1): 6, (2, 1): 7}


class Gather:
    def __init__(self, slot, plus, minus, pair, send, recv, over_pair):
        self.slot, self.plus, self.minus, self.pair = slot, plus, minus, pair
        self.send, self.recv, self.over_pair, self.started = send, recv, over_pair, []

    def _copy(self, dr, dp, h, to):
        device, ring, other = {"plus": (self.plus, -1, 0), "minus": (self.minus, 1, 0), "pair": (self.pair, 0, 1)}[to]
        there = dr + ring
        there = 2 if there == -2 else there
        place = PLACES[(there, (dp + other) % 2)] * 2 + h
        ref = self.slot(dr, dp, h)
        copy = pltpu.make_async_remote_copy(
            src_ref=ref,
            dst_ref=ref,
            send_sem=self.send.at[len(self.started)],
            recv_sem=self.recv.at[place],
            device_id=device,
            device_id_type=MESH,
        )
        copy.start()
        self.started.append(copy)

    def begin(self, h):
        for to in ("plus", "minus", "pair"):
            self._copy(0, 0, h, to)

    def arrive(self, dr, dp, h):
        ref = self.slot(dr, dp, h)
        place = PLACES[(dr, dp)] * 2 + h
        pltpu.make_async_remote_copy(
            src_ref=ref,
            dst_ref=ref,
            send_sem=self.send.at[0],
            recv_sem=self.recv.at[place],
            device_id=self.pair,
            device_id_type=MESH,
        ).wait_recv()
        if (dr, dp) == (0, 1):
            self._copy(dr, dp, h, "plus")
            self._copy(dr, dp, h, "minus")
        elif (dr, dp, h) == (-1, 0, 0) or (dr, dp, h, self.over_pair) == (-1, 1, 0, False):
            self._copy(dr, dp, h, "plus")
        elif (dr, dp, h) == (1, 0, 1) or (dr, dp, h, self.over_pair) == (1, 1, 1, False):
            self._copy(dr, dp, h, "minus")
        elif (dr, dp) == (2, 0) and self.over_pair:
            self._copy(dr, dp, h, "pair")

    def finish(self):
        for copy in self.started:
            copy.wait_send()


def kernel(
    g_ref, m_ref, nm_ref, up_ref,
    xs, xi, xt, ps, r1, keep, s_send, s_recv, gf, rt, ls, ms, mt, zs, zr,
    x_send, x_recv, xc_send, xc_recv, r1_send, r1_recv, r2_send, r2_recv,
    rt_send, rt_recv, l_send, l_recv, lc_send, lc_recv, m_send, m_recv, z_send, z_recv,
):
    row, col = lax.axis_index("row"), lax.axis_index("col")
    c, x, yl = row % 2, (row // 2) % 4, row // 8
    z, yh = col % 4, col // 4

    def device(x_, yl_, c_, yh_, z_):
        return ((yl_ * 4 + x_) * 2 + c_, yh_ * 4 + z_)

    core = device(x, yl, 1 - c, yh, z)
    xp, xm = device((x + 1) % 4, yl, c, yh, z), device((x + 3) % 4, yl, c, yh, z)
    zp, zm = device(x, yl, c, yh, (z + 1) % 4), device(x, yl, c, yh, (z + 3) % 4)
    z2 = device(x, yl, c, yh, (z + 2) % 4)
    yp, yq = device(x, 1 - yl, c, yh, z), device(x, yl, c, 1 - yh, z)
    barrier = pltpu.get_barrier_semaphore()
    partners = (core, xp, xm, zp, zm, z2, yp, yq)
    for partner in partners:
        pl.semaphore_signal(barrier, inc=1, device_id=partner, device_id_type=MESH)

    def remote(src, dst, send, recv, to):
        return pltpu.make_async_remote_copy(
            src_ref=src, dst_ref=dst, send_sem=send, recv_sem=recv, device_id=to, device_id_type=MESH
        )

    def chip_at(dr, dp):
        return ((yl + dp) % 2) * 4 + (x + dr + 4) % 4

    def nesterov_of(rows):
        new = MOMENTUM_RATE * m_ref[rows, :] + g_ref[rows, :]
        return new, g_ref[rows, :] + MOMENTUM_RATE * new

    own = chip_at(0, 0)

    gx = Gather(lambda dr, dp, h: xs.at[chip_at(dr, dp), pl.ds(h * HALF, HALF)], xp, xm, yp, x_send, x_recv, True)
    cores = []
    for h in range(2):
        rows = pl.ds(h * HALF, HALF)
        new, nest = nesterov_of(rows)
        nm_ref[rows, :] = new
        low = nest.astype(jnp.bfloat16)
        xs[own, rows, :] = low
        mine = pl.ds(pl.multiple_of(c * ROWS + h * HALF, 32), HALF)
        xi[mine, :] = low
        if h == 0:
            pl.semaphore_wait(barrier, len(partners))
        gx.begin(h)
        copy = remote(xi.at[mine], xi.at[mine], xc_send.at[h], xc_recv.at[h], core)
        copy.start()
        cores.append(copy)
    for h in range(2):
        theirs = pl.ds(pl.multiple_of((1 - c) * ROWS + h * HALF, 32), HALF)
        remote(xi.at[theirs], xi.at[theirs], xc_send.at[h], xc_recv.at[h], core).wait_recv()
    for k in range(COLS // 128):
        xt[k * 128 : (k + 1) * 128, :] = xi[:, k * 128 : (k + 1) * 128].T

    def piece_copy(j, src_z, dst_z):
        return remote(
            ps.at[j, dst_z], r1.at[j, src_z], r1_send.at[j, dst_z], r1_recv.at[j, src_z], device(x, yl, c, yh, dst_z)
        )

    def gram(dr, dp, h):
        j = chip_at(dr, dp)
        part = jnp.dot(xs[j, h * HALF : (h + 1) * HALF, :], xt[...], preferred_element_type=jnp.float32)
        ps[j, 2 * h : 2 * h + 2] = part.astype(jnp.bfloat16).reshape(2, PIECE, CHIP)
        for piece in (2 * h, 2 * h + 1):

            @pl.when(piece != z)
            def _(piece=piece):
                piece_copy(j, z, piece).start()

    def pair_copy(xj):
        return remote(s_send.at[xj], s_recv.at[xj], r2_send.at[xj], r2_recv.at[xj], yq)

    def reduce(dr, dp):
        j = chip_at(dr, dp)
        total = ps[j, z].astype(jnp.float32)
        for dz in (1, 3, 2):
            src_z = (z + dz) % 4
            piece_copy(j, src_z, src_z).wait_recv()
            total = total + r1[j, src_z].astype(jnp.float32)
        xj = (x + dr + 4) % 4

        @pl.when((yl + dp) % 2 == yh)
        def _():
            keep[xj] = total

        @pl.when((yl + dp) % 2 != yh)
        def _():
            s_send[xj] = total.astype(jnp.bfloat16)
            pair_copy(xj).start()

    def step(places, h):
        for dr, dp in places:
            gx.arrive(dr, dp, h)
        for dr, dp in places:
            gram(dr, dp, h)

    gram(0, 0, 0)
    gram(0, 0, 1)
    near, far = ((-1, 0), (1, 0), (0, 1)), ((-1, 1), (1, 1), (2, 1))
    step(near, 0)
    reduce(0, 0)
    step(near, 1)
    step(((2, 0),), 0)
    step(((2, 0),), 1)
    for place in near:
        reduce(*place)
    step(far, 0)
    reduce(2, 0)
    step(far, 1)
    for place in far:
        reduce(*place)

    gr = Gather(lambda dr, dp, h: rt.at[chip_at(dr, dp), pl.ds(h * 2, 2)], xp, xm, yp, rt_send, rt_recv, True)

    def col_slot(ref, lane):
        def slot(dr, dp, h):
            first = ((yh + dp) % 2) * 4 + h * 2
            at = (z + dr + 4) % 4
            return ref.at[pl.ds(first, 2), lane, at] if lane is not None else ref.at[pl.ds(first, 2), at]

        return slot

    mine_of, theirs_of = col_slot(ls, c), col_slot(ls, 1 - c)
    gl = Gather(mine_of, zp, zm, yq, l_send, l_recv, False)
    lanes = []

    def to_core(dr, dp, h):
        place = PLACES[(dr, dp)] * 2 + h
        copy = remote(mine_of(dr, dp, h), mine_of(dr, dp, h), lc_send.at[place], lc_recv.at[place], core)
        copy.start()
        lanes.append(copy)

    def from_core(dr, dp, h):
        place = PLACES[(dr, dp)] * 2 + h
        ref = theirs_of(dr, dp, h)
        remote(ref, ref, lc_send.at[place], lc_recv.at[place], core).wait_recv()

    for h in range(2):
        for xj in (2 * h, 2 * h + 1):
            pair_copy(xj).wait_recv()
            total = keep[xj] + s_recv[xj].astype(jnp.float32)
            gf[xj] = total
            low = total.astype(jnp.bfloat16)
            rt[own, xj] = low
            ls[yh * 4 + xj, c, z] = low
        gl.begin(h)
        gr.begin(h)
        to_core(0, 0, h)

    def arrive_l(dr, dp, h):
        gl.arrive(dr, dp, h)
        to_core(dr, dp, h)

    for h in range(2):
        for place in near:
            arrive_l(*place, h)
            gr.arrive(*place, h)
    for h in range(2):
        arrive_l(2, 0, h)
        gr.arrive(2, 0, h)
    for h in range(2):
        for place in far[:2]:
            arrive_l(*place, h)
            gr.arrive(*place, h)
    for h in range(2):
        gr.arrive(2, 1, h)

    def square(j):
        left = rt[j].reshape(ROWS, CHIP)
        right = ls[j].reshape(CHIP, CHIP)
        return jnp.dot(left, right, preferred_element_type=jnp.float32)

    for dr in (0, -1, 1, 2):
        for h in range(2):
            from_core(dr, 0, h)
    total = square(yh * 4)
    for k in range(1, 4):
        total = total + square(yh * 4 + k)
    for h in range(2):
        arrive_l(2, 1, h)
    for dr in (0, -1, 1, 2):
        for h in range(2):
            from_core(dr, 1, h)
    for k in range(4):
        total = total + square((1 - yh) * 4 + k)
    mixing = (COEF_B * gf[...].reshape(ROWS, CHIP) + COEF_C * total).astype(jnp.bfloat16)
    mixing = mixing.reshape(4, PIECE, CHIP)
    for xj in range(4):
        ms[yh * 4 + xj, z] = mixing[xj]
    gm = Gather(col_slot(ms, None), zp, zm, yq, m_send, m_recv, True)
    gm.begin(0)
    gm.begin(1)

    def product(dr, dp, first=False):
        side, at = ((yh + dp) % 2) * 4, (z + dr + 4) % 4
        mt[...] = ms[pl.ds(side, 4), at].reshape(ROWS, CHIP).T
        rows = pl.ds(pl.multiple_of(at * PIECE, 16), PIECE)
        for n in range(3):
            cols = pl.ds(n * 384, 384)
            right = xs[pl.ds(side, 4), rows, cols].reshape(ROWS, 384)
            part = jnp.dot(mt[...], right, preferred_element_type=jnp.float32)
            zs[:, cols] = part if first else zs[:, cols] + part

    product(0, 0, True)
    for h in range(2):
        for place in near:
            gm.arrive(*place, h)
    for h in range(2):
        gm.arrive(2, 0, h)
    for place in near:
        product(*place)
    product(2, 0)
    for place in far:
        for h in range(2):
            gm.arrive(*place, h)
        product(*place)
    theirs = pl.ds(pl.multiple_of((1 - c) * ROWS, 32), ROWS)
    mine = pl.ds(pl.multiple_of(c * ROWS, 32), ROWS)
    last = remote(zs.at[theirs], zr, z_send, z_recv, core)
    last.start()
    last.wait_recv()
    _, nest = nesterov_of(slice(None))
    up_ref[...] = SCALE * (COEF_A * nest + (zs[mine, :] + zr[...]))

    for copy in cores + lanes + [last]:
        copy.wait_send()
    for gather in (gx, gr, gl, gm):
        gather.finish()
    for j in range(8):
        for dz in (1, 2, 3):
            piece_copy(j, z, (z + dz) % 4).wait_send()
    for xj in range(4):
        pair_copy(xj).wait_send()


def local(gradient, momentum):
    shape = jax.ShapeDtypeStruct((ROWS, COLS), jnp.float32)
    vmem = pl.BlockSpec(memory_space=pltpu.VMEM)
    half, full = jnp.bfloat16, jnp.float32
    dma = pltpu.SemaphoreType.DMA
    return pl.pallas_call(
        kernel,
        out_shape=(shape, shape),
        in_specs=[vmem, vmem],
        out_specs=(vmem, vmem),
        scratch_shapes=[
            pltpu.VMEM((8, ROWS, COLS), half),
            pltpu.VMEM((CHIP, COLS), half),
            pltpu.VMEM((COLS, CHIP), half),
            pltpu.VMEM((8, 4, PIECE, CHIP), half),
            pltpu.VMEM((8, 4, PIECE, CHIP), half),
            pltpu.VMEM((4, PIECE, CHIP), full),
            pltpu.VMEM((4, PIECE, CHIP), half),
            pltpu.VMEM((4, PIECE, CHIP), half),
            pltpu.VMEM((4, PIECE, CHIP), full),
            pltpu.VMEM((8, 4, PIECE, CHIP), half),
            pltpu.VMEM((8, 2, 4, PIECE, CHIP), half),
            pltpu.VMEM((8, 4, PIECE, CHIP), half),
            pltpu.VMEM((CHIP, ROWS), half),
            pltpu.VMEM((CHIP, COLS), full),
            pltpu.VMEM((ROWS, COLS), full),
            dma((14,)), dma((16,)), dma((2,)), dma((2,)),
            dma((8, 4)), dma((8, 4)), dma((4,)), dma((4,)),
            dma((14,)), dma((16,)), dma((14,)), dma((16,)),
            dma((16,)), dma((16,)), dma((14,)), dma((16,)),
            dma(()), dma(()),
        ],
        name="muon",
        compiler_params=pltpu.CompilerParams(
            collective_id=0, has_side_effects=True, vmem_limit_bytes=60 * 2**20
        ),
    )(gradient, momentum)


def solution(mesh):
    specs = (P("row", "col"), P("row", "col"))
    return jax.shard_map(local, mesh=mesh, in_specs=specs, out_specs=specs, check_vma=False)
```

```python
import math

import jax
import jax.numpy as jnp
from jax import lax
from jax.experimental import pallas as pl
from jax.experimental.pallas import tpu as pltpu
from jax.sharding import PartitionSpec as P

HIDDEN_SIZE = 9216
MOMENTUM_RATE = 0.95
COEF_A = 3.4445
COEF_B = -4.775
COEF_C = 2.0315
SCALE = math.sqrt(HIDDEN_SIZE)

MESH = pl.DeviceIdType.MESH
ROWS = 320
COLS = 1152
HALF = ROWS // 2
CHIP = 2 * ROWS
PIECE = ROWS // 4
MAIN, EXTRA = 32, 16
PLACES = {(0, 0): 0, (-1, 0): 1, (1, 0): 2, (2, 0): 3, (0, 1): 4, (-1, 1): 5, (1, 1): 6, (2, 1): 7}


def spans(h):
    main = [(MAIN * piece, MAIN, piece, MAIN * h) for piece in range(4)]
    return main + [(4 * MAIN + EXTRA * e, EXTRA, 2 * h + e, 2 * MAIN) for e in range(2)]


class Gather:
    def __init__(self, slot, plus, minus, pair, send, recv, over_pair):
        self.slot, self.plus, self.minus, self.pair = slot, plus, minus, pair
        self.send, self.recv, self.over_pair, self.started = send, recv, over_pair, []

    def _copy(self, dr, dp, h, to):
        device, ring, other = {"plus": (self.plus, -1, 0), "minus": (self.minus, 1, 0), "pair": (self.pair, 0, 1)}[to]
        there = dr + ring
        there = 2 if there == -2 else there
        place = PLACES[(there, (dp + other) % 2)] * 2 + h
        ref = self.slot(dr, dp, h)
        copy = pltpu.make_async_remote_copy(
            src_ref=ref,
            dst_ref=ref,
            send_sem=self.send.at[len(self.started)],
            recv_sem=self.recv.at[place],
            device_id=device,
            device_id_type=MESH,
        )
        copy.start()
        self.started.append(copy)

    def begin(self, h):
        for to in ("plus", "minus", "pair"):
            self._copy(0, 0, h, to)

    def arrive(self, dr, dp, h):
        ref = self.slot(dr, dp, h)
        place = PLACES[(dr, dp)] * 2 + h
        pltpu.make_async_remote_copy(
            src_ref=ref,
            dst_ref=ref,
            send_sem=self.send.at[0],
            recv_sem=self.recv.at[place],
            device_id=self.pair,
            device_id_type=MESH,
        ).wait_recv()
        if (dr, dp) == (0, 1):
            self._copy(dr, dp, h, "plus")
            self._copy(dr, dp, h, "minus")
        elif (dr, dp, h) == (-1, 0, 0) or (dr, dp, h, self.over_pair) == (-1, 1, 0, False):
            self._copy(dr, dp, h, "plus")
        elif (dr, dp, h) == (1, 0, 1) or (dr, dp, h, self.over_pair) == (1, 1, 1, False):
            self._copy(dr, dp, h, "minus")
        elif (dr, dp) == (2, 0) and self.over_pair:
            self._copy(dr, dp, h, "pair")

    def finish(self):
        for copy in self.started:
            copy.wait_send()


def kernel(
    g_hbm, m_hbm, out_ref,
    g_ref, m_ref, xs, xi, xt, ps, r1, keep, s_send, s_recv, gf, rt, ls, ms, mt, zs, zr,
    in_sem, x_send, x_recv, xc_send, xc_recv, r1_send, r1_recv, r2_send, r2_recv,
    rt_send, rt_recv, l_send, l_recv, lc_send, lc_recv, m_send, m_recv, z_send, z_recv,
):
    row, col = lax.axis_index("row"), lax.axis_index("col")
    c, x, yl = row % 2, (row // 2) % 4, row // 8
    z, yh = col % 4, col // 4

    def device(x_, yl_, c_, yh_, z_):
        return ((yl_ * 4 + x_) * 2 + c_, yh_ * 4 + z_)

    core = device(x, yl, 1 - c, yh, z)
    xp, xm = device((x + 1) % 4, yl, c, yh, z), device((x + 3) % 4, yl, c, yh, z)
    zp, zm = device(x, yl, c, yh, (z + 1) % 4), device(x, yl, c, yh, (z + 3) % 4)
    z2 = device(x, yl, c, yh, (z + 2) % 4)
    yp, yq = device(x, 1 - yl, c, yh, z), device(x, yl, c, 1 - yh, z)
    barrier = pltpu.get_barrier_semaphore()
    partners = (core, xp, xm, zp, zm, z2, yp, yq)
    for partner in partners:
        pl.semaphore_signal(barrier, inc=1, device_id=partner, device_id_type=MESH)
    loads = []
    for h in range(2):
        rows = pl.ds(h * HALF, HALF)
        for k, (hbm, ref) in enumerate(((g_hbm, g_ref), (m_hbm, m_ref))):
            load = pltpu.make_async_copy(hbm.at[rows], ref.at[rows], in_sem.at[2 * h + k])
            load.start()
            loads.append(load)

    def remote(src, dst, send, recv, to):
        return pltpu.make_async_remote_copy(
            src_ref=src, dst_ref=dst, send_sem=send, recv_sem=recv, device_id=to, device_id_type=MESH
        )

    def chip_at(dr, dp):
        return ((yl + dp) % 2) * 4 + (x + dr + 4) % 4

    own = chip_at(0, 0)

    gx = Gather(lambda dr, dp, h: xs.at[chip_at(dr, dp), pl.ds(h * HALF, HALF)], xp, xm, yp, x_send, x_recv, True)
    mine = pl.ds(pl.multiple_of(c * ROWS, 32), ROWS)
    theirs = pl.ds(pl.multiple_of((1 - c) * ROWS, 32), ROWS)
    for h in range(2):
        rows = pl.ds(h * HALF, HALF)
        loads[2 * h].wait()
        loads[2 * h + 1].wait()
        new = MOMENTUM_RATE * m_ref[rows, :] + g_ref[rows, :]
        low = (g_ref[rows, :] + MOMENTUM_RATE * new).astype(jnp.bfloat16)
        xs[own, rows, :] = low
        if h == 0:
            pl.semaphore_wait(barrier, len(partners))
        gx.begin(h)
        for first, count, piece, at in spans(h):
            xi[pl.ds(pl.multiple_of(c * ROWS + piece * PIECE + at, 16), count), :] = low[first : first + count]
    swap = remote(xi.at[mine], xi.at[mine], xc_send, xc_recv, core)
    swap.start()
    remote(xi.at[theirs], xi.at[theirs], xc_send, xc_recv, core).wait_recv()
    for k in range(COLS // 128):
        xt[k * 128 : (k + 1) * 128, :] = xi[:, k * 128 : (k + 1) * 128].T

    def piece_copy(j, src_z, dst_z, kind):
        if kind < 2:
            src = ps.at[j, kind, pl.ds(pl.multiple_of(dst_z * MAIN, MAIN), MAIN)]
        else:
            src = ps.at[j, dst_z // 2, pl.ds(pl.multiple_of(4 * MAIN + dst_z % 2 * EXTRA, EXTRA), EXTRA)]
        dst = r1.at[j, src_z, pl.ds(kind * MAIN, MAIN if kind < 2 else EXTRA)]
        to = device(x, yl, c, yh, dst_z)
        return remote(src, dst, r1_send.at[j, dst_z, kind], r1_recv.at[j, src_z, kind], to)

    def gram(dr, dp, h):
        j = chip_at(dr, dp)
        part = jnp.dot(xs[j, h * HALF : (h + 1) * HALF, :], xt[...], preferred_element_type=jnp.float32)
        ps[j, h] = part.astype(jnp.bfloat16)
        for dz in (2, 1, 3):
            piece_copy(j, z, (z + dz) % 4, h).start()
        for piece in (2 * h, 2 * h + 1):

            @pl.when(piece != z)
            def _(piece=piece):
                piece_copy(j, z, piece, 2).start()

    def pair_copy(xj):
        return remote(s_send.at[xj], s_recv.at[xj], r2_send.at[xj], r2_recv.at[xj], yq)

    def reduce(dr, dp):
        j = chip_at(dr, dp)
        own_rows = [ps[j, h, pl.ds(pl.multiple_of(z * MAIN, MAIN), MAIN)] for h in range(2)]
        own_rows.append(ps[j, z // 2, pl.ds(pl.multiple_of(4 * MAIN + z % 2 * EXTRA, EXTRA), EXTRA)])
        total = jnp.concatenate(own_rows, axis=0).astype(jnp.float32)
        for dz in (1, 3, 2):
            src_z = (z + dz) % 4
            for kind in range(3):
                piece_copy(j, src_z, src_z, kind).wait_recv()
            total = total + r1[j, src_z].astype(jnp.float32)
        xj = (x + dr + 4) % 4

        @pl.when((yl + dp) % 2 == yh)
        def _():
            keep[xj] = total

        @pl.when((yl + dp) % 2 != yh)
        def _():
            s_send[xj] = total.astype(jnp.bfloat16)
            pair_copy(xj).start()

    def step(places, h):
        for dr, dp in places:
            gx.arrive(dr, dp, h)
        for dr, dp in places:
            gram(dr, dp, h)

    gram(0, 0, 0)
    gram(0, 0, 1)
    near, far = ((-1, 0), (1, 0), (0, 1)), ((-1, 1), (1, 1), (2, 1))
    step(near, 0)
    reduce(0, 0)
    step(near, 1)
    step(((2, 0),), 0)
    step(((2, 0),), 1)
    for place in near:
        reduce(*place)
    step(far, 0)
    reduce(2, 0)
    step(far, 1)
    for place in far:
        reduce(*place)

    gr = Gather(lambda dr, dp, h: rt.at[chip_at(dr, dp), pl.ds(h * 2, 2)], xp, xm, yp, rt_send, rt_recv, True)

    def col_slot(ref, lane):
        def slot(dr, dp, h):
            first = ((yh + dp) % 2) * 4 + h * 2
            at = (z + dr + 4) % 4
            return ref.at[pl.ds(first, 2), lane, at] if lane is not None else ref.at[pl.ds(first, 2), at]

        return slot

    mine_of, theirs_of = col_slot(ls, c), col_slot(ls, 1 - c)
    gl = Gather(mine_of, zp, zm, yq, l_send, l_recv, False)
    lanes = []

    def to_core(dr, dp, h):
        place = PLACES[(dr, dp)] * 2 + h
        copy = remote(mine_of(dr, dp, h), mine_of(dr, dp, h), lc_send.at[place], lc_recv.at[place], core)
        copy.start()
        lanes.append(copy)

    def from_core(dr, dp, h):
        place = PLACES[(dr, dp)] * 2 + h
        ref = theirs_of(dr, dp, h)
        remote(ref, ref, lc_send.at[place], lc_recv.at[place], core).wait_recv()

    for h in range(2):
        for xj in (2 * h, 2 * h + 1):
            pair_copy(xj).wait_recv()
            total = keep[xj] + s_recv[xj].astype(jnp.float32)
            gf[xj] = total
            low = total.astype(jnp.bfloat16)
            rt[own, xj] = low
            ls[yh * 4 + xj, c, z] = low
        gl.begin(h)
        to_core(0, 0, h)
    for h in range(2):
        gr.begin(h)

    def arrive_l(dr, dp, h):
        gl.arrive(dr, dp, h)
        to_core(dr, dp, h)

    for h in range(2):
        for arrive in (arrive_l, gr.arrive):
            arrive(-1, 0, h)
            arrive(1, 0, h)
        arrive_l(0, 1, h)
    for h in range(2):
        gr.arrive(2, 0, h)
        gr.arrive(0, 1, h)
        arrive_l(2, 0, h)
    for h in range(2):
        for arrive in (arrive_l, gr.arrive):
            arrive(-1, 1, h)
            arrive(1, 1, h)
    for h in range(2):
        gr.arrive(2, 1, h)

    def square(j):
        left = rt[j].reshape(ROWS, CHIP)
        right = ls[j].reshape(CHIP, CHIP)
        return jnp.dot(left, right, preferred_element_type=jnp.float32)

    for dr in (0, -1, 1, 2):
        for h in range(2):
            from_core(dr, 0, h)
    total = square(yh * 4)
    for k in range(1, 4):
        total = total + square(yh * 4 + k)
    for h in range(2):
        arrive_l(2, 1, h)
    for dr in (0, -1, 1, 2):
        for h in range(2):
            from_core(dr, 1, h)
    for k in range(4):
        total = total + square((1 - yh) * 4 + k)
    mixing = (COEF_B * gf[...].reshape(ROWS, CHIP) + COEF_C * total).astype(jnp.bfloat16)
    mixing = mixing.reshape(4, PIECE, CHIP)
    for xj in range(4):
        ms[yh * 4 + xj, z] = mixing[xj]
    gm = Gather(col_slot(ms, None), zp, zm, yq, m_send, m_recv, True)
    gm.begin(0)
    gm.begin(1)

    def rows_of(side, at, cols):
        blocks = []
        for k in range(4):
            for h in range(2):
                blocks.append(xs[side + k, pl.ds(pl.multiple_of(h * HALF + at * MAIN, MAIN), MAIN), cols])
            extra = at // 2 * HALF + 4 * MAIN + at % 2 * EXTRA
            blocks.append(xs[side + k, pl.ds(pl.multiple_of(extra, EXTRA), EXTRA), cols])
        return jnp.concatenate(blocks, axis=0)

    def turn(dr, dp, slot):
        side, at = ((yh + dp) % 2) * 4, (z + dr + 4) % 4
        mt[slot] = ms[pl.ds(side, 4), at].reshape(ROWS, CHIP).T

    def product(dr, dp, slot, rows, first=False):
        side, at = ((yh + dp) % 2) * 4, (z + dr + 4) % 4
        for n in range(3):
            cols = pl.ds(n * 384, 384)
            part = jnp.dot(mt[slot, rows, :], rows_of(side, at, cols), preferred_element_type=jnp.float32)
            zs[rows, cols] = part if first else zs[rows, cols] + part

    every = slice(None)
    turn(0, 0, 0)
    product(0, 0, 0, every, True)
    for h in range(2):
        gm.arrive(-1, 0, h)
        gm.arrive(1, 0, h)
        gm.arrive(0, 1, h)
    for h in range(2):
        gm.arrive(2, 0, h)
    for place in near + ((2, 0),):
        turn(*place, 0)
        product(*place, 0, every)
    for k, place in enumerate(far):
        for h in range(2):
            gm.arrive(*place, h)
        turn(*place, k)
        product(*place, k, theirs)
    last = remote(zs.at[theirs], zr, z_send, z_recv, core)
    last.start()
    for k, place in enumerate(far):
        product(*place, k, mine)
    last.wait_recv()
    total = zs[mine, :] + zr[...]
    for h in range(2):
        for first, count, piece, at in spans(h):
            out_ref[pl.ds(h * HALF + first, count), :] = total[piece * PIECE + at : piece * PIECE + at + count]

    for copy in lanes + [swap, last]:
        copy.wait_send()
    for gather in (gx, gr, gl, gm):
        gather.finish()
    for j in range(8):
        for dz in (1, 2, 3):
            for kind in range(3):
                piece_copy(j, z, (z + dz) % 4, kind).wait_send()
    for xj in range(4):
        pair_copy(xj).wait_send()


def local(gradient, momentum):
    half, full = jnp.bfloat16, jnp.float32
    dma = pltpu.SemaphoreType.DMA
    product = pl.pallas_call(
        kernel,
        out_shape=jax.ShapeDtypeStruct((ROWS, COLS), full),
        in_specs=[pl.BlockSpec(memory_space=pl.ANY)] * 2,
        out_specs=pl.BlockSpec(memory_space=pltpu.VMEM),
        scratch_shapes=[
            pltpu.VMEM((ROWS, COLS), full),
            pltpu.VMEM((ROWS, COLS), full),
            pltpu.VMEM((8, ROWS, COLS), half),
            pltpu.VMEM((CHIP, COLS), half),
            pltpu.VMEM((COLS, CHIP), half),
            pltpu.VMEM((8, 2, HALF, CHIP), half),
            pltpu.VMEM((8, 4, PIECE, CHIP), half),
            pltpu.VMEM((4, PIECE, CHIP), full),
            pltpu.VMEM((4, PIECE, CHIP), half),
            pltpu.VMEM((4, PIECE, CHIP), half),
            pltpu.VMEM((4, PIECE, CHIP), full),
            pltpu.VMEM((8, 4, PIECE, CHIP), half),
            pltpu.VMEM((8, 2, 4, PIECE, CHIP), half),
            pltpu.VMEM((8, 4, PIECE, CHIP), half),
            pltpu.VMEM((3, CHIP, ROWS), half),
            pltpu.VMEM((CHIP, COLS), full),
            pltpu.VMEM((ROWS, COLS), full),
            dma((4,)), dma((14,)), dma((16,)), dma(()), dma(()),
            dma((8, 4, 3)), dma((8, 4, 3)), dma((4,)), dma((4,)),
            dma((14,)), dma((16,)), dma((14,)), dma((16,)),
            dma((16,)), dma((16,)), dma((14,)), dma((16,)),
            dma(()), dma(()),
        ],
        name="muon",
        compiler_params=pltpu.CompilerParams(
            collective_id=0, has_side_effects=True, vmem_limit_bytes=60 * 2**20
        ),
    )(gradient, momentum)
    new_momentum = MOMENTUM_RATE * momentum + gradient
    nesterov = gradient + MOMENTUM_RATE * new_momentum
    return new_momentum, SCALE * (COEF_A * nesterov + product)


def solution(mesh):
    specs = (P("row", "col"), P("row", "col"))
    return jax.shard_map(local, mesh=mesh, in_specs=specs, out_specs=specs, check_vma=False)
```

```python
import math

import jax
import jax.numpy as jnp
from jax import lax
from jax.experimental import pallas as pl
from jax.experimental.pallas import tpu as pltpu
from jax.sharding import PartitionSpec as P

HIDDEN_SIZE = 9216
MOMENTUM_RATE = 0.95
COEF_A = 3.4445
COEF_B = -4.775
COEF_C = 2.0315
SCALE = math.sqrt(HIDDEN_SIZE)

MESH = pl.DeviceIdType.MESH
ROWS = 320
COLS = 1152
HALF = ROWS // 2
CHIP = 2 * ROWS
PIECE = ROWS // 4
MAIN, EXTRA = 32, 16
PLACES = {(0, 0): 0, (-1, 0): 1, (1, 0): 2, (2, 0): 3, (0, 1): 4, (-1, 1): 5, (1, 1): 6, (2, 1): 7}


def spans(h):
    main = [(MAIN * piece, MAIN, piece, MAIN * h) for piece in range(4)]
    return main + [(4 * MAIN + EXTRA * e, EXTRA, 2 * h + e, 2 * MAIN) for e in range(2)]


class Gather:
    def __init__(self, slot, plus, minus, pair, send, recv, over_pair, hold=False):
        self.slot, self.plus, self.minus, self.pair = slot, plus, minus, pair
        self.send, self.recv, self.over_pair, self.hold, self.started = send, recv, over_pair, hold, []

    def _copy(self, dr, dp, h, to):
        device, ring, other = {"plus": (self.plus, -1, 0), "minus": (self.minus, 1, 0), "pair": (self.pair, 0, 1)}[to]
        there = dr + ring
        there = 2 if there == -2 else there
        place = PLACES[(there, (dp + other) % 2)] * 2 + h
        ref = self.slot(dr, dp, h)
        copy = pltpu.make_async_remote_copy(
            src_ref=ref,
            dst_ref=ref,
            send_sem=self.send.at[len(self.started)],
            recv_sem=self.recv.at[place],
            device_id=device,
            device_id_type=MESH,
        )
        copy.start()
        self.started.append(copy)

    def begin(self, h):
        for to in ("plus", "minus", "pair"):
            self._copy(0, 0, h, to)

    def spread(self, h):
        self._copy(0, 1, h, "plus")
        self._copy(0, 1, h, "minus")

    def arrive(self, dr, dp, h):
        ref = self.slot(dr, dp, h)
        place = PLACES[(dr, dp)] * 2 + h
        pltpu.make_async_remote_copy(
            src_ref=ref,
            dst_ref=ref,
            send_sem=self.send.at[0],
            recv_sem=self.recv.at[place],
            device_id=self.pair,
            device_id_type=MESH,
        ).wait_recv()
        if (dr, dp) == (0, 1):
            if not self.hold:
                self.spread(h)
        elif (dr, dp, h) == (-1, 0, 0) or (dr, dp, h, self.over_pair) == (-1, 1, 0, False):
            self._copy(dr, dp, h, "plus")
        elif (dr, dp, h) == (1, 0, 1) or (dr, dp, h, self.over_pair) == (1, 1, 1, False):
            self._copy(dr, dp, h, "minus")
        elif (dr, dp) == (2, 0) and self.over_pair:
            self._copy(dr, dp, h, "pair")

    def finish(self):
        for copy in self.started:
            copy.wait_send()


def kernel(
    g_hbm, m_hbm, out_ref,
    g_ref, m_ref, xs, xi, xq, xt, ps, r1, keep, s_send, s_recv, gf, rt, ls, ms, mt, zs, zr,
    in_sem, x_send, x_recv, xc_send, xc_recv, xq_send, xq_recv, xq_sem, r1_send, r1_recv, r2_send, r2_recv,
    rt_send, rt_recv, l_send, l_recv, lc_send, lc_recv, m_send, m_recv, z_send, z_recv,
):
    row, col = lax.axis_index("row"), lax.axis_index("col")
    c, x, yl = row % 2, (row // 2) % 4, row // 8
    z, yh = col % 4, col // 4

    def device(x_, yl_, c_, yh_, z_):
        return ((yl_ * 4 + x_) * 2 + c_, yh_ * 4 + z_)

    core = device(x, yl, 1 - c, yh, z)
    xp, xm = device((x + 1) % 4, yl, c, yh, z), device((x + 3) % 4, yl, c, yh, z)
    zp, zm = device(x, yl, c, yh, (z + 1) % 4), device(x, yl, c, yh, (z + 3) % 4)
    z2 = device(x, yl, c, yh, (z + 2) % 4)
    yp, yq = device(x, 1 - yl, c, yh, z), device(x, yl, c, 1 - yh, z)
    yd = device(x, 1 - yl, c, 1 - yh, z)
    early = yl == yh
    barrier = pltpu.get_barrier_semaphore()
    partners = (core, xp, xm, zp, zm, z2, yp, yq, yd)
    for partner in partners:
        pl.semaphore_signal(barrier, inc=1, device_id=partner, device_id_type=MESH)
    loads = []
    for h in range(2):
        rows = pl.ds(h * HALF, HALF)
        for k, (hbm, ref) in enumerate(((g_hbm, g_ref), (m_hbm, m_ref))):
            load = pltpu.make_async_copy(hbm.at[rows], ref.at[rows], in_sem.at[2 * h + k])
            load.start()
            loads.append(load)

    def remote(src, dst, send, recv, to):
        return pltpu.make_async_remote_copy(
            src_ref=src, dst_ref=dst, send_sem=send, recv_sem=recv, device_id=to, device_id_type=MESH
        )

    def chip_at(dr, dp):
        return ((yl + dp) % 2) * 4 + (x + dr + 4) % 4

    own = chip_at(0, 0)

    gx = Gather(lambda dr, dp, h: xs.at[chip_at(dr, dp), pl.ds(h * HALF, HALF)], xp, xm, yp, x_send, x_recv, False, True)
    mine = pl.ds(pl.multiple_of(c * ROWS, 32), ROWS)
    theirs = pl.ds(pl.multiple_of((1 - c) * ROWS, 32), ROWS)
    for h in range(2):
        rows = pl.ds(h * HALF, HALF)
        loads[2 * h].wait()
        loads[2 * h + 1].wait()
        new = MOMENTUM_RATE * m_ref[rows, :] + g_ref[rows, :]
        low = (g_ref[rows, :] + MOMENTUM_RATE * new).astype(jnp.bfloat16)
        xs[own, rows, :] = low
        if h == 0:
            pl.semaphore_wait(barrier, len(partners))
        gx.begin(h)
        for first, count, piece, at in spans(h):
            xi[pl.ds(pl.multiple_of(c * ROWS + piece * PIECE + at, 16), count), :] = low[first : first + count]
    swap = remote(xi.at[mine], xi.at[mine], xc_send, xc_recv, core)
    swap.start()
    remote(xi.at[theirs], xi.at[theirs], xc_send, xc_recv, core).wait_recv()
    for k in range(COLS // 128):
        xt[0, k * 128 : (k + 1) * 128, :] = xi[:, k * 128 : (k + 1) * 128].T

    def piece_copy(j, src_z, dst_z, kind):
        if kind < 2:
            src = ps.at[j, kind, pl.ds(pl.multiple_of(dst_z * MAIN, MAIN), MAIN)]
        else:
            src = ps.at[j, dst_z // 2, pl.ds(pl.multiple_of(4 * MAIN + dst_z % 2 * EXTRA, EXTRA), EXTRA)]
        dst = r1.at[j, src_z, pl.ds(kind * MAIN, MAIN if kind < 2 else EXTRA)]
        to = device(x, yl, c, yh, dst_z)
        return remote(src, dst, r1_send.at[j, dst_z, kind], r1_recv.at[j, src_z, kind], to)

    def block_of(i, dr):
        return i * 4 + (x + dr + 4) % 4

    def gram(i, dr, h):
        j, block = chip_at(dr, 0), block_of(i, dr)
        part = jnp.dot(xs[j, h * HALF : (h + 1) * HALF, :], xt[i], preferred_element_type=jnp.float32)
        ps[block, h] = part.astype(jnp.bfloat16)
        for dz in (2, 1, 3):
            piece_copy(block, z, (z + dz) % 4, h).start()
        for piece in (2 * h, 2 * h + 1):

            @pl.when(piece != z)
            def _(piece=piece):
                piece_copy(block, z, piece, 2).start()

    def sum_copy(i, xj, slot, to):
        return remote(s_send.at[i, xj], s_recv.at[slot, xj], r2_send.at[i, xj], r2_recv.at[slot, xj], to)

    def sum_arrive(slot, xj):
        ref = s_recv.at[slot, xj]
        remote(ref, ref, r2_send.at[0, xj], r2_recv.at[slot, xj], yp).wait_recv()

    def reduce(i, dr):
        block = block_of(i, dr)
        own_rows = [ps[block, h, pl.ds(pl.multiple_of(z * MAIN, MAIN), MAIN)] for h in range(2)]
        own_rows.append(ps[block, z // 2, pl.ds(pl.multiple_of(4 * MAIN + z % 2 * EXTRA, EXTRA), EXTRA)])
        total = jnp.concatenate(own_rows, axis=0).astype(jnp.float32)
        for dz in (1, 3, 2):
            src_z = (z + dz) % 4
            for kind in range(3):
                piece_copy(block, src_z, src_z, kind).wait_recv()
            total = total + r1[block, src_z].astype(jnp.float32)
        xj = (x + dr + 4) % 4
        if i == 0:

            @pl.when(early)
            def _():
                keep[xj] = total

            @pl.when(jnp.logical_not(early))
            def _():
                s_send[i, xj] = total.astype(jnp.bfloat16)
                sum_copy(i, xj, 0, yq).start()

        else:
            s_send[i, xj] = total.astype(jnp.bfloat16)

            @pl.when(early)
            def _():
                sum_copy(i, xj, 0, yp).start()

            @pl.when(jnp.logical_not(early))
            def _():
                sum_copy(i, xj, 1, yd).start()

    def pass_pair(h):
        rows = pl.ds(h * HALF, HALF)
        src = xs.at[chip_at(0, 1), rows]
        over = remote(src, xq.at[c, rows], xq_send.at[h], xq_recv.at[h], core)
        over.start()
        here = pltpu.make_async_copy(src, xq.at[c, rows], xq_sem.at[h])
        here.start()
        return over, here

    gram(0, 0, 0)
    gram(0, 0, 1)
    passed = []
    for h in range(2):
        gx.arrive(-1, 0, h)
        gx.arrive(1, 0, h)
        gx.arrive(0, 1, h)
        passed.append(pass_pair(h))
        gram(0, -1, h)
        gram(0, 1, h)
    for h in range(2):
        gx.spread(h)
    for h in range(2):
        ref = xq.at[1 - c, pl.ds(h * HALF, HALF)]
        remote(ref, ref, xq_send.at[h], xq_recv.at[h], core).wait_recv()
        passed[h][1].wait()
    for k in range(COLS // 128):
        cols = slice(k * 128, (k + 1) * 128)
        blocks = []
        for lane in range(2):
            for piece in range(4):
                for first in (MAIN * piece, HALF + MAIN * piece):
                    blocks.append(xq[lane, first : first + MAIN, cols])
                first = piece // 2 * HALF + 4 * MAIN + piece % 2 * EXTRA
                blocks.append(xq[lane, first : first + EXTRA, cols])
        xt[1, cols, :] = jnp.concatenate(blocks, axis=0).T
    for dr in (0, -1, 1):
        for h in range(2):
            gram(1, dr, h)
    reduce(0, 0)
    for h in range(2):
        gx.arrive(2, 0, h)
        for i in range(2):
            gram(i, 2, h)
    for place in ((0, -1), (0, 1), (1, 0), (1, -1), (1, 1), (0, 2), (1, 2)):
        reduce(*place)

    gr = Gather(lambda dr, dp, h: rt.at[chip_at(dr, dp), pl.ds(h * 2, 2)], xp, xm, yp, rt_send, rt_recv, True)

    def col_slot(ref, lane):
        def slot(dr, dp, h):
            first = ((yh + dp) % 2) * 4 + h * 2
            at = (z + dr + 4) % 4
            return ref.at[pl.ds(first, 2), lane, at] if lane is not None else ref.at[pl.ds(first, 2), at]

        return slot

    mine_of, theirs_of = col_slot(ls, c), col_slot(ls, 1 - c)
    gl = Gather(mine_of, zp, zm, yq, l_send, l_recv, False)
    lanes = []

    def to_core(dr, dp, h):
        place = PLACES[(dr, dp)] * 2 + h
        copy = remote(mine_of(dr, dp, h), mine_of(dr, dp, h), lc_send.at[place], lc_recv.at[place], core)
        copy.start()
        lanes.append(copy)

    def from_core(dr, dp, h):
        place = PLACES[(dr, dp)] * 2 + h
        ref = theirs_of(dr, dp, h)
        remote(ref, ref, lc_send.at[place], lc_recv.at[place], core).wait_recv()

    for h in range(2):
        for xj in (2 * h, 2 * h + 1):
            sum_arrive(0, xj)

            @pl.when(jnp.logical_not(early))
            def _(xj=xj):
                sum_arrive(1, xj)
                keep[xj] = s_recv[1, xj].astype(jnp.float32)

            total = keep[xj] + s_recv[0, xj].astype(jnp.float32)
            gf[xj] = total
            low = total.astype(jnp.bfloat16)
            rt[own, xj] = low
            ls[yh * 4 + xj, c, z] = low
        gl.begin(h)
        to_core(0, 0, h)
    for h in range(2):
        gr.begin(h)

    near, far = ((-1, 0), (1, 0), (0, 1)), ((-1, 1), (1, 1), (2, 1))

    def arrive_l(dr, dp, h):
        gl.arrive(dr, dp, h)
        to_core(dr, dp, h)

    for h in range(2):
        for arrive in (arrive_l, gr.arrive):
            arrive(-1, 0, h)
            arrive(1, 0, h)
        arrive_l(0, 1, h)
    for h in range(2):
        gr.arrive(2, 0, h)
        gr.arrive(0, 1, h)
        arrive_l(2, 0, h)
    for h in range(2):
        for arrive in (arrive_l, gr.arrive):
            arrive(-1, 1, h)
            arrive(1, 1, h)
    for h in range(2):
        gr.arrive(2, 1, h)
        gx.arrive(-1, 1, h)
        gx.arrive(1, 1, h)

    def square(j):
        left = rt[j].reshape(ROWS, CHIP)
        right = ls[j].reshape(CHIP, CHIP)
        return jnp.dot(left, right, preferred_element_type=jnp.float32)

    for dr in (0, -1, 1, 2):
        for h in range(2):
            from_core(dr, 0, h)
    total = square(yh * 4)
    for k in range(1, 4):
        total = total + square(yh * 4 + k)
    for h in range(2):
        arrive_l(2, 1, h)
    for dr in (0, -1, 1, 2):
        for h in range(2):
            from_core(dr, 1, h)
    for k in range(4):
        total = total + square((1 - yh) * 4 + k)
    mixing = (COEF_B * gf[...].reshape(ROWS, CHIP) + COEF_C * total).astype(jnp.bfloat16)
    mixing = mixing.reshape(4, PIECE, CHIP)
    for xj in range(4):
        ms[yh * 4 + xj, z] = mixing[xj]
    gm = Gather(col_slot(ms, None), zp, zm, yq, m_send, m_recv, True)
    gm.begin(0)
    gm.begin(1)

    def rows_of(side, at, cols):
        blocks = []
        for k in range(4):
            for h in range(2):
                blocks.append(xs[side + k, pl.ds(pl.multiple_of(h * HALF + at * MAIN, MAIN), MAIN), cols])
            extra = at // 2 * HALF + 4 * MAIN + at % 2 * EXTRA
            blocks.append(xs[side + k, pl.ds(pl.multiple_of(extra, EXTRA), EXTRA), cols])
        return jnp.concatenate(blocks, axis=0)

    def turn(dr, dp, slot):
        side, at = ((yh + dp) % 2) * 4, (z + dr + 4) % 4
        mt[slot] = ms[pl.ds(side, 4), at].reshape(ROWS, CHIP).T

    def product(dr, dp, slot, rows, first=False):
        side, at = ((yh + dp) % 2) * 4, (z + dr + 4) % 4
        for n in range(3):
            cols = pl.ds(n * 384, 384)
            part = jnp.dot(mt[slot, rows, :], rows_of(side, at, cols), preferred_element_type=jnp.float32)
            zs[rows, cols] = part if first else zs[rows, cols] + part

    every = slice(None)
    for h in range(2):
        gx.arrive(2, 1, h)
    turn(0, 0, 0)
    product(0, 0, 0, every, True)
    for h in range(2):
        gm.arrive(-1, 0, h)
        gm.arrive(1, 0, h)
        gm.arrive(0, 1, h)
    for h in range(2):
        gm.arrive(2, 0, h)
    for place in near + ((2, 0),):
        turn(*place, 0)
        product(*place, 0, every)
    for k, place in enumerate(far):
        for h in range(2):
            gm.arrive(*place, h)
        turn(*place, k)
        product(*place, k, theirs)
    last = remote(zs.at[theirs], zr, z_send, z_recv, core)
    last.start()
    for k, place in enumerate(far):
        product(*place, k, mine)
    last.wait_recv()
    total = zs[mine, :] + zr[...]
    for h in range(2):
        for first, count, piece, at in spans(h):
            out_ref[pl.ds(h * HALF + first, count), :] = total[piece * PIECE + at : piece * PIECE + at + count]

    for copy in lanes + [swap, last] + [over for over, _ in passed]:
        copy.wait_send()
    for gather in (gx, gr, gl, gm):
        gather.finish()
    for j in range(8):
        for dz in (1, 2, 3):
            for kind in range(3):
                piece_copy(j, z, (z + dz) % 4, kind).wait_send()
    for xj in range(4):
        sum_copy(1, xj, 0, yp).wait_send()

        @pl.when(jnp.logical_not(early))
        def _(xj=xj):
            sum_copy(0, xj, 0, yq).wait_send()


def local(gradient, momentum):
    half, full = jnp.bfloat16, jnp.float32
    dma = pltpu.SemaphoreType.DMA
    product = pl.pallas_call(
        kernel,
        out_shape=jax.ShapeDtypeStruct((ROWS, COLS), full),
        in_specs=[pl.BlockSpec(memory_space=pl.ANY)] * 2,
        out_specs=pl.BlockSpec(memory_space=pltpu.VMEM),
        scratch_shapes=[
            pltpu.VMEM((ROWS, COLS), full),
            pltpu.VMEM((ROWS, COLS), full),
            pltpu.VMEM((8, ROWS, COLS), half),
            pltpu.VMEM((CHIP, COLS), half),
            pltpu.VMEM((2, ROWS, COLS), half),
            pltpu.VMEM((2, COLS, CHIP), half),
            pltpu.VMEM((8, 2, HALF, CHIP), half),
            pltpu.VMEM((8, 4, PIECE, CHIP), half),
            pltpu.VMEM((4, PIECE, CHIP), full),
            pltpu.VMEM((2, 4, PIECE, CHIP), half),
            pltpu.VMEM((2, 4, PIECE, CHIP), half),
            pltpu.VMEM((4, PIECE, CHIP), full),
            pltpu.VMEM((8, 4, PIECE, CHIP), half),
            pltpu.VMEM((8, 2, 4, PIECE, CHIP), half),
            pltpu.VMEM((8, 4, PIECE, CHIP), half),
            pltpu.VMEM((3, CHIP, ROWS), half),
            pltpu.VMEM((CHIP, COLS), full),
            pltpu.VMEM((ROWS, COLS), full),
            dma((4,)), dma((14,)), dma((16,)), dma(()), dma(()), dma((2,)), dma((2,)), dma((2,)),
            dma((8, 4, 3)), dma((8, 4, 3)), dma((2, 4)), dma((2, 4)),
            dma((14,)), dma((16,)), dma((14,)), dma((16,)),
            dma((16,)), dma((16,)), dma((14,)), dma((16,)),
            dma(()), dma(()),
        ],
        name="muon",
        compiler_params=pltpu.CompilerParams(
            collective_id=0, has_side_effects=True, vmem_limit_bytes=60 * 2**20
        ),
    )(gradient, momentum)
    new_momentum = MOMENTUM_RATE * momentum + gradient
    nesterov = gradient + MOMENTUM_RATE * new_momentum
    return new_momentum, SCALE * (COEF_A * nesterov + product)


def solution(mesh):
    specs = (P("row", "col"), P("row", "col"))
    return jax.shard_map(local, mesh=mesh, in_specs=specs, out_specs=specs, check_vma=False)
```

```python
import math

import jax
import jax.numpy as jnp
from jax import lax
from jax.experimental import pallas as pl
from jax.experimental.pallas import tpu as pltpu
from jax.sharding import PartitionSpec as P

HIDDEN_SIZE = 9216
MOMENTUM_RATE = 0.95
COEF_A = 3.4445
COEF_B = -4.775
COEF_C = 2.0315
SCALE = math.sqrt(HIDDEN_SIZE)

MESH = pl.DeviceIdType.MESH
ROWS = 320
COLS = 1152
HALF = ROWS // 2
CHIP = 2 * ROWS
PIECE = ROWS // 4
MAIN, EXTRA = 32, 16
ORDER = (0, -1, 1, 2)
PLACES = {(0, 0): 0, (-1, 0): 1, (1, 0): 2, (2, 0): 3, (0, 1): 4, (-1, 1): 5, (1, 1): 6, (2, 1): 7}


def spans(h):
    main = [(MAIN * piece, MAIN, piece, MAIN * h) for piece in range(4)]
    return main + [(4 * MAIN + EXTRA * e, EXTRA, 2 * h + e, 2 * MAIN) for e in range(2)]


class Gather:
    def __init__(self, slot, plus, minus, pair, send, recv, over_pair, parts=2, hold=False):
        self.slot, self.plus, self.minus, self.pair = slot, plus, minus, pair
        self.send, self.recv, self.over_pair = send, recv, over_pair
        self.parts, self.hold, self.started = parts, hold, []

    def _copy(self, dr, dp, h, to):
        device, ring, other = {"plus": (self.plus, -1, 0), "minus": (self.minus, 1, 0), "pair": (self.pair, 0, 1)}[to]
        there = dr + ring
        there = 2 if there == -2 else there
        place = PLACES[(there, (dp + other) % 2)] * self.parts + h
        ref = self.slot(dr, dp, h)
        copy = pltpu.make_async_remote_copy(
            src_ref=ref,
            dst_ref=ref,
            send_sem=self.send.at[len(self.started)],
            recv_sem=self.recv.at[place],
            device_id=device,
            device_id_type=MESH,
        )
        copy.start()
        self.started.append(copy)

    def begin(self, h):
        for to in ("plus", "minus", "pair"):
            self._copy(0, 0, h, to)

    def spread(self, h):
        self._copy(0, 1, h, "plus")
        self._copy(0, 1, h, "minus")

    def arrive(self, dr, dp, h):
        ref = self.slot(dr, dp, h)
        place = PLACES[(dr, dp)] * self.parts + h
        pltpu.make_async_remote_copy(
            src_ref=ref,
            dst_ref=ref,
            send_sem=self.send.at[0],
            recv_sem=self.recv.at[place],
            device_id=self.pair,
            device_id_type=MESH,
        ).wait_recv()
        if (dr, dp) == (0, 1):
            if not self.hold:
                self.spread(h)
        elif dr == -1 and h % 2 == 0 and not (dp and self.over_pair):
            self._copy(dr, dp, h, "plus")
        elif dr == 1 and h % 2 == 1 and not (dp and self.over_pair):
            self._copy(dr, dp, h, "minus")
        elif (dr, dp) == (2, 0) and self.over_pair:
            self._copy(dr, dp, h, "pair")

    def finish(self):
        for copy in self.started:
            copy.wait_send()


def kernel(
    g_hbm, m_hbm, out_ref,
    g_ref, m_ref, xs, xi, xq, xt, ps, r1, keep, s_send, s_recv, gf, rt, ls, ms, mt, zs, zr,
    in_sem, x_send, x_recv, xc_send, xc_recv, xq_send, xq_recv, xq_sem, r1_send, r1_recv, r2_send, r2_recv,
    rt_send, rt_recv, l_send, l_recv, lc_send, lc_recv, m_send, m_recv, z_send, z_recv,
):
    row, col = lax.axis_index("row"), lax.axis_index("col")
    c, x, yl = row % 2, (row // 2) % 4, row // 8
    z, yh = col % 4, col // 4

    def device(x_, yl_, c_, yh_, z_):
        return ((yl_ * 4 + x_) * 2 + c_, yh_ * 4 + z_)

    core = device(x, yl, 1 - c, yh, z)
    xp, xm = device((x + 1) % 4, yl, c, yh, z), device((x + 3) % 4, yl, c, yh, z)
    zp, zm = device(x, yl, c, yh, (z + 1) % 4), device(x, yl, c, yh, (z + 3) % 4)
    z2 = device(x, yl, c, yh, (z + 2) % 4)
    yp, yq = device(x, 1 - yl, c, yh, z), device(x, yl, c, 1 - yh, z)
    yd = device(x, 1 - yl, c, 1 - yh, z)
    early = yl == yh
    barrier = pltpu.get_barrier_semaphore()
    partners = (core, xp, xm, zp, zm, z2, yp, yq, yd)
    for partner in partners:
        pl.semaphore_signal(barrier, inc=1, device_id=partner, device_id_type=MESH)
    loads = []
    for h in range(2):
        rows = pl.ds(h * HALF, HALF)
        for k, (hbm, ref) in enumerate(((g_hbm, g_ref), (m_hbm, m_ref))):
            load = pltpu.make_async_copy(hbm.at[rows], ref.at[rows], in_sem.at[2 * h + k])
            load.start()
            loads.append(load)

    def remote(src, dst, send, recv, to):
        return pltpu.make_async_remote_copy(
            src_ref=src, dst_ref=dst, send_sem=send, recv_sem=recv, device_id=to, device_id_type=MESH
        )

    def chip_at(dr, dp):
        return ((yl + dp) % 2) * 4 + (x + dr + 4) % 4

    own = chip_at(0, 0)

    gx = Gather(lambda dr, dp, h: xs.at[chip_at(dr, dp), pl.ds(h * HALF, HALF)], xp, xm, yp, x_send, x_recv, False, hold=True)
    mine = pl.ds(pl.multiple_of(c * ROWS, 32), ROWS)
    theirs = pl.ds(pl.multiple_of((1 - c) * ROWS, 32), ROWS)
    for h in range(2):
        rows = pl.ds(h * HALF, HALF)
        loads[2 * h].wait()
        loads[2 * h + 1].wait()
        new = MOMENTUM_RATE * m_ref[rows, :] + g_ref[rows, :]
        low = (g_ref[rows, :] + MOMENTUM_RATE * new).astype(jnp.bfloat16)
        xs[own, rows, :] = low
        if h == 0:
            pl.semaphore_wait(barrier, len(partners))
        gx.begin(h)
        for first, count, piece, at in spans(h):
            xi[pl.ds(pl.multiple_of(c * ROWS + piece * PIECE + at, 16), count), :] = low[first : first + count]
    swap = remote(xi.at[mine], xi.at[mine], xc_send, xc_recv, core)
    swap.start()
    remote(xi.at[theirs], xi.at[theirs], xc_send, xc_recv, core).wait_recv()
    for k in range(COLS // 128):
        xt[0, k * 128 : (k + 1) * 128, :] = xi[:, k * 128 : (k + 1) * 128].T

    def piece_copy(j, src_z, dst_z, kind):
        if kind < 2:
            src = ps.at[j, kind, pl.ds(pl.multiple_of(dst_z * MAIN, MAIN), MAIN)]
        else:
            src = ps.at[j, dst_z // 2, pl.ds(pl.multiple_of(4 * MAIN + dst_z % 2 * EXTRA, EXTRA), EXTRA)]
        dst = r1.at[j, src_z, pl.ds(kind * MAIN, MAIN if kind < 2 else EXTRA)]
        to = device(x, yl, c, yh, dst_z)
        return remote(src, dst, r1_send.at[j, dst_z, kind], r1_recv.at[j, src_z, kind], to)

    def block_of(i, dr):
        return i * 4 + (x + dr + 4) % 4

    def gram(i, dr, h):
        j, block = chip_at(dr, 0), block_of(i, dr)
        part = jnp.dot(xs[j, h * HALF : (h + 1) * HALF, :], xt[i], preferred_element_type=jnp.float32)
        ps[block, h] = part.astype(jnp.bfloat16)
        for dz in (2, 1, 3):
            piece_copy(block, z, (z + dz) % 4, h).start()
        for piece in (2 * h, 2 * h + 1):

            @pl.when(piece != z)
            def _(piece=piece):
                piece_copy(block, z, piece, 2).start()

    def sum_copy(i, xj, slot, to):
        return remote(s_send.at[i, xj], s_recv.at[slot, xj], r2_send.at[i, xj], r2_recv.at[slot, xj], to)

    def sum_arrive(slot, xj):
        ref = s_recv.at[slot, xj]
        remote(ref, ref, r2_send.at[0, xj], r2_recv.at[slot, xj], yp).wait_recv()

    def reduce(i, dr):
        block = block_of(i, dr)
        own_rows = [ps[block, h, pl.ds(pl.multiple_of(z * MAIN, MAIN), MAIN)] for h in range(2)]
        own_rows.append(ps[block, z // 2, pl.ds(pl.multiple_of(4 * MAIN + z % 2 * EXTRA, EXTRA), EXTRA)])
        total = jnp.concatenate(own_rows, axis=0).astype(jnp.float32)
        for dz in (1, 3, 2):
            src_z = (z + dz) % 4
            for kind in range(3):
                piece_copy(block, src_z, src_z, kind).wait_recv()
            total = total + r1[block, src_z].astype(jnp.float32)
        xj = (x + dr + 4) % 4
        if i == 0:

            @pl.when(early)
            def _():
                keep[xj] = total

            @pl.when(jnp.logical_not(early))
            def _():
                s_send[i, xj] = total.astype(jnp.bfloat16)
                sum_copy(i, xj, 0, yq).start()

        else:
            s_send[i, xj] = total.astype(jnp.bfloat16)

            @pl.when(early)
            def _():
                sum_copy(i, xj, 0, yp).start()

            @pl.when(jnp.logical_not(early))
            def _():
                sum_copy(i, xj, 1, yd).start()

    def pass_pair(h):
        rows = pl.ds(h * HALF, HALF)
        src = xs.at[chip_at(0, 1), rows]
        over = remote(src, xq.at[c, rows], xq_send.at[h], xq_recv.at[h], core)
        over.start()
        here = pltpu.make_async_copy(src, xq.at[c, rows], xq_sem.at[h])
        here.start()
        return over, here

    def row_slot(dr, dp, k):
        return rt.at[chip_at(dr, dp), (x + dr + ORDER[k] + 4) % 4]

    def col_slot(lane):
        def slot(dr, dp, k):
            return ls.at[((yh + dp) % 2) * 4 + (x + ORDER[k] + 4) % 4, lane, (z + dr + 4) % 4]

        return slot

    gr = Gather(row_slot, xp, xm, yp, rt_send, rt_recv, True, 4)
    mine_of, theirs_of = col_slot(c), col_slot(1 - c)
    gl = Gather(mine_of, zp, zm, yq, l_send, l_recv, False, 4)
    lanes = []

    def to_core(dr, dp, k):
        place = PLACES[(dr, dp)] * 4 + k
        copy = remote(mine_of(dr, dp, k), mine_of(dr, dp, k), lc_send.at[place], lc_recv.at[place], core)
        copy.start()
        lanes.append(copy)

    def from_core(dr, dp, k):
        place = PLACES[(dr, dp)] * 4 + k
        ref = theirs_of(dr, dp, k)
        remote(ref, ref, lc_send.at[place], lc_recv.at[place], core).wait_recv()

    def arrive_l(dr, dp, k):
        gl.arrive(dr, dp, k)
        to_core(dr, dp, k)

    def finish_sum(k):
        xj = (x + ORDER[k] + 4) % 4
        sum_arrive(0, xj)

        @pl.when(jnp.logical_not(early))
        def _():
            sum_arrive(1, xj)
            keep[xj] = s_recv[1, xj].astype(jnp.float32)

        total = keep[xj] + s_recv[0, xj].astype(jnp.float32)
        gf[xj] = total
        low = total.astype(jnp.bfloat16)
        ls[yh * 4 + xj, c, z] = low
        gl.begin(k)
        rt[own, xj] = low
        gr.begin(k)
        to_core(0, 0, k)

    def near_of(k):
        for arrive in (arrive_l, gr.arrive):
            arrive(-1, 0, k)
            arrive(1, 0, k)
        arrive_l(0, 1, k)
        gr.arrive(0, 1, k)

    def far_of(k):
        gr.arrive(2, 0, k)
        for arrive in (arrive_l, gr.arrive):
            arrive(-1, 1, k)
            arrive(1, 1, k)
        arrive_l(2, 0, k)

    near, far = ((-1, 0), (1, 0), (0, 1)), ((-1, 1), (1, 1), (2, 1))
    gram(0, 0, 0)
    gram(0, 0, 1)
    passed = []
    for h in range(2):
        gx.arrive(-1, 0, h)
        gx.arrive(1, 0, h)
        gx.arrive(0, 1, h)
        passed.append(pass_pair(h))
        gram(0, -1, h)
        gram(0, 1, h)
        if h == 0:
            reduce(0, 0)
    for h in range(2):
        gx.spread(h)
    for h in range(2):
        ref = xq.at[1 - c, pl.ds(h * HALF, HALF)]
        remote(ref, ref, xq_send.at[h], xq_recv.at[h], core).wait_recv()
        passed[h][1].wait()
    for k in range(COLS // 128):
        cols = slice(k * 128, (k + 1) * 128)
        blocks = []
        for lane in range(2):
            for piece in range(4):
                for first in (MAIN * piece, HALF + MAIN * piece):
                    blocks.append(xq[lane, first : first + MAIN, cols])
                first = piece // 2 * HALF + 4 * MAIN + piece % 2 * EXTRA
                blocks.append(xq[lane, first : first + EXTRA, cols])
        xt[1, cols, :] = jnp.concatenate(blocks, axis=0).T
    for dr in (0, -1, 1):
        for h in range(2):
            gram(1, dr, h)
    for h in range(2):
        gx.arrive(2, 0, h)
        for i in range(2):
            gram(i, 2, h)
    reduce(0, -1)
    reduce(0, 1)
    reduce(1, 0)
    finish_sum(0)
    reduce(1, -1)
    finish_sum(1)
    reduce(1, 1)
    finish_sum(2)
    near_of(0)
    reduce(0, 2)
    reduce(1, 2)
    finish_sum(3)
    near_of(1)
    far_of(0)
    near_of(2)
    far_of(1)
    near_of(3)
    far_of(2)
    far_of(3)
    for k in range(4):
        gr.arrive(2, 1, k)
    for h in range(2):
        gx.arrive(-1, 1, h)
        gx.arrive(1, 1, h)

    def square(j):
        left = rt[j].reshape(ROWS, CHIP)
        right = ls[j].reshape(CHIP, CHIP)
        return jnp.dot(left, right, preferred_element_type=jnp.float32)

    for dr in (0, -1, 1, 2):
        for k in range(4):
            from_core(dr, 0, k)
    total = square(yh * 4)
    for k in range(1, 4):
        total = total + square(yh * 4 + k)
    for k in range(4):
        arrive_l(2, 1, k)
    for dr in (0, -1, 1, 2):
        for k in range(4):
            from_core(dr, 1, k)
    for k in range(4):
        total = total + square((1 - yh) * 4 + k)
    mixing = (COEF_B * gf[...].reshape(ROWS, CHIP) + COEF_C * total).astype(jnp.bfloat16)
    mixing = mixing.reshape(4, PIECE, CHIP)
    for xj in range(4):
        ms[yh * 4 + xj, z] = mixing[xj]
    def mix_slot(dr, dp, h):
        return ms.at[pl.ds(((yh + dp) % 2) * 4 + h * 2, 2), (z + dr + 4) % 4]

    gm = Gather(mix_slot, zp, zm, yq, m_send, m_recv, True)
    gm.begin(0)
    gm.begin(1)

    def rows_of(side, at, cols):
        blocks = []
        for k in range(4):
            for h in range(2):
                blocks.append(xs[side + k, pl.ds(pl.multiple_of(h * HALF + at * MAIN, MAIN), MAIN), cols])
            extra = at // 2 * HALF + 4 * MAIN + at % 2 * EXTRA
            blocks.append(xs[side + k, pl.ds(pl.multiple_of(extra, EXTRA), EXTRA), cols])
        return jnp.concatenate(blocks, axis=0)

    def turn(dr, dp, slot):
        side, at = ((yh + dp) % 2) * 4, (z + dr + 4) % 4
        mt[slot] = ms[pl.ds(side, 4), at].reshape(ROWS, CHIP).T

    def product(dr, dp, slot, rows, first=False):
        side, at = ((yh + dp) % 2) * 4, (z + dr + 4) % 4
        for n in range(3):
            cols = pl.ds(n * 384, 384)
            part = jnp.dot(mt[slot, rows, :], rows_of(side, at, cols), preferred_element_type=jnp.float32)
            zs[rows, cols] = part if first else zs[rows, cols] + part

    every = slice(None)
    for h in range(2):
        gx.arrive(2, 1, h)
    turn(0, 0, 0)
    product(0, 0, 0, every, True)
    for h in range(2):
        gm.arrive(-1, 0, h)
        gm.arrive(1, 0, h)
        gm.arrive(0, 1, h)
    for h in range(2):
        gm.arrive(2, 0, h)
    for place in near + ((2, 0),):
        turn(*place, 0)
        product(*place, 0, every)
    for k, place in enumerate(far):
        for h in range(2):
            gm.arrive(*place, h)
        turn(*place, k)
        product(*place, k, theirs)
    last = remote(zs.at[theirs], zr, z_send, z_recv, core)
    last.start()
    for k, place in enumerate(far):
        product(*place, k, mine)
    last.wait_recv()
    total = zs[mine, :] + zr[...]
    for h in range(2):
        for first, count, piece, at in spans(h):
            out_ref[pl.ds(h * HALF + first, count), :] = total[piece * PIECE + at : piece * PIECE + at + count]

    for copy in lanes + [swap, last] + [over for over, _ in passed]:
        copy.wait_send()
    for gather in (gx, gr, gl, gm):
        gather.finish()
    for j in range(8):
        for dz in (1, 2, 3):
            for kind in range(3):
                piece_copy(j, z, (z + dz) % 4, kind).wait_send()
    for xj in range(4):
        sum_copy(1, xj, 0, yp).wait_send()

        @pl.when(jnp.logical_not(early))
        def _(xj=xj):
            sum_copy(0, xj, 0, yq).wait_send()


def local(gradient, momentum):
    half, full = jnp.bfloat16, jnp.float32
    dma = pltpu.SemaphoreType.DMA
    product = pl.pallas_call(
        kernel,
        out_shape=jax.ShapeDtypeStruct((ROWS, COLS), full),
        in_specs=[pl.BlockSpec(memory_space=pl.ANY)] * 2,
        out_specs=pl.BlockSpec(memory_space=pltpu.VMEM),
        scratch_shapes=[
            pltpu.VMEM((ROWS, COLS), full),
            pltpu.VMEM((ROWS, COLS), full),
            pltpu.VMEM((8, ROWS, COLS), half),
            pltpu.VMEM((CHIP, COLS), half),
            pltpu.VMEM((2, ROWS, COLS), half),
            pltpu.VMEM((2, COLS, CHIP), half),
            pltpu.VMEM((8, 2, HALF, CHIP), half),
            pltpu.VMEM((8, 4, PIECE, CHIP), half),
            pltpu.VMEM((4, PIECE, CHIP), full),
            pltpu.VMEM((2, 4, PIECE, CHIP), half),
            pltpu.VMEM((2, 4, PIECE, CHIP), half),
            pltpu.VMEM((4, PIECE, CHIP), full),
            pltpu.VMEM((8, 4, PIECE, CHIP), half),
            pltpu.VMEM((8, 2, 4, PIECE, CHIP), half),
            pltpu.VMEM((8, 4, PIECE, CHIP), half),
            pltpu.VMEM((3, CHIP, ROWS), half),
            pltpu.VMEM((CHIP, COLS), full),
            pltpu.VMEM((ROWS, COLS), full),
            dma((4,)), dma((14,)), dma((16,)), dma(()), dma(()), dma((2,)), dma((2,)), dma((2,)),
            dma((8, 4, 3)), dma((8, 4, 3)), dma((2, 4)), dma((2, 4)),
            dma((28,)), dma((32,)), dma((28,)), dma((32,)),
            dma((32,)), dma((32,)), dma((14,)), dma((16,)),
            dma(()), dma(()),
        ],
        name="muon",
        compiler_params=pltpu.CompilerParams(
            collective_id=0, has_side_effects=True, vmem_limit_bytes=60 * 2**20
        ),
    )(gradient, momentum)
    new_momentum = MOMENTUM_RATE * momentum + gradient
    nesterov = gradient + MOMENTUM_RATE * new_momentum
    return new_momentum, SCALE * (COEF_A * nesterov + product)


def solution(mesh):
    specs = (P("row", "col"), P("row", "col"))
    return jax.shard_map(local, mesh=mesh, in_specs=specs, out_specs=specs, check_vma=False)
```

```python
import math

import jax
import jax.numpy as jnp
from jax import lax
from jax.experimental import pallas as pl
from jax.experimental.pallas import tpu as pltpu
from jax.sharding import PartitionSpec as P

HIDDEN_SIZE = 9216
MOMENTUM_RATE = 0.95
COEF_A = 3.4445
COEF_B = -4.775
COEF_C = 2.0315
SCALE = math.sqrt(HIDDEN_SIZE)

MESH = pl.DeviceIdType.MESH
ROWS = 320
COLS = 1152
HALF = ROWS // 2
CHIP = 2 * ROWS
PIECE = ROWS // 4
ORDER = (0, -1, 1, 2)
PLACES = {(0, 0): 0, (-1, 0): 1, (1, 0): 2, (2, 0): 3, (0, 1): 4, (-1, 1): 5, (1, 1): 6, (2, 1): 7}


class Gather:
    def __init__(self, slot, plus, minus, pair, send, recv, cross, parts=2, hold=False):
        self.slot, self.plus, self.minus, self.pair = slot, plus, minus, pair
        self.send, self.recv, self.cross = send, recv, cross
        self.parts, self.hold, self.started = parts, hold, []

    def _copy(self, dr, dp, h, to):
        device, ring, other = {"plus": (self.plus, -1, 0), "minus": (self.minus, 1, 0), "pair": (self.pair, 0, 1)}[to]
        there = dr + ring
        there = 2 if there == -2 else there
        place = PLACES[(there, (dp + other) % 2)] * self.parts + h
        ref = self.slot(dr, dp, h)
        copy = pltpu.make_async_remote_copy(
            src_ref=ref,
            dst_ref=ref,
            send_sem=self.send.at[len(self.started)],
            recv_sem=self.recv.at[place],
            device_id=device,
            device_id_type=MESH,
        )
        copy.start()
        self.started.append(copy)

    def begin(self, h, links=("plus", "minus", "pair")):
        for to in links:
            self._copy(0, 0, h, to)

    def spread(self, h):
        if not self.cross or h % 2 == 1:
            self._copy(0, 1, h, "plus")
        if not self.cross or h % 2 == 0:
            self._copy(0, 1, h, "minus")

    def arrive(self, dr, dp, h):
        ref = self.slot(dr, dp, h)
        place = PLACES[(dr, dp)] * self.parts + h
        pltpu.make_async_remote_copy(
            src_ref=ref,
            dst_ref=ref,
            send_sem=self.send.at[0],
            recv_sem=self.recv.at[place],
            device_id=self.pair,
            device_id_type=MESH,
        ).wait_recv()
        if (dr, dp) == (0, 1):
            if not self.hold:
                self.spread(h)
        elif (dr, h % 2) in ((-1, 0), (1, 1)):
            self._copy(dr, dp, h, "plus" if dr == -1 else "minus")
            if self.cross and dp == 0:
                self._copy(dr, dp, h, "pair")

    def finish(self):
        for copy in self.started:
            copy.wait_send()


def kernel(
    g_hbm, m_hbm, out_ref,
    g_ref, m_ref, xs, xi, xq, xt, ps, rl, mg, r1, keep, s_send, s_recv, gf, sq, rt, ls, ms, mt, zs, zb, zr,
    in_sem, x_send, x_recv, xc_send, xc_recv, xq_send, xq_recv, xq_sem, rl_send, rl_recv, r1_send, r1_recv, r2_send, r2_recv,
    rt_send, rt_recv, l_send, l_recv, lc_send, lc_recv, m_send, m_recv, z_send, z_recv,
):
    row, col = lax.axis_index("row"), lax.axis_index("col")
    c, x, yl = row % 2, (row // 2) % 4, row // 8
    z, yh = col % 4, col // 4

    def device(x_, yl_, c_, yh_, z_):
        return ((yl_ * 4 + x_) * 2 + c_, yh_ * 4 + z_)

    core = device(x, yl, 1 - c, yh, z)
    xp, xm = device((x + 1) % 4, yl, c, yh, z), device((x + 3) % 4, yl, c, yh, z)
    zp, zm = device(x, yl, c, yh, (z + 1) % 4), device(x, yl, c, yh, (z + 3) % 4)
    yp, yq = device(x, 1 - yl, c, yh, z), device(x, yl, c, 1 - yh, z)
    yd = device(x, 1 - yl, c, 1 - yh, z)
    early = yl == yh
    barrier = pltpu.get_barrier_semaphore()
    partners = (core, xp, xm, zp, zm, yp, yq, yd)
    for partner in partners:
        pl.semaphore_signal(barrier, inc=1, device_id=partner, device_id_type=MESH)
    loads = []
    for h in range(2):
        rows = pl.ds(h * HALF, HALF)
        for k, (hbm, ref) in enumerate(((g_hbm, g_ref), (m_hbm, m_ref))):
            load = pltpu.make_async_copy(hbm.at[rows], ref.at[rows], in_sem.at[2 * h + k])
            load.start()
            loads.append(load)

    def remote(src, dst, send, recv, to):
        return pltpu.make_async_remote_copy(
            src_ref=src, dst_ref=dst, send_sem=send, recv_sem=recv, device_id=to, device_id_type=MESH
        )

    def chip_at(dr, dp):
        return ((yl + dp) % 2) * 4 + (x + dr + 4) % 4

    own = chip_at(0, 0)

    gx = Gather(lambda dr, dp, h: xs.at[chip_at(dr, dp), pl.ds(h * HALF, HALF)], xp, xm, yp, x_send, x_recv, False, hold=True)
    mine = pl.ds(pl.multiple_of(c * ROWS, 32), ROWS)
    theirs = pl.ds(pl.multiple_of((1 - c) * ROWS, 32), ROWS)
    for h in range(2):
        rows = pl.ds(h * HALF, HALF)
        loads[2 * h].wait()
        loads[2 * h + 1].wait()
        new = MOMENTUM_RATE * m_ref[rows, :] + g_ref[rows, :]
        low = (g_ref[rows, :] + MOMENTUM_RATE * new).astype(jnp.bfloat16)
        xs[own, rows, :] = low
        if h == 0:
            pl.semaphore_wait(barrier, len(partners))
            gx.begin(0, ("plus", "pair"))
        else:
            gx.begin(1, ("minus", "plus", "pair"))
            gx.begin(0, ("minus",))
        xi[pl.ds(pl.multiple_of(c * ROWS + h * HALF, 32), HALF), :] = low
    swap = remote(xi.at[mine], xi.at[mine], xc_send, xc_recv, core)
    swap.start()
    remote(xi.at[theirs], xi.at[theirs], xc_send, xc_recv, core).wait_recv()
    for k in range(COLS // 128):
        xt[0, k * 128 : (k + 1) * 128, :] = xi[:, k * 128 : (k + 1) * 128].T

    sides = {(0, 0): 1, (0, -1): 1, (0, 1): -1, (1, 0): -1, (1, -1): 1, (1, 1): -1, (0, 2): 1, (1, 2): -1}

    def block_of(i, dr):
        return i * 4 + (x + dr + 4) % 4

    def relay_copy(i, dr):
        block, side = block_of(i, dr), sides[(i, dr)]
        src = ps.at[block, (z + 2) % 4]
        return remote(src, rl.at[block], rl_send.at[block], rl_recv.at[block], zp if side == 1 else zm)

    def piece_copy(i, dr, merged):
        block, side = block_of(i, dr), sides[(i, dr)]
        src = mg.at[block] if merged else ps.at[block, (z - side + 4) % 4]
        to = zp if (side == 1) == merged else zm
        k = int(merged)
        return remote(src, r1.at[block, k], r1_send.at[block, k], r1_recv.at[block, k], to)

    def gram(i, dr, h):
        j, block, side = chip_at(dr, 0), block_of(i, dr), sides[(i, dr)]
        part = jnp.dot(xs[j, h * HALF : (h + 1) * HALF, :], xt[i], preferred_element_type=jnp.float32)
        ps[block, 2 * h : 2 * h + 2] = part.astype(jnp.bfloat16).reshape(2, PIECE, CHIP)

        @pl.when((z + 2) % 4 // 2 == h)
        def _():
            relay_copy(i, dr).start()

        @pl.when((z - side + 4) % 4 // 2 == h)
        def _():
            piece_copy(i, dr, False).start()

    def relay(i, dr):
        block, side = block_of(i, dr), sides[(i, dr)]
        relay_copy(i, dr).wait_recv()
        total = rl[block].astype(jnp.float32) + ps[block, (z + side + 4) % 4].astype(jnp.float32)
        mg[block] = total.astype(jnp.bfloat16)
        piece_copy(i, dr, True).start()

    def sum_copy(i, xj, slot, to):
        return remote(s_send.at[i, xj], s_recv.at[slot, xj], r2_send.at[i, xj], r2_recv.at[slot, xj], to)

    def sum_arrive(slot, xj):
        ref = s_recv.at[slot, xj]
        remote(ref, ref, r2_send.at[0, xj], r2_recv.at[slot, xj], yp).wait_recv()

    def reduce(i, dr):
        block = block_of(i, dr)
        total = ps[block, z].astype(jnp.float32)
        for merged in (False, True):
            piece_copy(i, dr, merged).wait_recv()
            total = total + r1[block, int(merged)].astype(jnp.float32)
        xj = (x + dr + 4) % 4
        if i == 0:

            @pl.when(early)
            def _():
                keep[xj] = total

            @pl.when(jnp.logical_not(early))
            def _():
                s_send[i, xj] = total.astype(jnp.bfloat16)
                sum_copy(i, xj, 0, yq).start()

        else:
            s_send[i, xj] = total.astype(jnp.bfloat16)

            @pl.when(early)
            def _():
                sum_copy(i, xj, 0, yp).start()

            @pl.when(jnp.logical_not(early))
            def _():
                sum_copy(i, xj, 1, yd).start()

    def pass_pair(h):
        rows = pl.ds(h * HALF, HALF)
        src = xs.at[chip_at(0, 1), rows]
        over = remote(src, xq.at[c, rows], xq_send.at[h], xq_recv.at[h], core)
        over.start()
        here = pltpu.make_async_copy(src, xq.at[c, rows], xq_sem.at[h])
        here.start()
        return over, here

    def row_slot(dr, dp, k):
        return rt.at[chip_at(dr, dp), (x + dr + ORDER[k] + 4) % 4]

    def col_slot(lane):
        def slot(dr, dp, k):
            return ls.at[((yh + dp) % 2) * 4 + (x + ORDER[k] + 4) % 4, lane, (z + dr + 4) % 4]

        return slot

    gr = Gather(row_slot, xp, xm, yp, rt_send, rt_recv, True, 4)
    mine_of, theirs_of = col_slot(c), col_slot(1 - c)
    gl = Gather(mine_of, zp, zm, yq, l_send, l_recv, False, 4)
    lanes = []

    def to_core(dr, dp, k):
        place = PLACES[(dr, dp)] * 4 + k
        copy = remote(mine_of(dr, dp, k), mine_of(dr, dp, k), lc_send.at[place], lc_recv.at[place], core)
        copy.start()
        lanes.append(copy)

    def from_core(dr, dp, k):
        place = PLACES[(dr, dp)] * 4 + k
        ref = theirs_of(dr, dp, k)
        remote(ref, ref, lc_send.at[place], lc_recv.at[place], core).wait_recv()

    def arrive_l(dr, dp, k):
        gl.arrive(dr, dp, k)
        to_core(dr, dp, k)

    def finish_sum(k):
        xj = (x + ORDER[k] + 4) % 4
        sum_arrive(0, xj)

        @pl.when(jnp.logical_not(early))
        def _():
            sum_arrive(1, xj)
            keep[xj] = s_recv[1, xj].astype(jnp.float32)

        total = keep[xj] + s_recv[0, xj].astype(jnp.float32)
        gf[xj] = total
        low = total.astype(jnp.bfloat16)
        ls[yh * 4 + xj, c, z] = low
        gl.begin(k)
        rt[own, xj] = low
        gr.begin(k)
        to_core(0, 0, k)

    def near_of(k):
        for arrive in (arrive_l, gr.arrive):
            arrive(-1, 0, k)
            arrive(1, 0, k)
        arrive_l(0, 1, k)
        gr.arrive(0, 1, k)

    def far_of(k):
        for arrive in (gr.arrive, arrive_l):
            arrive(-1, 1, k)
            arrive(1, 1, k)
        arrive_l(2, 0, k)

    near, far = ((-1, 0), (1, 0), (0, 1)), ((-1, 1), (1, 1), (2, 1))
    gram(0, 0, 0)
    gram(0, 0, 1)
    passed = []
    for h in range(2):
        gx.arrive(-1, 0, h)
        gx.arrive(1, 0, 1 - h)
        gx.arrive(0, 1, h)
        passed.append(pass_pair(h))
        gram(0, -1, h)
        gram(0, 1, 1 - h)
        if h == 0:
            relay(0, 0)
        else:
            reduce(0, 0)
    for h in range(2):
        gx.spread(h)
    for h in range(2):
        ref = xq.at[1 - c, pl.ds(h * HALF, HALF)]
        remote(ref, ref, xq_send.at[h], xq_recv.at[h], core).wait_recv()
        passed[h][1].wait()
    for k in range(COLS // 128):
        cols = slice(k * 128, (k + 1) * 128)
        xt[1, cols, :] = xq[:, :, cols].reshape(CHIP, 128).T
    relay(0, -1)
    relay(0, 1)
    for dr in (0, -1, 1):
        for h in range(2):
            gram(1, dr, h)
    for h in range(2):
        gx.arrive(2, 0, h)
    for i in range(2):
        for h in range(2):
            gram(i, 2, h)
    for dr in (0, -1, 1):
        relay(1, dr)
    reduce(0, -1)
    reduce(0, 1)
    reduce(1, 0)
    finish_sum(0)
    relay(0, 2)
    relay(1, 2)
    reduce(1, -1)
    finish_sum(1)
    reduce(1, 1)
    finish_sum(2)
    reduce(0, 2)
    reduce(1, 2)
    near_of(0)
    finish_sum(3)
    near_of(1)
    far_of(0)
    near_of(2)
    far_of(1)
    near_of(3)
    far_of(2)
    far_of(3)
    for k in range(4):
        gr.arrive(2, 0, k)
        gr.arrive(2, 1, k)
    for h in range(2):
        gx.arrive(-1, 1, h)
        gx.arrive(1, 1, h)

    def square(j, rows):
        left = rt[j, rows].reshape(-1, CHIP)
        right = ls[j].reshape(CHIP, CHIP)
        return jnp.dot(left, right, preferred_element_type=jnp.float32)

    for dr in (0, -1, 1, 2):
        for k in range(4):
            from_core(dr, 0, k)
    for h in range(2):
        rows = slice(2 * h, 2 * h + 2)
        total = square(yh * 4, rows)
        for k in range(1, 4):
            total = total + square(yh * 4 + k, rows)
        sq[rows] = total.reshape(2, PIECE, CHIP)
    for k in range(4):
        arrive_l(2, 1, k)
    for dr in (0, -1, 1, 2):
        for k in range(4):
            from_core(dr, 1, k)
    def mix_slot(dr, dp, h):
        return ms.at[pl.ds(((yh + dp) % 2) * 4 + h * 2, 2), (z + dr + 4) % 4]

    gm = Gather(mix_slot, zp, zm, yq, m_send, m_recv, True)
    for h in range(2):
        rows = slice(2 * h, 2 * h + 2)
        total = sq[rows].reshape(HALF, CHIP)
        for k in range(4):
            total = total + square((1 - yh) * 4 + k, rows)
        mixing = COEF_B * gf[rows].reshape(HALF, CHIP) + COEF_C * total
        ms[pl.ds(yh * 4 + 2 * h, 2), z] = mixing.astype(jnp.bfloat16).reshape(2, PIECE, CHIP)
        if h == 0:
            gm.begin(0, ("plus", "pair"))
        else:
            gm.begin(1, ("minus", "plus", "pair"))
            gm.begin(0, ("minus",))

    def turn(dr, dp, slot):
        side, at = ((yh + dp) % 2) * 4, (z + dr + 4) % 4
        mt[slot] = ms[pl.ds(side, 4), at].reshape(ROWS, CHIP).T

    def product(dr, dp, slot, rows, n, first=False):
        side, at = ((yh + dp) % 2) * 4, (z + dr + 4) % 4
        cols = pl.ds(n * 384, 384)
        at_rows = pl.ds(pl.multiple_of(at * PIECE, 16), PIECE)
        right = xs[pl.ds(side, 4), at_rows, cols].reshape(ROWS, 384)
        part = jnp.dot(mt[slot, rows, :], right, preferred_element_type=jnp.float32)
        zs[rows, cols] = part if first else zs[rows, cols] + part

    every = slice(None)
    for h in range(2):
        gm.arrive(-1, 0, h)
        gm.arrive(1, 0, 1 - h)
        gm.arrive(0, 1, h)
    for h in range(2):
        gx.arrive(2, 1, h)
    turn(0, 0, 0)
    for n in range(3):
        product(0, 0, 0, every, n, True)
    for h in range(2):
        gm.arrive(-1, 1, h)
        gm.arrive(1, 1, 1 - h)
    for h in range(2):
        gm.arrive(2, 0, h)
    for place in near + ((2, 0),):
        turn(*place, 0)
        for n in range(3):
            product(*place, 0, every, n)
    for k, place in enumerate(far):
        if place == (2, 1):
            for h in range(2):
                gm.arrive(*place, h)
        turn(*place, k)
    last = []
    for n in range(3):
        for k, place in enumerate(far):
            product(*place, k, theirs, n)
        zb[n] = zs[theirs, pl.ds(n * 384, 384)].astype(jnp.bfloat16)
        last.append(remote(zb.at[n], zr.at[n], z_send.at[n], z_recv.at[n], core))
        last[n].start()
    for n in range(3):
        for k, place in enumerate(far):
            product(*place, k, mine, n)
        last[n].wait_recv()
        cols = pl.ds(n * 384, 384)
        out_ref[:, cols] = zs[mine, cols] + zr[n].astype(jnp.float32)

    for copy in lanes + [swap] + last + [over for over, _ in passed]:
        copy.wait_send()
    for gather in (gx, gr, gl, gm):
        gather.finish()
    for place in sides:
        relay_copy(*place).wait_send()
        piece_copy(*place, False).wait_send()
        piece_copy(*place, True).wait_send()
    for xj in range(4):
        sum_copy(1, xj, 0, yp).wait_send()

        @pl.when(jnp.logical_not(early))
        def _(xj=xj):
            sum_copy(0, xj, 0, yq).wait_send()


def local(gradient, momentum):
    half, full = jnp.bfloat16, jnp.float32
    dma = pltpu.SemaphoreType.DMA
    product = pl.pallas_call(
        kernel,
        out_shape=jax.ShapeDtypeStruct((ROWS, COLS), full),
        in_specs=[pl.BlockSpec(memory_space=pl.ANY)] * 2,
        out_specs=pl.BlockSpec(memory_space=pltpu.VMEM),
        scratch_shapes=[
            pltpu.VMEM((ROWS, COLS), full),
            pltpu.VMEM((ROWS, COLS), full),
            pltpu.VMEM((8, ROWS, COLS), half),
            pltpu.VMEM((CHIP, COLS), half),
            pltpu.VMEM((2, ROWS, COLS), half),
            pltpu.VMEM((2, COLS, CHIP), half),
            pltpu.VMEM((8, 4, PIECE, CHIP), half),
            pltpu.VMEM((8, PIECE, CHIP), half),
            pltpu.VMEM((8, PIECE, CHIP), half),
            pltpu.VMEM((8, 2, PIECE, CHIP), half),
            pltpu.VMEM((4, PIECE, CHIP), full),
            pltpu.VMEM((2, 4, PIECE, CHIP), half),
            pltpu.VMEM((2, 4, PIECE, CHIP), half),
            pltpu.VMEM((4, PIECE, CHIP), full),
            pltpu.VMEM((4, PIECE, CHIP), full),
            pltpu.VMEM((8, 4, PIECE, CHIP), half),
            pltpu.VMEM((8, 2, 4, PIECE, CHIP), half),
            pltpu.VMEM((8, 4, PIECE, CHIP), half),
            pltpu.VMEM((3, CHIP, ROWS), half),
            pltpu.VMEM((CHIP, COLS), full),
            pltpu.VMEM((3, ROWS, 384), half),
            pltpu.VMEM((3, ROWS, 384), half),
            dma((4,)), dma((14,)), dma((16,)), dma(()), dma(()), dma((2,)), dma((2,)), dma((2,)),
            dma((8,)), dma((8,)), dma((8, 2)), dma((8, 2)), dma((2, 4)), dma((2, 4)),
            dma((28,)), dma((32,)), dma((28,)), dma((32,)),
            dma((32,)), dma((32,)), dma((14,)), dma((16,)),
            dma((3,)), dma((3,)),
        ],
        name="muon",
        compiler_params=pltpu.CompilerParams(
            collective_id=0, has_side_effects=True, vmem_limit_bytes=60 * 2**20
        ),
    )(gradient, momentum)
    new_momentum = MOMENTUM_RATE * momentum + gradient
    nesterov = gradient + MOMENTUM_RATE * new_momentum
    return new_momentum, SCALE * (COEF_A * nesterov + product)


def solution(mesh):
    specs = (P("row", "col"), P("row", "col"))
    return jax.shard_map(local, mesh=mesh, in_specs=specs, out_specs=specs, check_vma=False)
```

```python
import math

import jax
import jax.numpy as jnp
from jax import lax
from jax.experimental import pallas as pl
from jax.experimental.pallas import tpu as pltpu
from jax.sharding import PartitionSpec as P

HIDDEN_SIZE = 9216
MOMENTUM_RATE = 0.95
COEF_A = 3.4445
COEF_B = -4.775
COEF_C = 2.0315
SCALE = math.sqrt(HIDDEN_SIZE)

MESH = pl.DeviceIdType.MESH
ROWS = 320
COLS = 1152
HALF = ROWS // 2
CHIP = 2 * ROWS
PIECE = ROWS // 4
ORDER = (0, -1, 1, 2)
PLACES = {(0, 0): 0, (-1, 0): 1, (1, 0): 2, (2, 0): 3, (0, 1): 4, (-1, 1): 5, (1, 1): 6, (2, 1): 7}


class Gather:
    def __init__(self, slot, plus, minus, pair, send, recv, mode, parts=2, hold=False):
        self.slot, self.plus, self.minus, self.pair = slot, plus, minus, pair
        self.send, self.recv, self.mode = send, recv, mode
        self.parts, self.hold, self.started = parts, hold, []

    def _copy(self, dr, dp, h, to):
        device, ring, other = {"plus": (self.plus, -1, 0), "minus": (self.minus, 1, 0), "pair": (self.pair, 0, 1)}[to]
        there = dr + ring
        there = 2 if there == -2 else there
        place = PLACES[(there, (dp + other) % 2)] * self.parts + h
        ref = self.slot(dr, dp, h)
        copy = pltpu.make_async_remote_copy(
            src_ref=ref,
            dst_ref=ref,
            send_sem=self.send.at[len(self.started)],
            recv_sem=self.recv.at[place],
            device_id=device,
            device_id_type=MESH,
        )
        copy.start()
        self.started.append(copy)

    def begin(self, h, links=("plus", "minus", "pair")):
        for to in links:
            self._copy(0, 0, h, to)

    def spread(self, h):
        if self.mode != "cross" or h % 2 == 1:
            self._copy(0, 1, h, "plus")
        if self.mode != "cross" or h % 2 == 0:
            self._copy(0, 1, h, "minus")

    def arrive(self, dr, dp, h):
        ref = self.slot(dr, dp, h)
        place = PLACES[(dr, dp)] * self.parts + h
        pltpu.make_async_remote_copy(
            src_ref=ref,
            dst_ref=ref,
            send_sem=self.send.at[0],
            recv_sem=self.recv.at[place],
            device_id=self.pair,
            device_id_type=MESH,
        ).wait_recv()
        if (dr, dp) == (0, 1):
            if not self.hold:
                self.spread(h)
        elif (dr, h % 2) in ((-1, 0), (1, 1)) and (dp == 0 or self.mode != "late"):
            self._copy(dr, dp, h, "plus" if dr == -1 else "minus")
            if self.mode == "cross" and dp == 0:
                self._copy(dr, dp, h, "pair")
        elif (dr, dp) == (2, 0) and self.mode == "late":
            self._copy(dr, dp, h, "pair")

    def finish(self):
        for copy in self.started:
            copy.wait_send()


def kernel(
    g_hbm, m_hbm, out_ref,
    g_ref, m_ref, xs, xi, xq, xt, ps, r1, keep, s_send, s_recv, gf, sq, rt, ls, ms, mt, zs, zb, zr,
    in_sem, x_send, x_recv, xc_send, xc_recv, xq_send, xq_recv, xq_sem, r1_send, r1_recv, r2_send, r2_recv,
    rt_send, rt_recv, l_send, l_recv, lc_send, lc_recv, m_send, m_recv, z_send, z_recv,
):
    row, col = lax.axis_index("row"), lax.axis_index("col")
    c, x, yl = row % 2, (row // 2) % 4, row // 8
    z, yh = col % 4, col // 4

    def device(x_, yl_, c_, yh_, z_):
        return ((yl_ * 4 + x_) * 2 + c_, yh_ * 4 + z_)

    core = device(x, yl, 1 - c, yh, z)
    xp, xm = device((x + 1) % 4, yl, c, yh, z), device((x + 3) % 4, yl, c, yh, z)
    zp, zm = device(x, yl, c, yh, (z + 1) % 4), device(x, yl, c, yh, (z + 3) % 4)
    z2 = device(x, yl, c, yh, (z + 2) % 4)
    yp, yq = device(x, 1 - yl, c, yh, z), device(x, yl, c, 1 - yh, z)
    yd = device(x, 1 - yl, c, 1 - yh, z)
    barrier = pltpu.get_barrier_semaphore()
    partners = (core, xp, xm, zp, zm, z2, yp, yq, yd)
    for partner in partners:
        pl.semaphore_signal(barrier, inc=1, device_id=partner, device_id_type=MESH)
    loads = []
    for h in range(2):
        rows = pl.ds(h * HALF, HALF)
        for k, (hbm, ref) in enumerate(((g_hbm, g_ref), (m_hbm, m_ref))):
            load = pltpu.make_async_copy(hbm.at[rows], ref.at[rows], in_sem.at[2 * h + k])
            load.start()
            loads.append(load)

    def remote(src, dst, send, recv, to):
        return pltpu.make_async_remote_copy(
            src_ref=src, dst_ref=dst, send_sem=send, recv_sem=recv, device_id=to, device_id_type=MESH
        )

    def chip_at(dr, dp):
        return ((yl + dp) % 2) * 4 + (x + dr + 4) % 4

    own = chip_at(0, 0)

    gx = Gather(lambda dr, dp, h: xs.at[chip_at(dr, dp), pl.ds(h * HALF, HALF)], xp, xm, yp, x_send, x_recv, "ring", hold=True)
    mine = pl.ds(pl.multiple_of(c * ROWS, 32), ROWS)
    theirs = pl.ds(pl.multiple_of((1 - c) * ROWS, 32), ROWS)
    for h in range(2):
        rows = pl.ds(h * HALF, HALF)
        loads[2 * h].wait()
        loads[2 * h + 1].wait()
        new = MOMENTUM_RATE * m_ref[rows, :] + g_ref[rows, :]
        low = (g_ref[rows, :] + MOMENTUM_RATE * new).astype(jnp.bfloat16)
        xs[own, rows, :] = low
        if h == 0:
            pl.semaphore_wait(barrier, len(partners))
            gx.begin(0, ("plus", "pair"))
        else:
            gx.begin(1, ("minus", "plus", "pair"))
            gx.begin(0, ("minus",))
        xi[pl.ds(pl.multiple_of(c * ROWS + h * HALF, 32), HALF), :] = low
    swap = remote(xi.at[mine], xi.at[mine], xc_send, xc_recv, core)
    swap.start()
    remote(xi.at[theirs], xi.at[theirs], xc_send, xc_recv, core).wait_recv()
    for k in range(COLS // 128):
        xt[0, k * 128 : (k + 1) * 128, :] = xi[:, k * 128 : (k + 1) * 128].T

    def block_of(i, dr):
        return i * 4 + (x + dr + 4) % 4

    def piece_copy(block, dz):
        src = ps.at[block, (z + dz) % 4]
        k = dz - 1
        return remote(src, r1.at[block, k], r1_send.at[block, k], r1_recv.at[block, k], (zp, z2, zm)[k])

    def gram(i, dr, h):
        j, block = chip_at(dr, 0), block_of(i, dr)
        part = jnp.dot(xs[j, h * HALF : (h + 1) * HALF, :], xt[i], preferred_element_type=jnp.float32)
        ps[block, 2 * h : 2 * h + 2] = part.astype(jnp.bfloat16).reshape(2, PIECE, CHIP)
        for dz in (2, 1, 3):

            @pl.when((z + dz) % 4 // 2 == h)
            def _(dz=dz):
                piece_copy(block, dz).start()

    def sum_copy(i, xj, slot):
        to = (yq, yp, yd)[slot]
        return remote(s_send.at[i, xj], s_recv.at[slot, xj], r2_send.at[slot, xj], r2_recv.at[slot, xj], to)

    def reduce(i, dr):
        block = block_of(i, dr)
        total = ps[block, z].astype(jnp.float32)
        for dz in (1, 3, 2):
            piece_copy(block, dz).wait_recv()
            total = total + r1[block, dz - 1].astype(jnp.float32)
        xj = (x + dr + 4) % 4
        s_send[i, xj] = total.astype(jnp.bfloat16)
        if i == 0:
            keep[xj] = total
            sum_copy(0, xj, 0).start()
        else:
            sum_copy(1, xj, 1).start()
            sum_copy(1, xj, 2).start()

    def pass_pair(h):
        rows = pl.ds(h * HALF, HALF)
        src = xs.at[chip_at(0, 1), rows]
        over = remote(src, xq.at[c, rows], xq_send.at[h], xq_recv.at[h], core)
        over.start()
        here = pltpu.make_async_copy(src, xq.at[c, rows], xq_sem.at[h])
        here.start()
        return over, here

    def row_block(dr, dp, k):
        at, side = (x + dr + 4) % 4, (yl + dp + k // 2) % 2
        return side, (at + 2 * (k % 2) + 3 * ((at + yh) % 2)) % 4

    def row_slot(dr, dp, k):
        side, xj = row_block(dr, dp, k)
        return rt.at[chip_at(dr, dp), side * 2 + xj // 2]

    gr = Gather(row_slot, xp, xm, yp, rt_send, rt_recv, "cross", 4)
    parts = ((0, 0), (0, -1), (0, 1), (1, 0), (1, -1), (0, 2), (1, 1), (1, 2))
    lanes, l_sent = [], []

    def l_slot(n, dz, lane):
        i, dr = parts[n]
        return ls.at[chip_at(dr, i), lane, (z + dz + 4) % 4]

    def l_copy(n, dz, side):
        there = {(0, 1): -1, (0, -1): 1, (-1, 1): 2, (1, -1): 2}[(dz, side)]
        ref = l_slot(n, dz, c)
        to = zp if side == 1 else zm
        copy = remote(ref, ref, l_send.at[len(l_sent)], l_recv.at[(there % 4) * 8 + n], to)
        copy.start()
        l_sent.append(copy)

    def to_core(n, dz):
        place = (dz % 4) * 8 + n
        copy = remote(l_slot(n, dz, c), l_slot(n, dz, c), lc_send.at[place], lc_recv.at[place], core)
        copy.start()
        lanes.append(copy)

    def from_core(n, dz):
        place = (dz % 4) * 8 + n
        ref = l_slot(n, dz, 1 - c)
        remote(ref, ref, lc_send.at[place], lc_recv.at[place], core).wait_recv()

    def l_arrive(n, dz):
        ref = l_slot(n, dz, c)
        remote(ref, ref, l_send.at[0], l_recv.at[(dz % 4) * 8 + n], zp).wait_recv()
        if dz == -1 and n % 2 == 0:
            l_copy(n, -1, 1)
        if dz == 1 and n % 2 == 1:
            l_copy(n, 1, -1)
        to_core(n, dz)

    def l_near(n):
        l_arrive(n, -1)
        l_arrive(n, 1)

    def finish_sum(n):
        i, dr = parts[n]
        xj, j = (x + dr + 4) % 4, chip_at(dr, i)
        for slot in (1, 2) if i else (0,):
            ref = s_recv.at[slot, xj]
            remote(ref, ref, r2_send.at[slot, xj], r2_recv.at[slot, xj], yp).wait_recv()
        if i:
            total = s_recv[1, xj].astype(jnp.float32) + s_recv[2, xj].astype(jnp.float32)
        else:
            total = keep[xj] + s_recv[0, xj].astype(jnp.float32)
        gf[j] = total
        ls[j, c, z] = total.astype(jnp.bfloat16)
        l_copy(n, 0, 1)
        l_copy(n, 0, -1)
        to_core(n, 0)

    def r_begin(k):
        side, xj = row_block(0, 0, k)
        rt[own, side * 2 + xj // 2] = ls[side * 4 + xj, c, z]
        gr.begin(k)

    def r_near(k):
        gr.arrive(-1, 0, k)
        gr.arrive(1, 0, k)
        gr.arrive(0, 1, k)

    def r_far(k):
        gr.arrive(-1, 1, k)
        gr.arrive(1, 1, k)

    near, far = ((-1, 0), (1, 0), (0, 1)), ((-1, 1), (1, 1), (2, 1))
    gram(0, 0, 0)
    gram(0, 0, 1)
    passed = []
    for h in range(2):
        gx.arrive(-1, 0, h)
        gx.arrive(1, 0, 1 - h)
        gx.arrive(0, 1, h)
        passed.append(pass_pair(h))
        gram(0, -1, h)
        gram(0, 1, 1 - h)
        if h == 0:
            reduce(0, 0)
    for h in range(2):
        gx.spread(h)
    finish_sum(0)
    for h in range(2):
        ref = xq.at[1 - c, pl.ds(h * HALF, HALF)]
        remote(ref, ref, xq_send.at[h], xq_recv.at[h], core).wait_recv()
        passed[h][1].wait()
    for k in range(COLS // 128):
        cols = slice(k * 128, (k + 1) * 128)
        xt[1, cols, :] = xq[:, :, cols].reshape(CHIP, 128).T
    for dr in (0, -1, 1):
        for h in range(2):
            gram(1, dr, h)
    for h in range(2):
        gx.arrive(2, 0, h)
    for i in range(2):
        for h in range(2):
            gram(i, 2, h)
    reduce(0, -1)
    reduce(0, 1)
    reduce(1, 0)
    reduce(1, -1)
    reduce(1, 1)
    l_near(0)
    finish_sum(1)
    finish_sum(2)
    r_begin(0)
    reduce(0, 2)
    reduce(1, 2)
    finish_sum(3)
    finish_sum(4)
    r_begin(2)
    l_near(1)
    l_near(2)
    finish_sum(5)
    r_begin(1)
    finish_sum(6)
    finish_sum(7)
    r_begin(3)
    l_near(3)
    l_near(4)
    r_near(0)
    l_near(5)
    r_near(2)
    l_near(6)
    r_near(1)
    r_far(0)
    r_far(2)
    l_near(7)
    r_near(3)
    r_far(1)
    r_far(3)
    for n in range(8):
        l_arrive(n, 2)
    for k in range(4):
        gr.arrive(2, 0, k)
        gr.arrive(2, 1, k)
    for h in range(2):
        gx.arrive(-1, 1, h)
        gx.arrive(1, 1, h)

    def square(j, rows):
        left = rt[j, rows].reshape(-1, CHIP)
        right = ls[j].reshape(CHIP, CHIP)
        return jnp.dot(left, right, preferred_element_type=jnp.float32)

    for n in range(8):
        for dz in (0, -1, 1, 2):
            if parts[n][0] == 0:
                from_core(n, dz)
    for h in range(2):
        rows = slice(2 * h, 2 * h + 2)
        total = square(yl * 4, rows)
        for k in range(1, 4):
            total = total + square(yl * 4 + k, rows)
        sq[rows] = total.reshape(2, PIECE, CHIP)
    for n in range(8):
        for dz in (0, -1, 1, 2):
            if parts[n][0] == 1:
                from_core(n, dz)

    def mix_slot(dr, dp, h):
        return ms.at[h, :, (yh + dp) % 2, (z + dr + 4) % 4]

    gm = Gather(mix_slot, zp, zm, yq, m_send, m_recv, "cross")
    for h in range(2):
        rows = slice(2 * h, 2 * h + 2)
        total = sq[rows].reshape(HALF, CHIP)
        for k in range(4):
            total = total + square((1 - yl) * 4 + k, rows)
        gram_rows = jnp.concatenate([gf[h * 4 + yh], gf[h * 4 + 2 + yh]], axis=0)
        mixing = (COEF_B * gram_rows + COEF_C * total).astype(jnp.bfloat16)
        ms[h, 0, yh, z] = mixing[:PIECE]
        ms[h, 1, yh, z] = mixing[PIECE:]
        if h == 0:
            gm.begin(0, ("plus", "pair"))
        else:
            gm.begin(1, ("minus", "plus", "pair"))
            gm.begin(0, ("minus",))

    def turn(dr, dp, slot):
        mt[slot] = ms[:, :, (yh + dp) % 2, (z + dr + 4) % 4].reshape(ROWS, CHIP).T

    def product(dr, dp, slot, rows, n, first=False):
        side, at = (yh + dp) % 2, (z + dr + 4) % 4
        cols = pl.ds(n * 384, 384)
        at_rows = pl.ds(pl.multiple_of(at * PIECE, 16), PIECE)
        right = jnp.concatenate([xs[2 * k + side, at_rows, cols] for k in range(4)], axis=0)
        part = jnp.dot(mt[slot, rows, :], right, preferred_element_type=jnp.float32)
        zs[rows, cols] = part if first else zs[rows, cols] + part

    every = slice(None)
    for h in range(2):
        gm.arrive(-1, 0, h)
        gm.arrive(1, 0, 1 - h)
        gm.arrive(0, 1, h)
    for h in range(2):
        gx.arrive(2, 1, h)
    turn(0, 0, 0)
    for n in range(3):
        product(0, 0, 0, every, n, True)
    for h in range(2):
        gm.arrive(-1, 1, h)
        gm.arrive(1, 1, 1 - h)
    for h in range(2):
        gm.arrive(2, 0, h)
    for place in near + ((2, 0),):
        turn(*place, 0)
        for n in range(3):
            product(*place, 0, every, n)
    for k, place in enumerate(far):
        if place == (2, 1):
            for h in range(2):
                gm.arrive(*place, h)
        turn(*place, k)
    last = []
    for n in range(3):
        for k, place in enumerate(far):
            product(*place, k, theirs, n)
        zb[n] = zs[theirs, pl.ds(n * 384, 384)].astype(jnp.bfloat16)
        last.append(remote(zb.at[n], zr.at[n], z_send.at[n], z_recv.at[n], core))
        last[n].start()
    for n in range(3):
        for k, place in enumerate(far):
            product(*place, k, mine, n)
        last[n].wait_recv()
        cols = pl.ds(n * 384, 384)
        out_ref[:, cols] = zs[mine, cols] + zr[n].astype(jnp.float32)

    for copy in lanes + l_sent + [swap] + last + [over for over, _ in passed]:
        copy.wait_send()
    for gather in (gx, gr, gm):
        gather.finish()
    for block in range(8):
        for dz in (1, 2, 3):
            piece_copy(block, dz).wait_send()
    for xj in range(4):
        for slot in range(3):
            sum_copy(min(slot, 1), xj, slot).wait_send()


def local(gradient, momentum):
    half, full = jnp.bfloat16, jnp.float32
    dma = pltpu.SemaphoreType.DMA
    product = pl.pallas_call(
        kernel,
        out_shape=jax.ShapeDtypeStruct((ROWS, COLS), full),
        in_specs=[pl.BlockSpec(memory_space=pl.ANY)] * 2,
        out_specs=pl.BlockSpec(memory_space=pltpu.VMEM),
        scratch_shapes=[
            pltpu.VMEM((ROWS, COLS), full),
            pltpu.VMEM((ROWS, COLS), full),
            pltpu.VMEM((8, ROWS, COLS), half),
            pltpu.VMEM((CHIP, COLS), half),
            pltpu.VMEM((2, ROWS, COLS), half),
            pltpu.VMEM((2, COLS, CHIP), half),
            pltpu.VMEM((8, 4, PIECE, CHIP), half),
            pltpu.VMEM((8, 3, PIECE, CHIP), half),
            pltpu.VMEM((4, PIECE, CHIP), full),
            pltpu.VMEM((2, 4, PIECE, CHIP), half),
            pltpu.VMEM((3, 4, PIECE, CHIP), half),
            pltpu.VMEM((8, PIECE, CHIP), full),
            pltpu.VMEM((4, PIECE, CHIP), full),
            pltpu.VMEM((8, 4, PIECE, CHIP), half),
            pltpu.VMEM((8, 2, 4, PIECE, CHIP), half),
            pltpu.VMEM((2, 2, 2, 4, PIECE, CHIP), half),
            pltpu.VMEM((3, CHIP, ROWS), half),
            pltpu.VMEM((CHIP, COLS), full),
            pltpu.VMEM((3, ROWS, 384), half),
            pltpu.VMEM((3, ROWS, 384), half),
            dma((4,)), dma((14,)), dma((16,)), dma(()), dma(()), dma((2,)), dma((2,)), dma((2,)),
            dma((8, 3)), dma((8, 3)), dma((3, 4)), dma((3, 4)),
            dma((28,)), dma((32,)), dma((28,)), dma((32,)),
            dma((32,)), dma((32,)), dma((14,)), dma((16,)),
            dma((3,)), dma((3,)),
        ],
        name="muon",
        compiler_params=pltpu.CompilerParams(
            collective_id=0, has_side_effects=True, vmem_limit_bytes=60 * 2**20
        ),
    )(gradient, momentum)
    new_momentum = MOMENTUM_RATE * momentum + gradient
    nesterov = gradient + MOMENTUM_RATE * new_momentum
    return new_momentum, SCALE * (COEF_A * nesterov + product)


def solution(mesh):
    specs = (P("row", "col"), P("row", "col"))
    return jax.shard_map(local, mesh=mesh, in_specs=specs, out_specs=specs, check_vma=False)
```

```python
import math

import jax
import jax.numpy as jnp
from jax import lax
from jax.experimental import pallas as pl
from jax.experimental.pallas import tpu as pltpu
from jax.sharding import PartitionSpec as P

HIDDEN_SIZE = 9216
MOMENTUM_RATE = 0.95
COEF_A = 3.4445
COEF_B = -4.775
COEF_C = 2.0315
SCALE = math.sqrt(HIDDEN_SIZE)

MESH = pl.DeviceIdType.MESH
ROWS = 320
COLS = 1152
HALF = ROWS // 2
CHIP = 2 * ROWS
PIECE = ROWS // 4
RELAY = {(0, 1): 1, (1, -1): 1, (1, 1): -1, (0, 2): 1, (1, 2): -1}
PLACES = {(0, 0): 0, (-1, 0): 1, (1, 0): 2, (2, 0): 3, (0, 1): 4, (-1, 1): 5, (1, 1): 6, (2, 1): 7}


class Gather:
    def __init__(self, slot, plus, minus, pair, send, recv, mode, parts=2, hold=False):
        self.slot, self.plus, self.minus, self.pair = slot, plus, minus, pair
        self.send, self.recv, self.mode = send, recv, mode
        self.parts, self.hold, self.started = parts, hold, []

    def _copy(self, dr, dp, h, to):
        device, ring, other = {"plus": (self.plus, -1, 0), "minus": (self.minus, 1, 0), "pair": (self.pair, 0, 1)}[to]
        there = dr + ring
        there = 2 if there == -2 else there
        place = PLACES[(there, (dp + other) % 2)] * self.parts + h
        ref = self.slot(dr, dp, h)
        copy = pltpu.make_async_remote_copy(
            src_ref=ref,
            dst_ref=ref,
            send_sem=self.send.at[len(self.started)],
            recv_sem=self.recv.at[place],
            device_id=device,
            device_id_type=MESH,
        )
        copy.start()
        self.started.append(copy)

    def begin(self, h, links=("plus", "minus", "pair")):
        for to in links:
            self._copy(0, 0, h, to)

    def spread(self, h):
        if self.mode != "cross" or h % 2 == 1:
            self._copy(0, 1, h, "plus")
        if self.mode != "cross" or h % 2 == 0:
            self._copy(0, 1, h, "minus")

    def arrive(self, dr, dp, h):
        ref = self.slot(dr, dp, h)
        place = PLACES[(dr, dp)] * self.parts + h
        pltpu.make_async_remote_copy(
            src_ref=ref,
            dst_ref=ref,
            send_sem=self.send.at[0],
            recv_sem=self.recv.at[place],
            device_id=self.pair,
            device_id_type=MESH,
        ).wait_recv()
        if (dr, dp) == (0, 1):
            if not self.hold:
                self.spread(h)
        elif (dr, h % 2) in ((-1, 0), (1, 1)) and (dp == 0 or self.mode != "late"):
            self._copy(dr, dp, h, "plus" if dr == -1 else "minus")
            if self.mode == "cross" and dp == 0:
                self._copy(dr, dp, h, "pair")
        elif (dr, dp) == (2, 0) and self.mode == "late":
            self._copy(dr, dp, h, "pair")

    def finish(self):
        for copy in self.started:
            copy.wait_send()


def kernel(
    g_hbm, m_hbm, out_ref,
    g_ref, m_ref, xs, xi, xq, xt, ps, rl, mg, r1, keep, s_send, s_recv, gf, sq, rt, ls, ms, mt, zs, zb, zr,
    in_sem, x_send, x_recv, xc_send, xc_recv, xq_send, xq_recv, xq_sem, rl_send, rl_recv, r1_send, r1_recv, r2_send, r2_recv,
    rt_send, rt_recv, l_send, l_recv, lc_send, lc_recv, m_send, m_recv, z_send, z_recv,
):
    row, col = lax.axis_index("row"), lax.axis_index("col")
    c, x, yl = row % 2, (row // 2) % 4, row // 8
    z, yh = col % 4, col // 4

    def device(x_, yl_, c_, yh_, z_):
        return ((yl_ * 4 + x_) * 2 + c_, yh_ * 4 + z_)

    core = device(x, yl, 1 - c, yh, z)
    xp, xm = device((x + 1) % 4, yl, c, yh, z), device((x + 3) % 4, yl, c, yh, z)
    zp, zm = device(x, yl, c, yh, (z + 1) % 4), device(x, yl, c, yh, (z + 3) % 4)
    z2 = device(x, yl, c, yh, (z + 2) % 4)
    yp, yq = device(x, 1 - yl, c, yh, z), device(x, yl, c, 1 - yh, z)
    yd = device(x, 1 - yl, c, 1 - yh, z)
    barrier = pltpu.get_barrier_semaphore()
    partners = (core, xp, xm, zp, zm, z2, yp, yq, yd)
    for partner in partners:
        pl.semaphore_signal(barrier, inc=1, device_id=partner, device_id_type=MESH)
    loads = []
    for h in range(2):
        rows = pl.ds(h * HALF, HALF)
        for k, (hbm, ref) in enumerate(((g_hbm, g_ref), (m_hbm, m_ref))):
            load = pltpu.make_async_copy(hbm.at[rows], ref.at[rows], in_sem.at[2 * h + k])
            load.start()
            loads.append(load)

    def remote(src, dst, send, recv, to):
        return pltpu.make_async_remote_copy(
            src_ref=src, dst_ref=dst, send_sem=send, recv_sem=recv, device_id=to, device_id_type=MESH
        )

    def chip_at(dr, dp):
        return ((yl + dp) % 2) * 4 + (x + dr + 4) % 4

    own = chip_at(0, 0)

    gx = Gather(lambda dr, dp, h: xs.at[chip_at(dr, dp), pl.ds(h * HALF, HALF)], xp, xm, yp, x_send, x_recv, "ring", hold=True)
    mine = pl.ds(pl.multiple_of(c * ROWS, 32), ROWS)
    theirs = pl.ds(pl.multiple_of((1 - c) * ROWS, 32), ROWS)
    for h in range(2):
        rows = pl.ds(h * HALF, HALF)
        loads[2 * h].wait()
        loads[2 * h + 1].wait()
        new = MOMENTUM_RATE * m_ref[rows, :] + g_ref[rows, :]
        low = (g_ref[rows, :] + MOMENTUM_RATE * new).astype(jnp.bfloat16)
        xs[own, rows, :] = low
        if h == 0:
            pl.semaphore_wait(barrier, len(partners))
            gx.begin(0, ("plus", "pair"))
        else:
            gx.begin(1, ("minus", "plus", "pair"))
            gx.begin(0, ("minus",))
        xi[pl.ds(pl.multiple_of(c * ROWS + h * HALF, 32), HALF), :] = low
    swap = remote(xi.at[mine], xi.at[mine], xc_send, xc_recv, core)
    swap.start()
    remote(xi.at[theirs], xi.at[theirs], xc_send, xc_recv, core).wait_recv()
    for k in range(COLS // 128):
        xt[0, k * 128 : (k + 1) * 128, :] = xi[:, k * 128 : (k + 1) * 128].T

    def block_of(i, dr):
        return i * 4 + (x + dr + 4) % 4

    def piece_copy(block, dz, src=None):
        src = ps.at[block, (z + dz) % 4] if src is None else src
        k = dz - 1
        return remote(src, r1.at[block, k], r1_send.at[block, k], r1_recv.at[block, k], (zp, z2, zm)[k])

    def relay_copy(i, dr):
        block = block_of(i, dr)
        to = zp if RELAY[(i, dr)] == 1 else zm
        return remote(ps.at[block, (z + 2) % 4], rl.at[block], rl_send.at[block], rl_recv.at[block], to)

    def pieces_of(i, dr):
        block = block_of(i, dr)
        if (i, dr) not in RELAY:
            return [(dz, piece_copy(block, dz)) for dz in (2, 1, 3)]
        back = 4 - RELAY[(i, dr)] if RELAY[(i, dr)] == 1 else 1
        return [(2, relay_copy(i, dr)), (back, piece_copy(block, back))]

    def gram(i, dr, h):
        j, block = chip_at(dr, 0), block_of(i, dr)
        part = jnp.dot(xs[j, h * HALF : (h + 1) * HALF, :], xt[i], preferred_element_type=jnp.float32)
        ps[block, 2 * h : 2 * h + 2] = part.astype(jnp.bfloat16).reshape(2, PIECE, CHIP)
        for dz, copy in pieces_of(i, dr):

            @pl.when((z + dz) % 4 // 2 == h)
            def _(copy=copy):
                copy.start()

    def onward(i, dr):
        block, dz = block_of(i, dr), RELAY[(i, dr)] % 4
        return piece_copy(block, dz, mg.at[block])

    def relay(i, dr):
        block = block_of(i, dr)
        relay_copy(i, dr).wait_recv()
        total = rl[block].astype(jnp.float32) + ps[block, (z + RELAY[(i, dr)] + 4) % 4].astype(jnp.float32)
        mg[block] = total.astype(jnp.bfloat16)
        onward(i, dr).start()

    def sum_copy(i, xj, slot):
        to = (yq, yp, yd)[slot]
        return remote(s_send.at[i, xj], s_recv.at[slot, xj], r2_send.at[slot, xj], r2_recv.at[slot, xj], to)

    def reduce(i, dr):
        block = block_of(i, dr)
        total = ps[block, z].astype(jnp.float32)
        for dz in (1, 3) if (i, dr) in RELAY else (1, 3, 2):
            piece_copy(block, dz).wait_recv()
            total = total + r1[block, dz - 1].astype(jnp.float32)
        xj = (x + dr + 4) % 4
        s_send[i, xj] = total.astype(jnp.bfloat16)
        if i == 0:
            keep[xj] = total
            sum_copy(0, xj, 0).start()
        else:
            sum_copy(1, xj, 1).start()
            sum_copy(1, xj, 2).start()

    def pass_pair(h):
        rows = pl.ds(h * HALF, HALF)
        src = xs.at[chip_at(0, 1), rows]
        over = remote(src, xq.at[c, rows], xq_send.at[h], xq_recv.at[h], core)
        over.start()
        here = pltpu.make_async_copy(src, xq.at[c, rows], xq_sem.at[h])
        here.start()
        return over, here

    def row_block(dr, dp, k):
        at, side = (x + dr + 4) % 4, (yl + dp + k // 2) % 2
        return side, (at + 2 * (k % 2) + 3 * ((at + yh) % 2)) % 4

    def row_slot(dr, dp, k):
        side, xj = row_block(dr, dp, k)
        return rt.at[chip_at(dr, dp), side * 2 + xj // 2]

    gr = Gather(row_slot, xp, xm, yp, rt_send, rt_recv, "cross", 4)
    parts = ((0, 0), (0, -1), (0, 1), (1, 0), (1, -1), (0, 2), (1, 1), (1, 2))
    lanes, l_sent = [], []

    def l_slot(n, dz, lane):
        i, dr = parts[n]
        return ls.at[chip_at(dr, i), lane, (z + dz + 4) % 4]

    def l_copy(n, dz, side):
        there = {(0, 1): -1, (0, -1): 1, (-1, 1): 2, (1, -1): 2}[(dz, side)]
        ref = l_slot(n, dz, c)
        to = zp if side == 1 else zm
        copy = remote(ref, ref, l_send.at[len(l_sent)], l_recv.at[(there % 4) * 8 + n], to)
        copy.start()
        l_sent.append(copy)

    def to_core(n, dz):
        place = (dz % 4) * 8 + n
        copy = remote(l_slot(n, dz, c), l_slot(n, dz, c), lc_send.at[place], lc_recv.at[place], core)
        copy.start()
        lanes.append(copy)

    def from_core(n, dz):
        place = (dz % 4) * 8 + n
        ref = l_slot(n, dz, 1 - c)
        remote(ref, ref, lc_send.at[place], lc_recv.at[place], core).wait_recv()

    def l_arrive(n, dz):
        ref = l_slot(n, dz, c)
        remote(ref, ref, l_send.at[0], l_recv.at[(dz % 4) * 8 + n], zp).wait_recv()
        if dz == -1 and n % 2 == 0:
            l_copy(n, -1, 1)
        if dz == 1 and n % 2 == 1:
            l_copy(n, 1, -1)
        to_core(n, dz)

    def finish_sum(n):
        i, dr = parts[n]
        xj, j = (x + dr + 4) % 4, chip_at(dr, i)
        for slot in (1, 2) if i else (0,):
            ref = s_recv.at[slot, xj]
            remote(ref, ref, r2_send.at[slot, xj], r2_recv.at[slot, xj], yp).wait_recv()
        if i:
            total = s_recv[1, xj].astype(jnp.float32) + s_recv[2, xj].astype(jnp.float32)
        else:
            total = keep[xj] + s_recv[0, xj].astype(jnp.float32)
        gf[j] = total
        ls[j, c, z] = total.astype(jnp.bfloat16)
        l_copy(n, 0, 1)
        l_copy(n, 0, -1)
        to_core(n, 0)

    def r_begin(k):
        side, xj = row_block(0, 0, k)
        rt[own, side * 2 + xj // 2] = ls[side * 4 + xj, c, z]
        gr.begin(k)

    def load_pair():
        for h in range(2):
            ref = xq.at[1 - c, pl.ds(h * HALF, HALF)]
            remote(ref, ref, xq_send.at[h], xq_recv.at[h], core).wait_recv()
            passed[h][1].wait()
        for k in range(COLS // 128):
            cols = slice(k * 128, (k + 1) * 128)
            xt[1, cols, :] = xq[:, :, cols].reshape(CHIP, 128).T

    passed = []
    gram(0, 0, 1)
    gx.arrive(-1, 0, 0)
    gram(0, -1, 0)
    gx.arrive(1, 0, 1)
    gram(0, 0, 0)
    gram(0, 1, 1)
    gx.arrive(0, 1, 0)
    passed.append(pass_pair(0))
    gx.arrive(-1, 0, 1)
    gram(0, -1, 1)
    gx.arrive(1, 0, 0)
    gx.arrive(0, 1, 1)
    passed.append(pass_pair(1))
    gram(0, 1, 0)
    load_pair()
    gram(1, 0, 0)
    gx.spread(1)
    gram(1, 1, 1)
    gram(1, -1, 1)
    gram(1, 0, 1)
    reduce(0, 0)
    gx.arrive(2, 0, 0)
    gram(1, -1, 0)
    gx.arrive(2, 0, 1)
    gx.spread(0)
    relay(0, 1)
    gram(0, 2, 0)
    gram(0, 2, 1)
    gram(1, 2, 1)
    reduce(0, -1)
    gram(1, 1, 0)
    relay(1, -1)
    gram(1, 2, 0)
    reduce(1, 0)
    reduce(0, 1)
    finish_sum(0)
    relay(1, 2)
    relay(1, 1)
    gx.arrive(1, 1, 1)
    relay(0, 2)
    finish_sum(1)
    r_begin(0)
    gx.arrive(-1, 1, 0)
    reduce(1, -1)
    finish_sum(2)
    finish_sum(3)
    reduce(1, 2)
    reduce(1, 1)
    finish_sum(4)
    r_begin(2)
    reduce(0, 2)
    finish_sum(6)
    finish_sum(7)
    l_arrive(0, -1)
    r_begin(3)
    l_arrive(2, -1)
    l_arrive(3, 1)
    gr.arrive(-1, 0, 0)
    gr.arrive(0, 1, 2)
    l_arrive(1, -1)
    gr.arrive(1, 0, 3)
    l_arrive(3, -1)
    gr.arrive(-1, 0, 2)
    gr.arrive(0, 1, 3)
    finish_sum(5)
    r_begin(1)
    gr.arrive(-1, 1, 0)
    gr.arrive(1, 1, 2)
    l_arrive(1, 1)
    gr.arrive(0, 1, 0)
    gr.arrive(2, 0, 0)
    l_arrive(5, 1)
    gr.arrive(1, 1, 3)
    gr.arrive(1, 0, 1)
    gr.arrive(2, 0, 3)
    gr.arrive(-1, 1, 2)
    l_arrive(6, -1)
    l_arrive(4, -1)
    l_arrive(6, 1)
    l_arrive(7, 1)
    l_arrive(3, 2)
    gr.arrive(0, 1, 1)
    gr.arrive(1, 1, 1)
    l_arrive(4, 1)
    gr.arrive(-1, 1, 3)
    l_arrive(5, -1)
    l_arrive(2, 1)
    l_arrive(2, 2)
    gr.arrive(-1, 0, 3)
    gr.arrive(1, 0, 2)
    gr.arrive(1, 0, 0)
    l_arrive(7, -1)
    gr.arrive(1, 1, 0)
    l_arrive(0, 2)
    l_arrive(5, 2)
    l_arrive(1, 2)
    l_arrive(6, 2)
    l_arrive(0, 1)
    gr.arrive(2, 0, 2)
    l_arrive(7, 2)
    l_arrive(4, 2)
    gr.arrive(-1, 0, 1)
    gr.arrive(2, 0, 1)
    gr.arrive(2, 1, 2)
    gr.arrive(2, 1, 0)
    gr.arrive(2, 1, 3)
    gr.arrive(-1, 1, 1)
    gr.arrive(2, 1, 1)
    gx.arrive(-1, 1, 1)
    gx.arrive(1, 1, 0)

    def square(j, rows):
        left = rt[j, rows].reshape(-1, CHIP)
        right = ls[j].reshape(CHIP, CHIP)
        return jnp.dot(left, right, preferred_element_type=jnp.float32)

    def squares(ns, rows):
        return sum(square(chip_at(parts[n][1], parts[n][0]), rows) for n in ns)

    done = ((0, 1, 2, 5), (3, 4), (6, 7))
    for ns in done[:2]:
        for n in ns:
            for dz in (0, -1, 1, 2):
                from_core(n, dz)
        total = squares(ns, slice(None)).reshape(4, PIECE, CHIP)
        sq[...] = total if ns == done[0] else sq[...] + total
    for n in done[2]:
        for dz in (0, -1, 1, 2):
            from_core(n, dz)

    def mix_slot(dr, dp, h):
        return ms.at[h, :, (yh + dp) % 2, (z + dr + 4) % 4]

    gm = Gather(mix_slot, zp, zm, yq, m_send, m_recv, "cross")
    for h in range(2):
        rows = slice(2 * h, 2 * h + 2)
        total = sq[rows].reshape(HALF, CHIP) + squares(done[2], rows)
        gram_rows = jnp.concatenate([gf[h * 4 + yh], gf[h * 4 + 2 + yh]], axis=0)
        mixing = (COEF_B * gram_rows + COEF_C * total).astype(jnp.bfloat16)
        ms[h, 0, yh, z] = mixing[:PIECE]
        ms[h, 1, yh, z] = mixing[PIECE:]
        if h == 0:
            gm.begin(0, ("plus", "pair"))
        else:
            gm.begin(1, ("minus", "plus", "pair"))
            gm.begin(0, ("minus",))

    def turn(dr, dp):
        mt[...] = ms[:, :, (yh + dp) % 2, (z + dr + 4) % 4].reshape(ROWS, CHIP).T

    def product(dr, dp, rows, n, first=False):
        side, at = (yh + dp) % 2, (z + dr + 4) % 4
        cols = pl.ds(n * 384, 384)
        at_rows = pl.ds(pl.multiple_of(at * PIECE, 16), PIECE)
        right = jnp.concatenate([xs[2 * k + side, at_rows, cols] for k in range(4)], axis=0)
        part = jnp.dot(mt[rows, :], right, preferred_element_type=jnp.float32)
        zs[rows, cols] = part if first else zs[rows, cols] + part

    def unit(dr, dp, first=False):
        turn(dr, dp)
        for n in range(3):
            product(dr, dp, every, n, first)

    every = slice(None)
    for h in range(2):
        gm.arrive(-1, 0, h)
        gm.arrive(1, 0, 1 - h)
        gm.arrive(0, 1, h)
    for h in range(2):
        gx.arrive(2, 1, h)
    unit(0, 0, True)
    unit(-1, 0)
    unit(1, 0)
    gm.arrive(-1, 1, 0)
    gm.arrive(1, 1, 1)
    unit(0, 1)
    for h in range(2):
        gm.arrive(2, 0, h)
    unit(2, 0)
    gm.arrive(-1, 1, 1)
    gm.arrive(1, 1, 0)
    unit(-1, 1)
    unit(1, 1)
    for h in range(2):
        gm.arrive(2, 1, h)
    turn(2, 1)
    last = []
    for n in range(3):
        product(2, 1, theirs, n)
        zb[n] = zs[theirs, pl.ds(n * 384, 384)].astype(jnp.bfloat16)
        last.append(remote(zb.at[n], zr.at[n], z_send.at[n], z_recv.at[n], core))
        last[n].start()
    for n in range(3):
        product(2, 1, mine, n)
    for n in range(3):
        last[n].wait_recv()
        cols = pl.ds(n * 384, 384)
        out_ref[:, cols] = zs[mine, cols] + zr[n].astype(jnp.float32)

    for copy in lanes + l_sent + [swap] + last + [over for over, _ in passed]:
        copy.wait_send()
    for gather in (gx, gr, gm):
        gather.finish()
    for place in parts:
        for _, copy in pieces_of(*place):
            copy.wait_send()
        if place in RELAY:
            onward(*place).wait_send()
    for xj in range(4):
        for slot in range(3):
            sum_copy(min(slot, 1), xj, slot).wait_send()


def local(gradient, momentum):
    half, full = jnp.bfloat16, jnp.float32
    dma = pltpu.SemaphoreType.DMA
    product = pl.pallas_call(
        kernel,
        out_shape=jax.ShapeDtypeStruct((ROWS, COLS), full),
        in_specs=[pl.BlockSpec(memory_space=pl.ANY)] * 2,
        out_specs=pl.BlockSpec(memory_space=pltpu.VMEM),
        scratch_shapes=[
            pltpu.VMEM((ROWS, COLS), full),
            pltpu.VMEM((ROWS, COLS), full),
            pltpu.VMEM((8, ROWS, COLS), half),
            pltpu.VMEM((CHIP, COLS), half),
            pltpu.VMEM((2, ROWS, COLS), half),
            pltpu.VMEM((2, COLS, CHIP), half),
            pltpu.VMEM((8, 4, PIECE, CHIP), half),
            pltpu.VMEM((8, PIECE, CHIP), half),
            pltpu.VMEM((8, PIECE, CHIP), half),
            pltpu.VMEM((8, 3, PIECE, CHIP), half),
            pltpu.VMEM((4, PIECE, CHIP), full),
            pltpu.VMEM((2, 4, PIECE, CHIP), half),
            pltpu.VMEM((3, 4, PIECE, CHIP), half),
            pltpu.VMEM((8, PIECE, CHIP), full),
            pltpu.VMEM((4, PIECE, CHIP), full),
            pltpu.VMEM((8, 4, PIECE, CHIP), half),
            pltpu.VMEM((8, 2, 4, PIECE, CHIP), half),
            pltpu.VMEM((2, 2, 2, 4, PIECE, CHIP), half),
            pltpu.VMEM((CHIP, ROWS), half),
            pltpu.VMEM((CHIP, COLS), full),
            pltpu.VMEM((3, ROWS, 384), half),
            pltpu.VMEM((3, ROWS, 384), half),
            dma((4,)), dma((14,)), dma((16,)), dma(()), dma(()), dma((2,)), dma((2,)), dma((2,)),
            dma((8,)), dma((8,)), dma((8, 3)), dma((8, 3)), dma((3, 4)), dma((3, 4)),
            dma((28,)), dma((32,)), dma((28,)), dma((32,)),
            dma((32,)), dma((32,)), dma((14,)), dma((16,)),
            dma((3,)), dma((3,)),
        ],
        name="muon",
        compiler_params=pltpu.CompilerParams(
            collective_id=0, has_side_effects=True, vmem_limit_bytes=60 * 2**20
        ),
    )(gradient, momentum)
    new_momentum = MOMENTUM_RATE * momentum + gradient
    nesterov = gradient + MOMENTUM_RATE * new_momentum
    return new_momentum, SCALE * (COEF_A * nesterov + product)


def solution(mesh):
    specs = (P("row", "col"), P("row", "col"))
    return jax.shard_map(local, mesh=mesh, in_specs=specs, out_specs=specs, check_vma=False)
```

```python
import math

import jax
import jax.numpy as jnp
from jax import lax
from jax.experimental import pallas as pl
from jax.experimental.pallas import tpu as pltpu
from jax.sharding import PartitionSpec as P

HIDDEN_SIZE = 9216
MOMENTUM_RATE = 0.95
COEF_A = 3.4445
COEF_B = -4.775
COEF_C = 2.0315
SCALE = math.sqrt(HIDDEN_SIZE)

MESH = pl.DeviceIdType.MESH
ROWS = 320
COLS = 1152
HALF = ROWS // 2
CHIP = 2 * ROWS
PIECE = ROWS // 4
RELAY = {(1, 0): -1, (1, -1): 1, (1, 1): -1, (0, 2): 1, (1, 2): 1}
PLACES = {(0, 0): 0, (-1, 0): 1, (1, 0): 2, (2, 0): 3, (0, 1): 4, (-1, 1): 5, (1, 1): 6, (2, 1): 7}


class Gather:
    def __init__(self, slot, plus, minus, pair, send, recv, mode, parts=2, hold=False):
        self.slot, self.plus, self.minus, self.pair = slot, plus, minus, pair
        self.send, self.recv, self.mode = send, recv, mode
        self.parts, self.hold, self.started = parts, hold, []

    def _copy(self, dr, dp, h, to):
        device, ring, other = {"plus": (self.plus, -1, 0), "minus": (self.minus, 1, 0), "pair": (self.pair, 0, 1)}[to]
        there = dr + ring
        there = 2 if there == -2 else there
        place = PLACES[(there, (dp + other) % 2)] * self.parts + h
        ref = self.slot(dr, dp, h)
        copy = pltpu.make_async_remote_copy(
            src_ref=ref,
            dst_ref=ref,
            send_sem=self.send.at[len(self.started)],
            recv_sem=self.recv.at[place],
            device_id=device,
            device_id_type=MESH,
        )
        copy.start()
        self.started.append(copy)

    def begin(self, h, links=("plus", "minus", "pair")):
        for to in links:
            self._copy(0, 0, h, to)

    def spread(self, h):
        if self.mode != "cross" or h % 2 == 1:
            self._copy(0, 1, h, "plus")
        if self.mode != "cross" or h % 2 == 0:
            self._copy(0, 1, h, "minus")

    def pass_far(self, h):
        self._copy(2, 0, h, "pair")

    def arrive(self, dr, dp, h):
        ref = self.slot(dr, dp, h)
        place = PLACES[(dr, dp)] * self.parts + h
        pltpu.make_async_remote_copy(
            src_ref=ref,
            dst_ref=ref,
            send_sem=self.send.at[0],
            recv_sem=self.recv.at[place],
            device_id=self.pair,
            device_id_type=MESH,
        ).wait_recv()
        if (dr, dp) == (0, 1):
            if not self.hold:
                self.spread(h)
        elif (dr, h % 2) in ((-1, 0), (1, 1)) and (dp == 0 or self.mode != "late"):
            self._copy(dr, dp, h, "plus" if dr == -1 else "minus")
            if self.mode == "cross" and dp == 0:
                self._copy(dr, dp, h, "pair")

    def finish(self):
        for copy in self.started:
            copy.wait_send()


def kernel(
    g_hbm, m_hbm, out_ref,
    g_ref, m_ref, xs, xi, xq, xt, ps, rl, mg, r1, keep, s_send, s_recv, gf, sq, rt, ls, ms, mt, zs, zb, zr,
    in_sem, x_send, x_recv, xc_send, xc_recv, xq_send, xq_recv, xq_sem, rl_send, rl_recv, r1_send, r1_recv, r2_send, r2_recv,
    rt_send, rt_recv, l_send, l_recv, lc_send, lc_recv, m_send, m_recv, z_send, z_recv,
):
    row, col = lax.axis_index("row"), lax.axis_index("col")
    c, x, yl = row % 2, (row // 2) % 4, row // 8
    z, yh = col % 4, col // 4

    def device(x_, yl_, c_, yh_, z_):
        return ((yl_ * 4 + x_) * 2 + c_, yh_ * 4 + z_)

    core = device(x, yl, 1 - c, yh, z)
    xp, xm = device((x + 1) % 4, yl, c, yh, z), device((x + 3) % 4, yl, c, yh, z)
    zp, zm = device(x, yl, c, yh, (z + 1) % 4), device(x, yl, c, yh, (z + 3) % 4)
    z2 = device(x, yl, c, yh, (z + 2) % 4)
    yp, yq = device(x, 1 - yl, c, yh, z), device(x, yl, c, 1 - yh, z)
    yd = device(x, 1 - yl, c, 1 - yh, z)
    barrier = pltpu.get_barrier_semaphore()
    partners = (core, xp, xm, zp, zm, z2, yp, yq, yd)
    for partner in partners:
        pl.semaphore_signal(barrier, inc=1, device_id=partner, device_id_type=MESH)
    loads = []
    for h in range(2):
        rows = pl.ds(h * HALF, HALF)
        for k, (hbm, ref) in enumerate(((g_hbm, g_ref), (m_hbm, m_ref))):
            load = pltpu.make_async_copy(hbm.at[rows], ref.at[rows], in_sem.at[2 * h + k])
            load.start()
            loads.append(load)

    def remote(src, dst, send, recv, to):
        return pltpu.make_async_remote_copy(
            src_ref=src, dst_ref=dst, send_sem=send, recv_sem=recv, device_id=to, device_id_type=MESH
        )

    def chip_at(dr, dp):
        return ((yl + dp) % 2) * 4 + (x + dr + 4) % 4

    own = chip_at(0, 0)

    gx = Gather(lambda dr, dp, h: xs.at[chip_at(dr, dp), pl.ds(h * HALF, HALF)], xp, xm, yp, x_send, x_recv, "late", hold=True)
    mine = pl.ds(pl.multiple_of(c * ROWS, 32), ROWS)
    theirs = pl.ds(pl.multiple_of((1 - c) * ROWS, 32), ROWS)
    for h in range(2):
        rows = pl.ds(h * HALF, HALF)
        loads[2 * h].wait()
        loads[2 * h + 1].wait()
        new = MOMENTUM_RATE * m_ref[rows, :] + g_ref[rows, :]
        low = (g_ref[rows, :] + MOMENTUM_RATE * new).astype(jnp.bfloat16)
        xs[own, rows, :] = low
        if h == 0:
            pl.semaphore_wait(barrier, len(partners))
            gx.begin(0, ("plus", "pair"))
        else:
            gx.begin(1, ("minus", "plus", "pair"))
            gx.begin(0, ("minus",))
        xi[pl.ds(pl.multiple_of(c * ROWS + h * HALF, 32), HALF), :] = low
    swap = remote(xi.at[mine], xi.at[mine], xc_send, xc_recv, core)
    swap.start()
    remote(xi.at[theirs], xi.at[theirs], xc_send, xc_recv, core).wait_recv()
    for k in range(COLS // 128):
        xt[0, k * 128 : (k + 1) * 128, :] = xi[:, k * 128 : (k + 1) * 128].T

    def block_of(i, dr):
        return i * 4 + (x + dr + 4) % 4

    def piece_copy(block, dz, src=None):
        src = ps.at[block, (z + dz) % 4] if src is None else src
        k = dz - 1
        return remote(src, r1.at[block, k], r1_send.at[block, k], r1_recv.at[block, k], (zp, z2, zm)[k])

    def relay_copy(i, dr):
        block = block_of(i, dr)
        to = zp if RELAY[(i, dr)] == 1 else zm
        return remote(ps.at[block, (z + 2) % 4], rl.at[block], rl_send.at[block], rl_recv.at[block], to)

    def pieces_of(i, dr):
        block = block_of(i, dr)
        if (i, dr) not in RELAY:
            return [(dz, piece_copy(block, dz)) for dz in (2, 1, 3)]
        back = 4 - RELAY[(i, dr)] if RELAY[(i, dr)] == 1 else 1
        return [(2, relay_copy(i, dr)), (back, piece_copy(block, back))]

    def gram(i, dr, h):
        j, block = chip_at(dr, 0), block_of(i, dr)
        part = jnp.dot(xs[j, h * HALF : (h + 1) * HALF, :], xt[i], preferred_element_type=jnp.float32)
        ps[block, 2 * h : 2 * h + 2] = part.astype(jnp.bfloat16).reshape(2, PIECE, CHIP)
        for dz, copy in pieces_of(i, dr):

            @pl.when((z + dz) % 4 // 2 == h)
            def _(copy=copy):
                copy.start()

    def onward(i, dr):
        block, dz = block_of(i, dr), RELAY[(i, dr)] % 4
        return piece_copy(block, dz, mg.at[block])

    def relay(i, dr):
        block = block_of(i, dr)
        relay_copy(i, dr).wait_recv()
        total = rl[block].astype(jnp.float32) + ps[block, (z + RELAY[(i, dr)] + 4) % 4].astype(jnp.float32)
        mg[block] = total.astype(jnp.bfloat16)
        onward(i, dr).start()

    def sum_copy(i, xj, slot):
        to = (yq, yp, yd)[slot]
        return remote(s_send.at[i, xj], s_recv.at[slot, xj], r2_send.at[slot, xj], r2_recv.at[slot, xj], to)

    def reduce(i, dr):
        block = block_of(i, dr)
        total = ps[block, z].astype(jnp.float32)
        for dz in (1, 3) if (i, dr) in RELAY else (1, 3, 2):
            piece_copy(block, dz).wait_recv()
            total = total + r1[block, dz - 1].astype(jnp.float32)
        xj = (x + dr + 4) % 4
        s_send[i, xj] = total.astype(jnp.bfloat16)
        if i == 0:
            keep[xj] = total
            sum_copy(0, xj, 0).start()
        else:
            sum_copy(1, xj, 1).start()
            sum_copy(1, xj, 2).start()

    def pass_pair(h):
        rows = pl.ds(h * HALF, HALF)
        src = xs.at[chip_at(0, 1), rows]
        over = remote(src, xq.at[c, rows], xq_send.at[h], xq_recv.at[h], core)
        over.start()
        here = pltpu.make_async_copy(src, xq.at[c, rows], xq_sem.at[h])
        here.start()
        return over, here

    def row_block(dr, dp, k):
        at, side = (x + dr + 4) % 4, (yl + dp + k // 2) % 2
        return side, (at + 2 * (k % 2) + 3 * ((at + yh) % 2)) % 4

    def row_slot(dr, dp, k):
        side, xj = row_block(dr, dp, k)
        return rt.at[chip_at(dr, dp), side * 2 + xj // 2]

    gr = Gather(row_slot, xp, xm, yp, rt_send, rt_recv, "cross", 4)
    parts = ((0, 0), (0, -1), (0, 1), (1, 0), (1, -1), (0, 2), (1, 1), (1, 2))
    lanes, l_sent = [], []

    def l_slot(n, dz, lane):
        i, dr = parts[n]
        return ls.at[chip_at(dr, i), lane, (z + dz + 4) % 4]

    def l_copy(n, dz, side):
        there = {(0, 1): -1, (0, -1): 1, (-1, 1): 2, (1, -1): 2}[(dz, side)]
        ref = l_slot(n, dz, c)
        to = zp if side == 1 else zm
        copy = remote(ref, ref, l_send.at[len(l_sent)], l_recv.at[(there % 4) * 8 + n], to)
        copy.start()
        l_sent.append(copy)

    def to_core(n, dz):
        place = (dz % 4) * 8 + n
        copy = remote(l_slot(n, dz, c), l_slot(n, dz, c), lc_send.at[place], lc_recv.at[place], core)
        copy.start()
        lanes.append(copy)

    def from_core(n, dz):
        place = (dz % 4) * 8 + n
        ref = l_slot(n, dz, 1 - c)
        remote(ref, ref, lc_send.at[place], lc_recv.at[place], core).wait_recv()

    def l_arrive(n, dz):
        ref = l_slot(n, dz, c)
        remote(ref, ref, l_send.at[0], l_recv.at[(dz % 4) * 8 + n], zp).wait_recv()
        if dz == -1 and n % 2 == 0:
            l_copy(n, -1, 1)
        if dz == 1 and n % 2 == 1:
            l_copy(n, 1, -1)
        to_core(n, dz)

    def finish_sum(n):
        i, dr = parts[n]
        xj, j = (x + dr + 4) % 4, chip_at(dr, i)
        for slot in (1, 2) if i else (0,):
            ref = s_recv.at[slot, xj]
            remote(ref, ref, r2_send.at[slot, xj], r2_recv.at[slot, xj], yp).wait_recv()
        if i:
            total = s_recv[1, xj].astype(jnp.float32) + s_recv[2, xj].astype(jnp.float32)
        else:
            total = keep[xj] + s_recv[0, xj].astype(jnp.float32)
        gf[j] = total
        ls[j, c, z] = total.astype(jnp.bfloat16)
        l_copy(n, 0, 1)
        l_copy(n, 0, -1)
        to_core(n, 0)

    def r_begin(k):
        side, xj = row_block(0, 0, k)
        rt[own, side * 2 + xj // 2] = ls[side * 4 + xj, c, z]
        gr.begin(k)

    def load_pair():
        for h in range(2):
            ref = xq.at[1 - c, pl.ds(h * HALF, HALF)]
            remote(ref, ref, xq_send.at[h], xq_recv.at[h], core).wait_recv()
            passed[h][1].wait()
        for k in range(COLS // 128):
            cols = slice(k * 128, (k + 1) * 128)
            xt[1, cols, :] = xq[:, :, cols].reshape(CHIP, 128).T

    passed = []
    gram(0, 0, 1)
    gram(0, 0, 0)
    gx.arrive(-1, 0, 0)
    gx.arrive(1, 0, 1)
    gx.arrive(0, 1, 0)
    passed.append(pass_pair(0))
    gram(0, 1, 1)
    gram(0, -1, 0)
    gx.arrive(-1, 0, 1)
    gram(0, -1, 1)
    gx.arrive(1, 0, 0)
    reduce(0, 0)
    gx.arrive(0, 1, 1)
    passed.append(pass_pair(1))
    gram(0, 1, 0)
    load_pair()
    gram(1, 0, 1)
    gx.spread(1)
    gram(1, -1, 0)
    gram(1, -1, 1)
    reduce(0, -1)
    gram(1, 0, 0)
    gx.arrive(2, 0, 1)
    gx.arrive(2, 0, 0)
    gram(1, 1, 1)
    gx.pass_far(1)
    gram(1, 1, 0)
    reduce(0, 1)
    relay(1, -1)
    gram(1, 2, 1)
    relay(1, 0)
    gx.spread(0)
    relay(1, 1)
    gram(1, 2, 0)
    finish_sum(1)
    reduce(1, -1)
    relay(1, 2)
    gram(0, 2, 1)
    reduce(1, 0)
    gram(0, 2, 0)
    finish_sum(0)
    r_begin(0)
    reduce(1, 1)
    l_arrive(1, 1)
    finish_sum(4)
    relay(0, 2)
    reduce(1, 2)
    gr.arrive(-1, 0, 0)
    finish_sum(3)
    finish_sum(2)
    r_begin(2)
    finish_sum(6)
    reduce(0, 2)
    gr.arrive(0, 1, 0)
    l_arrive(4, 1)
    finish_sum(7)
    r_begin(3)
    gr.arrive(-1, 1, 0)
    l_arrive(2, 1)
    gr.arrive(0, 1, 2)
    gr.arrive(-1, 0, 2)
    l_arrive(2, -1)
    l_arrive(1, -1)
    gr.arrive(1, 0, 0)
    gr.arrive(2, 0, 0)
    finish_sum(5)
    l_arrive(0, -1)
    l_arrive(0, 1)
    r_begin(1)
    l_arrive(4, -1)
    gr.arrive(1, 0, 2)
    l_arrive(7, 1)
    l_arrive(3, -1)
    gr.arrive(1, 0, 3)
    l_arrive(6, -1)
    l_arrive(5, 1)
    l_arrive(7, -1)
    gr.arrive(1, 0, 1)
    gr.arrive(0, 1, 3)
    gr.arrive(-1, 0, 3)
    gx.pass_far(0)
    l_arrive(3, 1)
    gr.arrive(1, 1, 2)
    l_arrive(7, 2)
    gr.arrive(-1, 0, 1)
    gr.arrive(-1, 1, 2)
    gr.arrive(1, 1, 3)
    gr.arrive(2, 0, 1)
    l_arrive(5, 2)
    gr.arrive(0, 1, 1)
    gr.arrive(1, 1, 1)
    l_arrive(2, 2)
    l_arrive(1, 2)
    gr.arrive(2, 1, 2)
    gr.arrive(1, 1, 0)
    l_arrive(3, 2)
    gr.arrive(2, 1, 0)
    l_arrive(4, 2)
    l_arrive(5, -1)
    l_arrive(6, 1)
    l_arrive(0, 2)
    gr.arrive(2, 0, 3)
    l_arrive(6, 2)
    gr.arrive(-1, 1, 3)
    gr.arrive(2, 1, 3)
    gr.arrive(-1, 1, 1)
    gr.arrive(2, 0, 2)
    gr.arrive(2, 1, 1)
    for h in range(2):
        gx.arrive(-1, 1, h)
        gx.arrive(1, 1, h)

    def square(j, rows):
        left = rt[j, rows].reshape(-1, CHIP)
        right = ls[j].reshape(CHIP, CHIP)
        return jnp.dot(left, right, preferred_element_type=jnp.float32)

    def squares(ns, rows):
        return sum(square(chip_at(parts[n][1], parts[n][0]), rows) for n in ns)

    done = ((0, 1, 2, 5), (3, 4), (6, 7))
    for ns in done[:2]:
        for n in ns:
            for dz in (0, -1, 1, 2):
                from_core(n, dz)
        total = squares(ns, slice(None)).reshape(4, PIECE, CHIP)
        sq[...] = total if ns == done[0] else sq[...] + total
    for n in done[2]:
        for dz in (0, -1, 1, 2):
            from_core(n, dz)

    def mix_slot(dr, dp, h):
        return ms.at[h, :, (yh + dp) % 2, (z + dr + 4) % 4]

    gm = Gather(mix_slot, zp, zm, yq, m_send, m_recv, "cross")
    for h in range(2):
        rows = slice(2 * h, 2 * h + 2)
        total = sq[rows].reshape(HALF, CHIP) + squares(done[2], rows)
        gram_rows = jnp.concatenate([gf[h * 4 + yh], gf[h * 4 + 2 + yh]], axis=0)
        mixing = (COEF_B * gram_rows + COEF_C * total).astype(jnp.bfloat16)
        ms[h, 0, yh, z] = mixing[:PIECE]
        ms[h, 1, yh, z] = mixing[PIECE:]
        if h == 0:
            gm.begin(0, ("plus", "pair"))
        else:
            gm.begin(1, ("minus", "plus", "pair"))
            gm.begin(0, ("minus",))

    def turn(dr, dp):
        mt[...] = ms[:, :, (yh + dp) % 2, (z + dr + 4) % 4].reshape(ROWS, CHIP).T

    def product(dr, dp, rows, n, first=False):
        side, at = (yh + dp) % 2, (z + dr + 4) % 4
        cols = pl.ds(n * 384, 384)
        at_rows = pl.ds(pl.multiple_of(at * PIECE, 16), PIECE)
        right = jnp.concatenate([xs[2 * k + side, at_rows, cols] for k in range(4)], axis=0)
        part = jnp.dot(mt[rows, :], right, preferred_element_type=jnp.float32)
        zs[rows, cols] = part if first else zs[rows, cols] + part

    def unit(dr, dp, first=False):
        turn(dr, dp)
        for n in range(3):
            product(dr, dp, every, n, first)

    every = slice(None)
    for h in range(2):
        gm.arrive(-1, 0, h)
        gm.arrive(1, 0, 1 - h)
        gm.arrive(0, 1, h)
    for h in range(2):
        gx.arrive(2, 1, h)
    unit(0, 0, True)
    unit(-1, 0)
    unit(1, 0)
    gm.arrive(-1, 1, 0)
    gm.arrive(1, 1, 1)
    unit(0, 1)
    for h in range(2):
        gm.arrive(2, 0, h)
    unit(2, 0)
    gm.arrive(-1, 1, 1)
    gm.arrive(1, 1, 0)
    unit(-1, 1)
    unit(1, 1)
    for h in range(2):
        gm.arrive(2, 1, h)
    turn(2, 1)
    last = []
    for n in range(3):
        product(2, 1, theirs, n)
        zb[n] = zs[theirs, pl.ds(n * 384, 384)].astype(jnp.bfloat16)
        last.append(remote(zb.at[n], zr.at[n], z_send.at[n], z_recv.at[n], core))
        last[n].start()
    for n in range(3):
        product(2, 1, mine, n)
    for n in range(3):
        last[n].wait_recv()
        cols = pl.ds(n * 384, 384)
        out_ref[:, cols] = zs[mine, cols] + zr[n].astype(jnp.float32)

    for copy in lanes + l_sent + [swap] + last + [over for over, _ in passed]:
        copy.wait_send()
    for gather in (gx, gr, gm):
        gather.finish()
    for place in parts:
        for _, copy in pieces_of(*place):
            copy.wait_send()
        if place in RELAY:
            onward(*place).wait_send()
    for xj in range(4):
        for slot in range(3):
            sum_copy(min(slot, 1), xj, slot).wait_send()


def local(gradient, momentum):
    half, full = jnp.bfloat16, jnp.float32
    dma = pltpu.SemaphoreType.DMA
    product = pl.pallas_call(
        kernel,
        out_shape=jax.ShapeDtypeStruct((ROWS, COLS), full),
        in_specs=[pl.BlockSpec(memory_space=pl.ANY)] * 2,
        out_specs=pl.BlockSpec(memory_space=pltpu.VMEM),
        scratch_shapes=[
            pltpu.VMEM((ROWS, COLS), full),
            pltpu.VMEM((ROWS, COLS), full),
            pltpu.VMEM((8, ROWS, COLS), half),
            pltpu.VMEM((CHIP, COLS), half),
            pltpu.VMEM((2, ROWS, COLS), half),
            pltpu.VMEM((2, COLS, CHIP), half),
            pltpu.VMEM((8, 4, PIECE, CHIP), half),
            pltpu.VMEM((8, PIECE, CHIP), half),
            pltpu.VMEM((8, PIECE, CHIP), half),
            pltpu.VMEM((8, 3, PIECE, CHIP), half),
            pltpu.VMEM((4, PIECE, CHIP), full),
            pltpu.VMEM((2, 4, PIECE, CHIP), half),
            pltpu.VMEM((3, 4, PIECE, CHIP), half),
            pltpu.VMEM((8, PIECE, CHIP), full),
            pltpu.VMEM((4, PIECE, CHIP), full),
            pltpu.VMEM((8, 4, PIECE, CHIP), half),
            pltpu.VMEM((8, 2, 4, PIECE, CHIP), half),
            pltpu.VMEM((2, 2, 2, 4, PIECE, CHIP), half),
            pltpu.VMEM((CHIP, ROWS), half),
            pltpu.VMEM((CHIP, COLS), full),
            pltpu.VMEM((3, ROWS, 384), half),
            pltpu.VMEM((3, ROWS, 384), half),
            dma((4,)), dma((14,)), dma((16,)), dma(()), dma(()), dma((2,)), dma((2,)), dma((2,)),
            dma((8,)), dma((8,)), dma((8, 3)), dma((8, 3)), dma((3, 4)), dma((3, 4)),
            dma((28,)), dma((32,)), dma((28,)), dma((32,)),
            dma((32,)), dma((32,)), dma((14,)), dma((16,)),
            dma((3,)), dma((3,)),
        ],
        name="muon",
        compiler_params=pltpu.CompilerParams(
            collective_id=0, has_side_effects=True, vmem_limit_bytes=52 * 2**20
        ),
    )(gradient, momentum)
    new_momentum = MOMENTUM_RATE * momentum + gradient
    nesterov = gradient + MOMENTUM_RATE * new_momentum
    return new_momentum, SCALE * (COEF_A * nesterov + product)


def solution(mesh):
    specs = (P("row", "col"), P("row", "col"))
    return jax.shard_map(local, mesh=mesh, in_specs=specs, out_specs=specs, check_vma=False)
```

```python
import math

import jax
import jax.numpy as jnp
from jax import lax
from jax.experimental import pallas as pl
from jax.experimental.pallas import tpu as pltpu
from jax.sharding import PartitionSpec as P

HIDDEN_SIZE = 9216
MOMENTUM_RATE = 0.95
COEF_A = 3.4445
COEF_B = -4.775
COEF_C = 2.0315
SCALE = math.sqrt(HIDDEN_SIZE)

MESH = pl.DeviceIdType.MESH
ROWS = 320
COLS = 1152
HALF = ROWS // 2
CHIP = 2 * ROWS
PIECE = ROWS // 4
RELAY = {(1, 0): -1, (1, -1): -1, (1, 1): -1, (0, 2): 1, (1, 2): 1}
PLACES = {(0, 0): 0, (-1, 0): 1, (1, 0): 2, (2, 0): 3, (0, 1): 4, (-1, 1): 5, (1, 1): 6, (2, 1): 7}


class Gather:
    def __init__(self, slot, plus, minus, pair, send, recv, mode, parts=2, hold=False):
        self.slot, self.plus, self.minus, self.pair = slot, plus, minus, pair
        self.send, self.recv, self.mode = send, recv, mode
        self.parts, self.hold, self.started = parts, hold, []

    def _copy(self, dr, dp, h, to):
        device, ring, other = {"plus": (self.plus, -1, 0), "minus": (self.minus, 1, 0), "pair": (self.pair, 0, 1)}[to]
        there = dr + ring
        there = 2 if there == -2 else there
        place = PLACES[(there, (dp + other) % 2)] * self.parts + h
        ref = self.slot(dr, dp, h)
        copy = pltpu.make_async_remote_copy(
            src_ref=ref,
            dst_ref=ref,
            send_sem=self.send.at[len(self.started)],
            recv_sem=self.recv.at[place],
            device_id=device,
            device_id_type=MESH,
        )
        copy.start()
        self.started.append(copy)

    def begin(self, h, links=("plus", "minus", "pair")):
        for to in links:
            self._copy(0, 0, h, to)

    def spread(self, h):
        if self.mode != "cross" or h % 2 == 1:
            self._copy(0, 1, h, "plus")
        if self.mode != "cross" or h % 2 == 0:
            self._copy(0, 1, h, "minus")

    def pass_far(self, h):
        self._copy(2, 0, h, "pair")

    def arrive(self, dr, dp, h):
        ref = self.slot(dr, dp, h)
        place = PLACES[(dr, dp)] * self.parts + h
        pltpu.make_async_remote_copy(
            src_ref=ref,
            dst_ref=ref,
            send_sem=self.send.at[0],
            recv_sem=self.recv.at[place],
            device_id=self.pair,
            device_id_type=MESH,
        ).wait_recv()
        if (dr, dp) == (0, 1):
            if not self.hold:
                self.spread(h)
        elif (dr, h % 2) in ((-1, 0), (1, 1)) and (dp == 0 or self.mode != "late"):
            self._copy(dr, dp, h, "plus" if dr == -1 else "minus")
            if self.mode == "cross" and dp == 0:
                self._copy(dr, dp, h, "pair")

    def finish(self):
        for copy in self.started:
            copy.wait_send()


def kernel(
    g_hbm, m_hbm, out_ref,
    g_ref, m_ref, xs, xi, xq, xt, ps, rl, mg, r1, keep, s_send, s_recv, gf, sq, rt, ls, ms, mt, zs, zb, zr,
    in_sem, x_send, x_recv, xc_send, xc_recv, xq_send, xq_recv, xq_sem, rl_send, rl_recv, r1_send, r1_recv, r2_send, r2_recv,
    rt_send, rt_recv, l_send, l_recv, lc_send, lc_recv, m_send, m_recv, z_send, z_recv,
):
    row, col = lax.axis_index("row"), lax.axis_index("col")
    c, x, yl = row % 2, (row // 2) % 4, row // 8
    z, yh = col % 4, col // 4

    def device(x_, yl_, c_, yh_, z_):
        return ((yl_ * 4 + x_) * 2 + c_, yh_ * 4 + z_)

    core = device(x, yl, 1 - c, yh, z)
    xp, xm = device((x + 1) % 4, yl, c, yh, z), device((x + 3) % 4, yl, c, yh, z)
    zp, zm = device(x, yl, c, yh, (z + 1) % 4), device(x, yl, c, yh, (z + 3) % 4)
    z2 = device(x, yl, c, yh, (z + 2) % 4)
    yp, yq = device(x, 1 - yl, c, yh, z), device(x, yl, c, 1 - yh, z)
    yd = device(x, 1 - yl, c, 1 - yh, z)
    barrier = pltpu.get_barrier_semaphore()
    partners = (core, xp, xm, zp, zm, z2, yp, yq, yd)
    for partner in partners:
        pl.semaphore_signal(barrier, inc=1, device_id=partner, device_id_type=MESH)
    loads = []
    for h in range(2):
        rows = pl.ds(h * HALF, HALF)
        for k, (hbm, ref) in enumerate(((g_hbm, g_ref), (m_hbm, m_ref))):
            load = pltpu.make_async_copy(hbm.at[rows], ref.at[rows], in_sem.at[2 * h + k])
            load.start()
            loads.append(load)

    def remote(src, dst, send, recv, to):
        return pltpu.make_async_remote_copy(
            src_ref=src, dst_ref=dst, send_sem=send, recv_sem=recv, device_id=to, device_id_type=MESH
        )

    def chip_at(dr, dp):
        return ((yl + dp) % 2) * 4 + (x + dr + 4) % 4

    own = chip_at(0, 0)

    gx = Gather(lambda dr, dp, h: xs.at[chip_at(dr, dp), pl.ds(h * HALF, HALF)], xp, xm, yp, x_send, x_recv, "late", hold=True)
    mine = pl.ds(pl.multiple_of(c * ROWS, 32), ROWS)
    theirs = pl.ds(pl.multiple_of((1 - c) * ROWS, 32), ROWS)
    for h in range(2):
        rows = pl.ds(h * HALF, HALF)
        loads[2 * h].wait()
        loads[2 * h + 1].wait()
        new = MOMENTUM_RATE * m_ref[rows, :] + g_ref[rows, :]
        low = (g_ref[rows, :] + MOMENTUM_RATE * new).astype(jnp.bfloat16)
        xs[own, rows, :] = low
        if h == 0:
            pl.semaphore_wait(barrier, len(partners))
            gx.begin(0, ("plus", "pair"))
        else:
            gx.begin(1, ("minus", "plus", "pair"))
            gx.begin(0, ("minus",))
        xi[pl.ds(pl.multiple_of(c * ROWS + h * HALF, 32), HALF), :] = low
    swap = remote(xi.at[mine], xi.at[mine], xc_send, xc_recv, core)
    swap.start()
    remote(xi.at[theirs], xi.at[theirs], xc_send, xc_recv, core).wait_recv()
    for k in range(COLS // 128):
        xt[0, k * 128 : (k + 1) * 128, :] = xi[:, k * 128 : (k + 1) * 128].T

    def block_of(i, dr):
        return i * 4 + (x + dr + 4) % 4

    def piece_copy(block, dz, src=None):
        src = ps.at[block, (z + dz) % 4] if src is None else src
        k = dz - 1
        return remote(src, r1.at[block, k], r1_send.at[block, k], r1_recv.at[block, k], (zp, z2, zm)[k])

    def relay_copy(i, dr):
        block = block_of(i, dr)
        to = zp if RELAY[(i, dr)] == 1 else zm
        return remote(ps.at[block, (z + 2) % 4], rl.at[block], rl_send.at[block], rl_recv.at[block], to)

    def pieces_of(i, dr):
        block = block_of(i, dr)
        if (i, dr) not in RELAY:
            return [(dz, piece_copy(block, dz)) for dz in (2, 1, 3)]
        back = 4 - RELAY[(i, dr)] if RELAY[(i, dr)] == 1 else 1
        return [(2, relay_copy(i, dr)), (back, piece_copy(block, back))]

    def gram(i, dr, h):
        j, block = chip_at(dr, 0), block_of(i, dr)
        part = jnp.dot(xs[j, h * HALF : (h + 1) * HALF, :], xt[i], preferred_element_type=jnp.float32)
        ps[block, 2 * h : 2 * h + 2] = part.astype(jnp.bfloat16).reshape(2, PIECE, CHIP)
        for dz, copy in pieces_of(i, dr):

            @pl.when((z + dz) % 4 // 2 == h)
            def _(copy=copy):
                copy.start()

    def onward(i, dr):
        block, dz = block_of(i, dr), RELAY[(i, dr)] % 4
        return piece_copy(block, dz, mg.at[block])

    def relay(i, dr):
        block = block_of(i, dr)
        relay_copy(i, dr).wait_recv()
        total = rl[block].astype(jnp.float32) + ps[block, (z + RELAY[(i, dr)] + 4) % 4].astype(jnp.float32)
        mg[block] = total.astype(jnp.bfloat16)
        onward(i, dr).start()

    def sum_copy(i, xj, slot):
        to = (yq, yp, yd)[slot]
        return remote(s_send.at[i, xj], s_recv.at[slot, xj], r2_send.at[slot, xj], r2_recv.at[slot, xj], to)

    def reduce(i, dr):
        block = block_of(i, dr)
        total = ps[block, z].astype(jnp.float32)
        for dz in (1, 3) if (i, dr) in RELAY else (1, 3, 2):
            piece_copy(block, dz).wait_recv()
            total = total + r1[block, dz - 1].astype(jnp.float32)
        xj = (x + dr + 4) % 4
        s_send[i, xj] = total.astype(jnp.bfloat16)
        if i == 0:
            keep[xj] = total
            sum_copy(0, xj, 0).start()
        else:
            sum_copy(1, xj, 1).start()
            sum_copy(1, xj, 2).start()

    def pass_pair(h):
        rows = pl.ds(h * HALF, HALF)
        src = xs.at[chip_at(0, 1), rows]
        over = remote(src, xq.at[c, rows], xq_send.at[h], xq_recv.at[h], core)
        over.start()
        here = pltpu.make_async_copy(src, xq.at[c, rows], xq_sem.at[h])
        here.start()
        return over, here

    def row_block(dr, dp, k):
        at, side = (x + dr + 4) % 4, (yl + dp + k // 2) % 2
        return side, (at + 2 * (k % 2) + 3 * ((at + yh) % 2)) % 4

    def row_slot(dr, dp, k):
        side, xj = row_block(dr, dp, k)
        return rt.at[chip_at(dr, dp), side * 2 + xj // 2]

    gr = Gather(row_slot, xp, xm, yp, rt_send, rt_recv, "cross", 4)
    parts = ((0, 0), (0, -1), (0, 1), (1, 0), (1, -1), (0, 2), (1, 1), (1, 2))
    lanes, l_sent = [], []

    def l_slot(n, dz, lane):
        i, dr = parts[n]
        return ls.at[chip_at(dr, i), lane, (z + dz + 4) % 4]

    def l_copy(n, dz, side):
        there = {(0, 1): -1, (0, -1): 1, (-1, 1): 2, (1, -1): 2}[(dz, side)]
        ref = l_slot(n, dz, c)
        to = zp if side == 1 else zm
        copy = remote(ref, ref, l_send.at[len(l_sent)], l_recv.at[(there % 4) * 8 + n], to)
        copy.start()
        l_sent.append(copy)

    def to_core(n, dz):
        place = (dz % 4) * 8 + n
        copy = remote(l_slot(n, dz, c), l_slot(n, dz, c), lc_send.at[place], lc_recv.at[place], core)
        copy.start()
        lanes.append(copy)

    def from_core(n, dz):
        place = (dz % 4) * 8 + n
        ref = l_slot(n, dz, 1 - c)
        remote(ref, ref, lc_send.at[place], lc_recv.at[place], core).wait_recv()

    def l_arrive(n, dz):
        ref = l_slot(n, dz, c)
        remote(ref, ref, l_send.at[0], l_recv.at[(dz % 4) * 8 + n], zp).wait_recv()
        if dz == -1 and n % 2 == 0:
            l_copy(n, -1, 1)
        if dz == 1 and n % 2 == 1:
            l_copy(n, 1, -1)
        to_core(n, dz)

    def finish_sum(n):
        i, dr = parts[n]
        xj, j = (x + dr + 4) % 4, chip_at(dr, i)
        for slot in (1, 2) if i else (0,):
            ref = s_recv.at[slot, xj]
            remote(ref, ref, r2_send.at[slot, xj], r2_recv.at[slot, xj], yp).wait_recv()
        if i:
            total = s_recv[1, xj].astype(jnp.float32) + s_recv[2, xj].astype(jnp.float32)
        else:
            total = keep[xj] + s_recv[0, xj].astype(jnp.float32)
        gf[j] = total
        ls[j, c, z] = total.astype(jnp.bfloat16)
        l_copy(n, 0, 1)
        l_copy(n, 0, -1)
        to_core(n, 0)

    def r_begin(k):
        side, xj = row_block(0, 0, k)
        rt[own, side * 2 + xj // 2] = ls[side * 4 + xj, c, z]
        gr.begin(k)

    def load_pair():
        for h in range(2):
            ref = xq.at[1 - c, pl.ds(h * HALF, HALF)]
            remote(ref, ref, xq_send.at[h], xq_recv.at[h], core).wait_recv()
            passed[h][1].wait()
        for k in range(COLS // 128):
            cols = slice(k * 128, (k + 1) * 128)
            xt[1, cols, :] = xq[:, :, cols].reshape(CHIP, 128).T

    def square(j, rows):
        left = rt[j, rows].reshape(-1, CHIP)
        right = ls[j].reshape(CHIP, CHIP)
        return jnp.dot(left, right, preferred_element_type=jnp.float32)

    def squares(ns, rows):
        return sum(square(chip_at(parts[n][1], parts[n][0]), rows) for n in ns)

    def square_add(n, first=False):
        for dz in (0, -1, 1, 2):
            from_core(n, dz)
        total = squares((n,), slice(None)).reshape(4, PIECE, CHIP)
        sq[...] = total if first else sq[...] + total

    passed = []
    gram(0, 0, 1)
    gx.arrive(1, 0, 1)
    gx.arrive(-1, 0, 0)
    gram(0, -1, 0)
    gx.arrive(0, 1, 0)
    passed.append(pass_pair(0))
    gram(0, 1, 1)
    gram(0, 0, 0)
    gx.arrive(0, 1, 1)
    passed.append(pass_pair(1))
    gx.arrive(-1, 0, 1)
    gram(0, -1, 1)
    gx.spread(1)
    gx.arrive(1, 0, 0)
    gram(0, 1, 0)
    load_pair()
    reduce(0, 0)
    gram(1, -1, 0)
    gram(1, 1, 1)
    gram(1, 0, 1)
    gram(1, -1, 1)
    reduce(0, -1)
    gx.arrive(2, 0, 1)
    gram(1, 1, 0)
    gx.pass_far(1)
    gram(1, 0, 0)
    relay(1, -1)
    reduce(0, 1)
    gx.arrive(2, 0, 0)
    gram(1, 2, 0)
    finish_sum(1)
    relay(1, 0)
    gram(0, 2, 1)
    relay(1, 1)
    gram(1, 2, 1)
    finish_sum(0)
    r_begin(0)
    gram(0, 2, 0)
    reduce(1, -1)
    gr.arrive(-1, 0, 0)
    gx.spread(0)
    relay(1, 2)
    finish_sum(2)
    reduce(1, 0)
    gr.arrive(0, 1, 0)
    reduce(1, 1)
    relay(0, 2)
    reduce(1, 2)
    finish_sum(4)
    finish_sum(3)
    r_begin(2)
    l_arrive(1, -1)
    finish_sum(6)
    l_arrive(2, -1)
    reduce(0, 2)
    l_arrive(4, -1)
    l_arrive(0, -1)
    gr.arrive(-1, 0, 2)
    finish_sum(7)
    r_begin(3)
    l_arrive(0, 1)
    gr.arrive(1, 0, 0)
    finish_sum(5)
    r_begin(1)
    l_arrive(3, 1)
    l_arrive(1, 1)
    l_arrive(2, 1)
    gr.arrive(0, 1, 2)
    l_arrive(3, -1)
    gr.arrive(-1, 1, 0)
    gr.arrive(1, 0, 3)
    l_arrive(6, -1)
    l_arrive(5, 1)
    gr.arrive(0, 1, 1)
    gr.arrive(1, 0, 1)
    l_arrive(7, 1)
    gr.arrive(2, 0, 2)
    gr.arrive(-1, 0, 1)
    gr.arrive(1, 1, 2)
    gr.arrive(-1, 0, 3)
    gx.pass_far(0)
    l_arrive(3, 2)
    l_arrive(4, 2)
    l_arrive(0, 2)
    gr.arrive(1, 1, 3)
    gr.arrive(-1, 1, 2)
    l_arrive(2, 2)
    l_arrive(4, 1)
    l_arrive(1, 2)
    gr.arrive(0, 1, 3)
    gr.arrive(1, 1, 1)
    gr.arrive(2, 0, 0)
    square_add(0, True)
    l_arrive(5, -1)
    square_add(3)
    square_add(1)
    l_arrive(5, 2)
    gr.arrive(2, 1, 0)
    l_arrive(6, 1)
    l_arrive(6, 2)
    gr.arrive(1, 0, 2)
    gr.arrive(1, 1, 0)
    gr.arrive(2, 0, 1)
    gr.arrive(2, 1, 2)
    square_add(2)
    l_arrive(7, 2)
    gr.arrive(2, 1, 3)
    gr.arrive(2, 0, 3)
    l_arrive(7, -1)
    square_add(5)
    gr.arrive(-1, 1, 1)
    gr.arrive(-1, 1, 3)
    square_add(6)
    gr.arrive(2, 1, 1)
    for h in range(2):
        gx.arrive(-1, 1, h)
        gx.arrive(1, 1, h)

    done = (4, 7)
    for n in done:
        for dz in (0, -1, 1, 2):
            from_core(n, dz)

    def mix_slot(dr, dp, h):
        return ms.at[h, :, (yh + dp) % 2, (z + dr + 4) % 4]

    gm = Gather(mix_slot, zp, zm, yq, m_send, m_recv, "cross")
    for h in range(2):
        rows = slice(2 * h, 2 * h + 2)
        total = sq[rows].reshape(HALF, CHIP) + squares(done, rows)
        gram_rows = jnp.concatenate([gf[h * 4 + yh], gf[h * 4 + 2 + yh]], axis=0)
        mixing = (COEF_B * gram_rows + COEF_C * total).astype(jnp.bfloat16)
        ms[h, 0, yh, z] = mixing[:PIECE]
        ms[h, 1, yh, z] = mixing[PIECE:]
        if h == 0:
            gm.begin(0, ("plus", "pair"))
        else:
            gm.begin(1, ("minus", "plus", "pair"))
            gm.begin(0, ("minus",))

    def turn(dr, dp):
        mt[...] = ms[:, :, (yh + dp) % 2, (z + dr + 4) % 4].reshape(ROWS, CHIP).T

    def product(dr, dp, rows, n, first=False):
        side, at = (yh + dp) % 2, (z + dr + 4) % 4
        cols = pl.ds(n * 384, 384)
        at_rows = pl.ds(pl.multiple_of(at * PIECE, 16), PIECE)
        right = jnp.concatenate([xs[2 * k + side, at_rows, cols] for k in range(4)], axis=0)
        part = jnp.dot(mt[rows, :], right, preferred_element_type=jnp.float32)
        zs[rows, cols] = part if first else zs[rows, cols] + part

    def unit(dr, dp, first=False):
        turn(dr, dp)
        for n in range(3):
            product(dr, dp, every, n, first)

    every = slice(None)
    for h in range(2):
        gm.arrive(-1, 0, h)
        gm.arrive(1, 0, 1 - h)
        gm.arrive(0, 1, h)
    for h in range(2):
        gx.arrive(2, 1, h)
    unit(0, 0, True)
    unit(-1, 0)
    unit(1, 0)
    gm.arrive(-1, 1, 0)
    gm.arrive(1, 1, 1)
    unit(0, 1)
    for h in range(2):
        gm.arrive(2, 0, h)
    unit(2, 0)
    gm.arrive(-1, 1, 1)
    gm.arrive(1, 1, 0)
    unit(-1, 1)
    unit(1, 1)
    for h in range(2):
        gm.arrive(2, 1, h)
    turn(2, 1)
    last = []
    for n in range(3):
        product(2, 1, theirs, n)
        zb[n] = zs[theirs, pl.ds(n * 384, 384)].astype(jnp.bfloat16)
        last.append(remote(zb.at[n], zr.at[n], z_send.at[n], z_recv.at[n], core))
        last[n].start()
    for n in range(3):
        product(2, 1, mine, n)
    for n in range(3):
        last[n].wait_recv()
        cols = pl.ds(n * 384, 384)
        out_ref[:, cols] = zs[mine, cols] + zr[n].astype(jnp.float32)

    for copy in lanes + l_sent + [swap] + last + [over for over, _ in passed]:
        copy.wait_send()
    for gather in (gx, gr, gm):
        gather.finish()
    for place in parts:
        for _, copy in pieces_of(*place):
            copy.wait_send()
        if place in RELAY:
            onward(*place).wait_send()
    for xj in range(4):
        for slot in range(3):
            sum_copy(min(slot, 1), xj, slot).wait_send()


def local(gradient, momentum):
    half, full = jnp.bfloat16, jnp.float32
    dma = pltpu.SemaphoreType.DMA
    product = pl.pallas_call(
        kernel,
        out_shape=jax.ShapeDtypeStruct((ROWS, COLS), full),
        in_specs=[pl.BlockSpec(memory_space=pl.ANY)] * 2,
        out_specs=pl.BlockSpec(memory_space=pltpu.VMEM),
        scratch_shapes=[
            pltpu.VMEM((ROWS, COLS), full),
            pltpu.VMEM((ROWS, COLS), full),
            pltpu.VMEM((8, ROWS, COLS), half),
            pltpu.VMEM((CHIP, COLS), half),
            pltpu.VMEM((2, ROWS, COLS), half),
            pltpu.VMEM((2, COLS, CHIP), half),
            pltpu.VMEM((8, 4, PIECE, CHIP), half),
            pltpu.VMEM((8, PIECE, CHIP), half),
            pltpu.VMEM((8, PIECE, CHIP), half),
            pltpu.VMEM((8, 3, PIECE, CHIP), half),
            pltpu.VMEM((4, PIECE, CHIP), full),
            pltpu.VMEM((2, 4, PIECE, CHIP), half),
            pltpu.VMEM((3, 4, PIECE, CHIP), half),
            pltpu.VMEM((8, PIECE, CHIP), full),
            pltpu.VMEM((4, PIECE, CHIP), full),
            pltpu.VMEM((8, 4, PIECE, CHIP), half),
            pltpu.VMEM((8, 2, 4, PIECE, CHIP), half),
            pltpu.VMEM((2, 2, 2, 4, PIECE, CHIP), half),
            pltpu.VMEM((CHIP, ROWS), half),
            pltpu.VMEM((CHIP, COLS), full),
            pltpu.VMEM((3, ROWS, 384), half),
            pltpu.VMEM((3, ROWS, 384), half),
            dma((4,)), dma((14,)), dma((16,)), dma(()), dma(()), dma((2,)), dma((2,)), dma((2,)),
            dma((8,)), dma((8,)), dma((8, 3)), dma((8, 3)), dma((3, 4)), dma((3, 4)),
            dma((28,)), dma((32,)), dma((28,)), dma((32,)),
            dma((32,)), dma((32,)), dma((14,)), dma((16,)),
            dma((3,)), dma((3,)),
        ],
        name="muon",
        compiler_params=pltpu.CompilerParams(
            collective_id=0, has_side_effects=True, vmem_limit_bytes=52 * 2**20
        ),
    )(gradient, momentum)
    new_momentum = MOMENTUM_RATE * momentum + gradient
    nesterov = gradient + MOMENTUM_RATE * new_momentum
    return new_momentum, SCALE * (COEF_A * nesterov + product)


def solution(mesh):
    specs = (P("row", "col"), P("row", "col"))
    return jax.shard_map(local, mesh=mesh, in_specs=specs, out_specs=specs, check_vma=False)
```

```python
import math

import jax
import jax.numpy as jnp
from jax import lax
from jax.experimental import pallas as pl
from jax.experimental.pallas import tpu as pltpu
from jax.sharding import PartitionSpec as P

HIDDEN_SIZE = 9216
MOMENTUM_RATE = 0.95
COEF_A = 3.4445
COEF_B = -4.775
COEF_C = 2.0315
SCALE = math.sqrt(HIDDEN_SIZE)

MESH = pl.DeviceIdType.MESH
ROWS = 320
COLS = 1152
HALF = ROWS // 2
CHIP = 2 * ROWS
PIECE = ROWS // 4
RELAY = {(1, 0): -1, (1, -1): -1, (1, 1): -1, (0, 2): 1, (1, 2): 1}
PLACES = {(0, 0): 0, (-1, 0): 1, (1, 0): 2, (2, 0): 3, (0, 1): 4, (-1, 1): 5, (1, 1): 6, (2, 1): 7}


class Gather:
    def __init__(self, slot, plus, minus, pair, send, recv, mode, parts=2, hold=False):
        self.slot, self.plus, self.minus, self.pair = slot, plus, minus, pair
        self.send, self.recv, self.mode = send, recv, mode
        self.parts, self.hold, self.started = parts, hold, []

    def _copy(self, dr, dp, h, to):
        device, ring, other = {"plus": (self.plus, -1, 0), "minus": (self.minus, 1, 0), "pair": (self.pair, 0, 1)}[to]
        there = dr + ring
        there = 2 if there == -2 else there
        place = PLACES[(there, (dp + other) % 2)] * self.parts + h
        ref = self.slot(dr, dp, h)
        copy = pltpu.make_async_remote_copy(
            src_ref=ref,
            dst_ref=ref,
            send_sem=self.send.at[len(self.started)],
            recv_sem=self.recv.at[place],
            device_id=device,
            device_id_type=MESH,
        )
        copy.start()
        self.started.append(copy)

    def begin(self, h, links=("plus", "minus", "pair")):
        for to in links:
            self._copy(0, 0, h, to)

    def spread(self, h):
        if self.mode != "cross" or h % 2 == 1:
            self._copy(0, 1, h, "plus")
        if self.mode != "cross" or h % 2 == 0:
            self._copy(0, 1, h, "minus")

    def pass_far(self, h):
        self._copy(2, 0, h, "pair")

    def arrive(self, dr, dp, h):
        ref = self.slot(dr, dp, h)
        place = PLACES[(dr, dp)] * self.parts + h
        pltpu.make_async_remote_copy(
            src_ref=ref,
            dst_ref=ref,
            send_sem=self.send.at[0],
            recv_sem=self.recv.at[place],
            device_id=self.pair,
            device_id_type=MESH,
        ).wait_recv()
        if (dr, dp) == (0, 1):
            if not self.hold:
                self.spread(h)
        elif (dr, h % 2) in ((-1, 0), (1, 1)) and (dp == 0 or self.mode != "late"):
            self._copy(dr, dp, h, "plus" if dr == -1 else "minus")
            if self.mode == "cross" and dp == 0:
                self._copy(dr, dp, h, "pair")

    def finish(self):
        for copy in self.started:
            copy.wait_send()


def kernel(
    g_hbm, m_hbm, out_ref,
    g_ref, m_ref, xs, xi, xq, xt, ps, rl, mg, r1, keep, s_send, s_recv, gf, sq, rt, ls, ms, mt, zs, zb, zr,
    in_sem, x_send, x_recv, xc_send, xc_recv, xq_send, xq_recv, xq_sem, rl_send, rl_recv, r1_send, r1_recv, r2_send, r2_recv,
    rt_send, rt_recv, l_send, l_recv, lc_send, lc_recv, m_send, m_recv, z_send, z_recv,
):
    row, col = lax.axis_index("row"), lax.axis_index("col")
    c, x, yl = row % 2, (row // 2) % 4, row // 8
    z, yh = col % 4, col // 4

    def device(x_, yl_, c_, yh_, z_):
        return ((yl_ * 4 + x_) * 2 + c_, yh_ * 4 + z_)

    core = device(x, yl, 1 - c, yh, z)
    xp, xm = device((x + 1) % 4, yl, c, yh, z), device((x + 3) % 4, yl, c, yh, z)
    zp, zm = device(x, yl, c, yh, (z + 1) % 4), device(x, yl, c, yh, (z + 3) % 4)
    z2 = device(x, yl, c, yh, (z + 2) % 4)
    yp, yq = device(x, 1 - yl, c, yh, z), device(x, yl, c, 1 - yh, z)
    yd = device(x, 1 - yl, c, 1 - yh, z)
    barrier = pltpu.get_barrier_semaphore()
    partners = (core, xp, xm, zp, zm, z2, yp, yq, yd)
    loads = []
    for h in range(2):
        rows = pl.ds(h * HALF, HALF)
        for k, (hbm, ref) in enumerate(((g_hbm, g_ref), (m_hbm, m_ref))):
            load = pltpu.make_async_copy(hbm.at[rows], ref.at[rows], in_sem.at[2 * h + k])
            load.start()
            loads.append(load)
    for partner in partners:
        pl.semaphore_signal(barrier, inc=1, device_id=partner, device_id_type=MESH)

    def remote(src, dst, send, recv, to):
        return pltpu.make_async_remote_copy(
            src_ref=src, dst_ref=dst, send_sem=send, recv_sem=recv, device_id=to, device_id_type=MESH
        )

    def chip_at(dr, dp):
        return ((yl + dp) % 2) * 4 + (x + dr + 4) % 4

    own = chip_at(0, 0)

    gx = Gather(lambda dr, dp, h: xs.at[chip_at(dr, dp), pl.ds(h * HALF, HALF)], xp, xm, yp, x_send, x_recv, "late", hold=True)
    mine = pl.ds(pl.multiple_of(c * ROWS, 32), ROWS)
    theirs = pl.ds(pl.multiple_of((1 - c) * ROWS, 32), ROWS)
    for h in range(2):
        rows = pl.ds(h * HALF, HALF)
        loads[2 * h].wait()
        loads[2 * h + 1].wait()
        new = MOMENTUM_RATE * m_ref[rows, :] + g_ref[rows, :]
        low = (g_ref[rows, :] + MOMENTUM_RATE * new).astype(jnp.bfloat16)
        xs[own, rows, :] = low
        if h == 0:
            pl.semaphore_wait(barrier, len(partners))
            gx.begin(0, ("plus", "pair"))
        else:
            gx.begin(1, ("minus", "plus", "pair"))
            gx.begin(0, ("minus",))
        xi[pl.ds(pl.multiple_of(c * ROWS + h * HALF, 32), HALF), :] = low
    swap = remote(xi.at[mine], xi.at[mine], xc_send, xc_recv, core)
    swap.start()
    remote(xi.at[theirs], xi.at[theirs], xc_send, xc_recv, core).wait_recv()
    for k in range(COLS // 128):
        xt[0, k * 128 : (k + 1) * 128, :] = xi[:, k * 128 : (k + 1) * 128].T

    def block_of(i, dr):
        return i * 4 + (x + dr + 4) % 4

    def piece_copy(block, dz, src=None):
        src = ps.at[block, (z + dz) % 4] if src is None else src
        k = dz - 1
        return remote(src, r1.at[block, k], r1_send.at[block, k], r1_recv.at[block, k], (zp, z2, zm)[k])

    def relay_copy(i, dr):
        block = block_of(i, dr)
        to = zp if RELAY[(i, dr)] == 1 else zm
        return remote(ps.at[block, (z + 2) % 4], rl.at[block], rl_send.at[block], rl_recv.at[block], to)

    def pieces_of(i, dr):
        block = block_of(i, dr)
        if (i, dr) not in RELAY:
            return [(dz, piece_copy(block, dz)) for dz in (2, 1, 3)]
        back = 4 - RELAY[(i, dr)] if RELAY[(i, dr)] == 1 else 1
        return [(2, relay_copy(i, dr)), (back, piece_copy(block, back))]

    def gram(i, dr, h):
        j, block = chip_at(dr, 0), block_of(i, dr)
        part = jnp.dot(xs[j, h * HALF : (h + 1) * HALF, :], xt[i], preferred_element_type=jnp.float32)
        ps[block, 2 * h : 2 * h + 2] = part.astype(jnp.bfloat16).reshape(2, PIECE, CHIP)
        for dz, copy in pieces_of(i, dr):

            @pl.when((z + dz) % 4 // 2 == h)
            def _(copy=copy):
                copy.start()

    def onward(i, dr):
        block, dz = block_of(i, dr), RELAY[(i, dr)] % 4
        return piece_copy(block, dz, mg.at[block])

    def relay(i, dr):
        block = block_of(i, dr)
        relay_copy(i, dr).wait_recv()
        total = rl[block].astype(jnp.float32) + ps[block, (z + RELAY[(i, dr)] + 4) % 4].astype(jnp.float32)
        mg[block] = total.astype(jnp.bfloat16)
        onward(i, dr).start()

    def sum_copy(i, xj, slot):
        to = (yq, yp, yd)[slot]
        return remote(s_send.at[i, xj], s_recv.at[slot, xj], r2_send.at[slot, xj], r2_recv.at[slot, xj], to)

    def reduce(i, dr):
        block = block_of(i, dr)
        total = ps[block, z].astype(jnp.float32)
        for dz in (1, 3) if (i, dr) in RELAY else (1, 3, 2):
            piece_copy(block, dz).wait_recv()
            total = total + r1[block, dz - 1].astype(jnp.float32)
        xj = (x + dr + 4) % 4
        s_send[i, xj] = total.astype(jnp.bfloat16)
        if i == 0:
            keep[xj] = total
            sum_copy(0, xj, 0).start()
        else:
            sum_copy(1, xj, 1).start()
            sum_copy(1, xj, 2).start()

    def pass_pair(h):
        rows = pl.ds(h * HALF, HALF)
        src = xs.at[chip_at(0, 1), rows]
        over = remote(src, xq.at[c, rows], xq_send.at[h], xq_recv.at[h], core)
        over.start()
        here = pltpu.make_async_copy(src, xq.at[c, rows], xq_sem.at[h])
        here.start()
        return over, here

    def row_block(dr, dp, k):
        at, side = (x + dr + 4) % 4, (yl + dp + k // 2) % 2
        return side, (at + 2 * (k % 2) + 3 * ((at + yh) % 2)) % 4

    def row_slot(dr, dp, k):
        side, xj = row_block(dr, dp, k)
        return rt.at[chip_at(dr, dp), side * 2 + xj // 2]

    gr = Gather(row_slot, xp, xm, yp, rt_send, rt_recv, "cross", 4)
    parts = ((0, 0), (0, -1), (0, 1), (1, 0), (1, -1), (0, 2), (1, 1), (1, 2))
    lanes, l_sent = [], []

    def l_slot(n, dz, lane):
        i, dr = parts[n]
        return ls.at[chip_at(dr, i), lane, (z + dz + 4) % 4]

    def l_copy(n, dz, side):
        there = {(0, 1): -1, (0, -1): 1, (-1, 1): 2, (1, -1): 2}[(dz, side)]
        ref = l_slot(n, dz, c)
        to = zp if side == 1 else zm
        copy = remote(ref, ref, l_send.at[len(l_sent)], l_recv.at[(there % 4) * 8 + n], to)
        copy.start()
        l_sent.append(copy)

    def to_core(n, dz):
        place = (dz % 4) * 8 + n
        copy = remote(l_slot(n, dz, c), l_slot(n, dz, c), lc_send.at[place], lc_recv.at[place], core)
        copy.start()
        lanes.append(copy)

    def from_core(n, dz):
        place = (dz % 4) * 8 + n
        ref = l_slot(n, dz, 1 - c)
        remote(ref, ref, lc_send.at[place], lc_recv.at[place], core).wait_recv()

    def l_arrive(n, dz):
        ref = l_slot(n, dz, c)
        remote(ref, ref, l_send.at[0], l_recv.at[(dz % 4) * 8 + n], zp).wait_recv()
        if dz == -1 and n % 2 == 0:
            l_copy(n, -1, 1)
        if dz == 1 and n % 2 == 1:
            l_copy(n, 1, -1)
        to_core(n, dz)

    def finish_sum(n):
        i, dr = parts[n]
        xj, j = (x + dr + 4) % 4, chip_at(dr, i)
        for slot in (1, 2) if i else (0,):
            ref = s_recv.at[slot, xj]
            remote(ref, ref, r2_send.at[slot, xj], r2_recv.at[slot, xj], yp).wait_recv()
        if i:
            total = s_recv[1, xj].astype(jnp.float32) + s_recv[2, xj].astype(jnp.float32)
        else:
            total = keep[xj] + s_recv[0, xj].astype(jnp.float32)
        gf[j] = total
        ls[j, c, z] = total.astype(jnp.bfloat16)
        l_copy(n, 0, 1)
        l_copy(n, 0, -1)
        to_core(n, 0)

    def r_begin(k):
        side, xj = row_block(0, 0, k)
        rt[own, side * 2 + xj // 2] = ls[side * 4 + xj, c, z]
        gr.begin(k)

    def load_pair():
        for h in range(2):
            ref = xq.at[1 - c, pl.ds(h * HALF, HALF)]
            remote(ref, ref, xq_send.at[h], xq_recv.at[h], core).wait_recv()
            passed[h][1].wait()
        for k in range(COLS // 128):
            cols = slice(k * 128, (k + 1) * 128)
            xt[1, cols, :] = xq[:, :, cols].reshape(CHIP, 128).T

    def square(j, rows):
        left = rt[j, rows].reshape(-1, CHIP)
        right = ls[j].reshape(CHIP, CHIP)
        return jnp.dot(left, right, preferred_element_type=jnp.float32)

    def squares(ns, rows):
        return sum(square(chip_at(parts[n][1], parts[n][0]), rows) for n in ns)

    def square_add(n, first=False):
        for dz in (0, -1, 1, 2):
            from_core(n, dz)
        total = squares((n,), slice(None)).reshape(4, PIECE, CHIP)
        sq[...] = total if first else sq[...] + total

    passed = []
    gram(0, 0, 1)
    gx.arrive(1, 0, 1)
    gx.arrive(-1, 0, 0)
    gram(0, -1, 0)
    gx.arrive(0, 1, 0)
    passed.append(pass_pair(0))
    gram(0, 1, 1)
    gram(0, 0, 0)
    gx.arrive(0, 1, 1)
    passed.append(pass_pair(1))
    gx.arrive(-1, 0, 1)
    gram(0, -1, 1)
    gx.spread(1)
    gx.arrive(1, 0, 0)
    gram(0, 1, 0)
    load_pair()
    reduce(0, 0)
    gram(1, -1, 0)
    gram(1, 1, 1)
    gram(1, 0, 1)
    gram(1, -1, 1)
    reduce(0, -1)
    gx.arrive(2, 0, 1)
    gram(1, 1, 0)
    gx.pass_far(1)
    gram(1, 0, 0)
    relay(1, -1)
    reduce(0, 1)
    gx.arrive(2, 0, 0)
    gram(1, 2, 0)
    finish_sum(1)
    relay(1, 0)
    gram(0, 2, 1)
    relay(1, 1)
    gram(1, 2, 1)
    finish_sum(0)
    r_begin(0)
    gram(0, 2, 0)
    reduce(1, -1)
    gr.arrive(-1, 0, 0)
    gx.spread(0)
    relay(1, 2)
    finish_sum(2)
    reduce(1, 0)
    gr.arrive(0, 1, 0)
    reduce(1, 1)
    relay(0, 2)
    reduce(1, 2)
    finish_sum(4)
    finish_sum(3)
    r_begin(2)
    l_arrive(1, -1)
    finish_sum(6)
    l_arrive(2, -1)
    reduce(0, 2)
    l_arrive(4, -1)
    l_arrive(0, -1)
    gr.arrive(-1, 0, 2)
    finish_sum(7)
    r_begin(3)
    l_arrive(0, 1)
    gr.arrive(1, 0, 0)
    finish_sum(5)
    r_begin(1)
    l_arrive(3, 1)
    l_arrive(1, 1)
    l_arrive(2, 1)
    gr.arrive(0, 1, 2)
    l_arrive(3, -1)
    gr.arrive(-1, 1, 0)
    gr.arrive(1, 0, 3)
    l_arrive(6, -1)
    l_arrive(5, 1)
    gr.arrive(0, 1, 1)
    gr.arrive(1, 0, 1)
    l_arrive(7, 1)
    gr.arrive(2, 0, 2)
    gr.arrive(-1, 0, 1)
    gr.arrive(1, 1, 2)
    gr.arrive(-1, 0, 3)
    gx.pass_far(0)
    l_arrive(3, 2)
    l_arrive(4, 2)
    l_arrive(0, 2)
    gr.arrive(1, 1, 3)
    gr.arrive(-1, 1, 2)
    l_arrive(2, 2)
    l_arrive(4, 1)
    l_arrive(1, 2)
    gr.arrive(0, 1, 3)
    gr.arrive(1, 1, 1)
    gr.arrive(2, 0, 0)
    square_add(0, True)
    l_arrive(5, -1)
    square_add(3)
    square_add(1)
    l_arrive(5, 2)
    gr.arrive(2, 1, 0)
    l_arrive(6, 1)
    l_arrive(6, 2)
    gr.arrive(1, 0, 2)
    gr.arrive(1, 1, 0)
    gr.arrive(2, 0, 1)
    gr.arrive(2, 1, 2)
    square_add(2)
    l_arrive(7, 2)
    gr.arrive(2, 1, 3)
    gr.arrive(2, 0, 3)
    l_arrive(7, -1)
    square_add(5)
    gr.arrive(-1, 1, 1)
    gr.arrive(-1, 1, 3)
    square_add(6)
    gr.arrive(2, 1, 1)
    for h in range(2):
        gx.arrive(-1, 1, h)
        gx.arrive(1, 1, h)

    done = (4, 7)
    for n in done:
        for dz in (0, -1, 1, 2):
            from_core(n, dz)

    def mix_slot(dr, dp, h):
        return ms.at[h, :, (yh + dp) % 2, (z + dr + 4) % 4]

    gm = Gather(mix_slot, zp, zm, yq, m_send, m_recv, "cross")
    for h in range(2):
        rows = slice(2 * h, 2 * h + 2)
        total = sq[rows].reshape(HALF, CHIP) + squares(done, rows)
        gram_rows = jnp.concatenate([gf[h * 4 + yh], gf[h * 4 + 2 + yh]], axis=0)
        mixing = (COEF_B * gram_rows + COEF_C * total).astype(jnp.bfloat16)
        ms[h, 0, yh, z] = mixing[:PIECE]
        ms[h, 1, yh, z] = mixing[PIECE:]
        if h == 0:
            gm.begin(0, ("plus", "pair"))
        else:
            gm.begin(1, ("minus", "plus", "pair"))
            gm.begin(0, ("minus",))

    def turn(dr, dp):
        mt[...] = ms[:, :, (yh + dp) % 2, (z + dr + 4) % 4].reshape(ROWS, CHIP).T

    def product(dr, dp, rows, n, first=False):
        side, at = (yh + dp) % 2, (z + dr + 4) % 4
        cols = pl.ds(n * 384, 384)
        at_rows = pl.ds(pl.multiple_of(at * PIECE, 16), PIECE)
        right = jnp.concatenate([xs[2 * k + side, at_rows, cols] for k in range(4)], axis=0)
        part = jnp.dot(mt[rows, :], right, preferred_element_type=jnp.float32)
        zs[rows, cols] = part if first else zs[rows, cols] + part

    def unit(dr, dp, first=False):
        turn(dr, dp)
        for n in range(3):
            product(dr, dp, every, n, first)

    every = slice(None)
    for h in range(2):
        gm.arrive(-1, 0, h)
        gm.arrive(1, 0, 1 - h)
        gm.arrive(0, 1, h)
    for h in range(2):
        gx.arrive(2, 1, h)
    unit(0, 0, True)
    unit(-1, 0)
    unit(1, 0)
    gm.arrive(-1, 1, 0)
    gm.arrive(1, 1, 1)
    unit(0, 1)
    for h in range(2):
        gm.arrive(2, 0, h)
    unit(2, 0)
    gm.arrive(-1, 1, 1)
    gm.arrive(1, 1, 0)
    unit(-1, 1)
    unit(1, 1)
    for h in range(2):
        gm.arrive(2, 1, h)
    turn(2, 1)
    last = []
    for n in range(3):
        product(2, 1, theirs, n)
        zb[n] = zs[theirs, pl.ds(n * 384, 384)].astype(jnp.bfloat16)
        last.append(remote(zb.at[n], zr.at[n], z_send.at[n], z_recv.at[n], core))
        last[n].start()
    for n in range(3):
        product(2, 1, mine, n)
    for n in range(3):
        last[n].wait_recv()
        cols = pl.ds(n * 384, 384)
        out_ref[:, cols] = zs[mine, cols] + zr[n].astype(jnp.float32)

    for copy in lanes + l_sent + [swap] + last + [over for over, _ in passed]:
        copy.wait_send()
    for gather in (gx, gr, gm):
        gather.finish()
    for place in parts:
        for _, copy in pieces_of(*place):
            copy.wait_send()
        if place in RELAY:
            onward(*place).wait_send()
    for xj in range(4):
        for slot in range(3):
            sum_copy(min(slot, 1), xj, slot).wait_send()


def local(gradient, momentum):
    half, full = jnp.bfloat16, jnp.float32
    dma = pltpu.SemaphoreType.DMA
    product = pl.pallas_call(
        kernel,
        out_shape=jax.ShapeDtypeStruct((ROWS, COLS), full),
        in_specs=[pl.BlockSpec(memory_space=pl.ANY)] * 2,
        out_specs=pl.BlockSpec(memory_space=pltpu.VMEM),
        scratch_shapes=[
            pltpu.VMEM((ROWS, COLS), full),
            pltpu.VMEM((ROWS, COLS), full),
            pltpu.VMEM((8, ROWS, COLS), half),
            pltpu.VMEM((CHIP, COLS), half),
            pltpu.VMEM((2, ROWS, COLS), half),
            pltpu.VMEM((2, COLS, CHIP), half),
            pltpu.VMEM((8, 4, PIECE, CHIP), half),
            pltpu.VMEM((8, PIECE, CHIP), half),
            pltpu.VMEM((8, PIECE, CHIP), half),
            pltpu.VMEM((8, 3, PIECE, CHIP), half),
            pltpu.VMEM((4, PIECE, CHIP), full),
            pltpu.VMEM((2, 4, PIECE, CHIP), half),
            pltpu.VMEM((3, 4, PIECE, CHIP), half),
            pltpu.VMEM((8, PIECE, CHIP), full),
            pltpu.VMEM((4, PIECE, CHIP), full),
            pltpu.VMEM((8, 4, PIECE, CHIP), half),
            pltpu.VMEM((8, 2, 4, PIECE, CHIP), half),
            pltpu.VMEM((2, 2, 2, 4, PIECE, CHIP), half),
            pltpu.VMEM((CHIP, ROWS), half),
            pltpu.VMEM((CHIP, COLS), full),
            pltpu.VMEM((3, ROWS, 384), half),
            pltpu.VMEM((3, ROWS, 384), half),
            dma((4,)), dma((14,)), dma((16,)), dma(()), dma(()), dma((2,)), dma((2,)), dma((2,)),
            dma((8,)), dma((8,)), dma((8, 3)), dma((8, 3)), dma((3, 4)), dma((3, 4)),
            dma((28,)), dma((32,)), dma((28,)), dma((32,)),
            dma((32,)), dma((32,)), dma((14,)), dma((16,)),
            dma((3,)), dma((3,)),
        ],
        name="muon",
        compiler_params=pltpu.CompilerParams(
            collective_id=0, has_side_effects=True, vmem_limit_bytes=52 * 2**20
        ),
    )(gradient, momentum)
    new_momentum = MOMENTUM_RATE * momentum + gradient
    nesterov = gradient + MOMENTUM_RATE * new_momentum
    return new_momentum, SCALE * (COEF_A * nesterov + product)


def solution(mesh):
    specs = (P("row", "col"), P("row", "col"))
    return jax.shard_map(local, mesh=mesh, in_specs=specs, out_specs=specs, check_vma=False)
```

```python
import math

import jax
import jax.numpy as jnp
from jax import lax
from jax.experimental import pallas as pl
from jax.experimental.pallas import tpu as pltpu
from jax.sharding import PartitionSpec as P

HIDDEN_SIZE = 9216
MOMENTUM_RATE = 0.95
COEF_A = 3.4445
COEF_B = -4.775
COEF_C = 2.0315
SCALE = math.sqrt(HIDDEN_SIZE)

MESH = pl.DeviceIdType.MESH
ROWS = 320
COLS = 1152
HALF = ROWS // 2
CHIP = 2 * ROWS
PIECE = ROWS // 4
RELAY = {(1, 0): -1, (1, -1): -1, (1, 1): -1, (0, 2): 1, (1, 2): 1}
PLACES = {(0, 0): 0, (-1, 0): 1, (1, 0): 2, (2, 0): 3, (0, 1): 4, (-1, 1): 5, (1, 1): 6, (2, 1): 7}


class Gather:
    def __init__(self, slot, plus, minus, pair, send, recv, mode, parts=2, hold=False):
        self.slot, self.plus, self.minus, self.pair = slot, plus, minus, pair
        self.send, self.recv, self.mode = send, recv, mode
        self.parts, self.hold, self.started = parts, hold, []

    def _copy(self, dr, dp, h, to):
        device, ring, other = {"plus": (self.plus, -1, 0), "minus": (self.minus, 1, 0), "pair": (self.pair, 0, 1)}[to]
        there = dr + ring
        there = 2 if there == -2 else there
        place = PLACES[(there, (dp + other) % 2)] * self.parts + h
        ref = self.slot(dr, dp, h)
        copy = pltpu.make_async_remote_copy(
            src_ref=ref,
            dst_ref=ref,
            send_sem=self.send.at[len(self.started)],
            recv_sem=self.recv.at[place],
            device_id=device,
            device_id_type=MESH,
        )
        copy.start()
        self.started.append(copy)

    def begin(self, h, links=("plus", "minus", "pair")):
        for to in links:
            self._copy(0, 0, h, to)

    def spread(self, h):
        if self.mode != "cross" or h % 2 == 1:
            self._copy(0, 1, h, "plus")
        if self.mode != "cross" or h % 2 == 0:
            self._copy(0, 1, h, "minus")

    def pass_far(self, h):
        self._copy(2, 0, h, "pair")

    def arrive(self, dr, dp, h):
        ref = self.slot(dr, dp, h)
        place = PLACES[(dr, dp)] * self.parts + h
        pltpu.make_async_remote_copy(
            src_ref=ref,
            dst_ref=ref,
            send_sem=self.send.at[0],
            recv_sem=self.recv.at[place],
            device_id=self.pair,
            device_id_type=MESH,
        ).wait_recv()
        if (dr, dp) == (0, 1):
            if not self.hold:
                self.spread(h)
        elif (dr, h % 2) in ((-1, 0), (1, 1)) and (dp == 0 or self.mode != "late"):
            self._copy(dr, dp, h, "plus" if dr == -1 else "minus")
            if self.mode == "cross" and dp == 0:
                self._copy(dr, dp, h, "pair")

    def finish(self):
        for copy in self.started:
            copy.wait_send()


def kernel(
    g_hbm, m_hbm, out_ref,
    g_ref, m_ref, xs, xi, xq, xt, ps, rl, mg, r1, keep, s_send, s_recv, gf, sq, rt, ls, ms, mt, zs, zb, zr,
    in_sem, x_send, x_recv, xc_send, xc_recv, xq_send, xq_recv, xq_sem, rl_send, rl_recv, r1_send, r1_recv, r2_send, r2_recv,
    rt_send, rt_recv, l_send, l_recv, lc_send, lc_recv, m_send, m_recv, z_send, z_recv,
):
    row, col = lax.axis_index("row"), lax.axis_index("col")
    c, x, yl = row % 2, (row // 2) % 4, row // 8
    z, yh = col % 4, col // 4

    def device(x_, yl_, c_, yh_, z_):
        return ((yl_ * 4 + x_) * 2 + c_, yh_ * 4 + z_)

    core = device(x, yl, 1 - c, yh, z)
    xp, xm = device((x + 1) % 4, yl, c, yh, z), device((x + 3) % 4, yl, c, yh, z)
    zp, zm = device(x, yl, c, yh, (z + 1) % 4), device(x, yl, c, yh, (z + 3) % 4)
    z2 = device(x, yl, c, yh, (z + 2) % 4)
    yp, yq = device(x, 1 - yl, c, yh, z), device(x, yl, c, 1 - yh, z)
    yd = device(x, 1 - yl, c, 1 - yh, z)
    barrier = pltpu.get_barrier_semaphore()
    partners = (core, xp, xm, zp, zm, z2, yp, yq, yd)
    loads = []
    for h in range(2):
        rows = pl.ds(h * HALF, HALF)
        for k, (hbm, ref) in enumerate(((g_hbm, g_ref), (m_hbm, m_ref))):
            load = pltpu.make_async_copy(hbm.at[rows], ref.at[rows], in_sem.at[2 * h + k])
            load.start()
            loads.append(load)
    for partner in partners:
        pl.semaphore_signal(barrier, inc=1, device_id=partner, device_id_type=MESH)

    def remote(src, dst, send, recv, to):
        return pltpu.make_async_remote_copy(
            src_ref=src, dst_ref=dst, send_sem=send, recv_sem=recv, device_id=to, device_id_type=MESH
        )

    def chip_at(dr, dp):
        return ((yl + dp) % 2) * 4 + (x + dr + 4) % 4

    own = chip_at(0, 0)

    gx = Gather(lambda dr, dp, h: xs.at[chip_at(dr, dp), pl.ds(h * HALF, HALF)], xp, xm, yp, x_send, x_recv, "late", hold=True)
    mine = pl.ds(pl.multiple_of(c * ROWS, 32), ROWS)
    theirs = pl.ds(pl.multiple_of((1 - c) * ROWS, 32), ROWS)
    for h in range(2):
        rows = pl.ds(h * HALF, HALF)
        loads[2 * h].wait()
        loads[2 * h + 1].wait()
        new = MOMENTUM_RATE * m_ref[rows, :] + g_ref[rows, :]
        low = (g_ref[rows, :] + MOMENTUM_RATE * new).astype(jnp.bfloat16)
        xs[own, rows, :] = low
        if h == 0:
            pl.semaphore_wait(barrier, len(partners))
            gx.begin(0, ("plus", "pair"))
        else:
            gx.begin(1, ("minus", "plus", "pair"))
            gx.begin(0, ("minus",))
        xi[pl.ds(pl.multiple_of(c * ROWS + h * HALF, 32), HALF), :] = low
    swap = remote(xi.at[mine], xi.at[mine], xc_send, xc_recv, core)
    swap.start()
    remote(xi.at[theirs], xi.at[theirs], xc_send, xc_recv, core).wait_recv()
    for k in range(COLS // 128):
        xt[0, k * 128 : (k + 1) * 128, :] = xi[:, k * 128 : (k + 1) * 128].T

    def block_of(i, dr):
        return i * 4 + (x + dr + 4) % 4

    def piece_copy(block, dz, src=None):
        src = ps.at[block, (z + dz) % 4] if src is None else src
        k = dz - 1
        return remote(src, r1.at[block, k], r1_send.at[block, k], r1_recv.at[block, k], (zp, z2, zm)[k])

    def relay_copy(i, dr):
        block = block_of(i, dr)
        to = zp if RELAY[(i, dr)] == 1 else zm
        return remote(ps.at[block, (z + 2) % 4], rl.at[block], rl_send.at[block], rl_recv.at[block], to)

    def pieces_of(i, dr):
        block = block_of(i, dr)
        if (i, dr) not in RELAY:
            return [(dz, piece_copy(block, dz)) for dz in (2, 1, 3)]
        back = 4 - RELAY[(i, dr)] if RELAY[(i, dr)] == 1 else 1
        return [(2, relay_copy(i, dr)), (back, piece_copy(block, back))]

    def gram(i, dr, h):
        j, block = chip_at(dr, 0), block_of(i, dr)
        part = jnp.dot(xs[j, h * HALF : (h + 1) * HALF, :], xt[i], preferred_element_type=jnp.float32)
        ps[block, 2 * h : 2 * h + 2] = part.astype(jnp.bfloat16).reshape(2, PIECE, CHIP)
        for dz, copy in pieces_of(i, dr):

            @pl.when((z + dz) % 4 // 2 == h)
            def _(copy=copy):
                copy.start()

    def onward(i, dr):
        block, dz = block_of(i, dr), RELAY[(i, dr)] % 4
        return piece_copy(block, dz, mg.at[block])

    def relay(i, dr):
        block = block_of(i, dr)
        relay_copy(i, dr).wait_recv()
        total = rl[block].astype(jnp.float32) + ps[block, (z + RELAY[(i, dr)] + 4) % 4].astype(jnp.float32)
        mg[block] = total.astype(jnp.bfloat16)
        onward(i, dr).start()

    def sum_copy(i, xj, slot):
        to = (yq, yp, yd)[slot]
        return remote(s_send.at[i, xj], s_recv.at[slot, xj], r2_send.at[slot, xj], r2_recv.at[slot, xj], to)

    def reduce(i, dr):
        block = block_of(i, dr)
        total = ps[block, z].astype(jnp.float32)
        for dz in (1, 3) if (i, dr) in RELAY else (1, 3, 2):
            piece_copy(block, dz).wait_recv()
            total = total + r1[block, dz - 1].astype(jnp.float32)
        xj = (x + dr + 4) % 4
        s_send[i, xj] = total.astype(jnp.bfloat16)
        if i == 0:
            keep[xj] = total
            sum_copy(0, xj, 0).start()
        else:
            sum_copy(1, xj, 1).start()
            sum_copy(1, xj, 2).start()

    def pass_pair(h):
        rows = pl.ds(h * HALF, HALF)
        src = xs.at[chip_at(0, 1), rows]
        over = remote(src, xq.at[c, rows], xq_send.at[h], xq_recv.at[h], core)
        over.start()
        here = pltpu.make_async_copy(src, xq.at[c, rows], xq_sem.at[h])
        here.start()
        return over, here

    def row_block(dr, dp, k):
        at, side = (x + dr + 4) % 4, (yl + dp + k // 2) % 2
        return side, (at + 2 * (k % 2) + 3 * ((at + yh) % 2)) % 4

    def row_slot(dr, dp, k):
        side, xj = row_block(dr, dp, k)
        return rt.at[chip_at(dr, dp), side * 2 + xj // 2]

    gr = Gather(row_slot, xp, xm, yp, rt_send, rt_recv, "cross", 4)
    parts = ((0, 0), (0, -1), (0, 1), (1, 0), (1, -1), (0, 2), (1, 1), (1, 2))
    lanes, l_sent = [], []

    def l_slot(n, dz, lane):
        i, dr = parts[n]
        return ls.at[chip_at(dr, i), lane, (z + dz + 4) % 4]

    def l_copy(n, dz, side):
        there = {(0, 1): -1, (0, -1): 1, (-1, 1): 2, (1, -1): 2}[(dz, side)]
        ref = l_slot(n, dz, c)
        to = zp if side == 1 else zm
        copy = remote(ref, ref, l_send.at[len(l_sent)], l_recv.at[(there % 4) * 8 + n], to)
        copy.start()
        l_sent.append(copy)

    def to_core(n, dz):
        place = (dz % 4) * 8 + n
        copy = remote(l_slot(n, dz, c), l_slot(n, dz, c), lc_send.at[place], lc_recv.at[place], core)
        copy.start()
        lanes.append(copy)

    def from_core(n, dz):
        place = (dz % 4) * 8 + n
        ref = l_slot(n, dz, 1 - c)
        remote(ref, ref, lc_send.at[place], lc_recv.at[place], core).wait_recv()

    def l_arrive(n, dz):
        ref = l_slot(n, dz, c)
        remote(ref, ref, l_send.at[0], l_recv.at[(dz % 4) * 8 + n], zp).wait_recv()
        if dz == -1 and n % 2 == 0:
            l_copy(n, -1, 1)
        if dz == 1 and n % 2 == 1:
            l_copy(n, 1, -1)
        to_core(n, dz)

    def finish_sum(n):
        i, dr = parts[n]
        xj, j = (x + dr + 4) % 4, chip_at(dr, i)
        for slot in (1, 2) if i else (0,):
            ref = s_recv.at[slot, xj]
            remote(ref, ref, r2_send.at[slot, xj], r2_recv.at[slot, xj], yp).wait_recv()
        if i:
            total = s_recv[1, xj].astype(jnp.float32) + s_recv[2, xj].astype(jnp.float32)
        else:
            total = keep[xj] + s_recv[0, xj].astype(jnp.float32)
        gf[j] = total
        ls[j, c, z] = total.astype(jnp.bfloat16)
        l_copy(n, 0, 1)
        l_copy(n, 0, -1)
        to_core(n, 0)

    def r_begin(k):
        side, xj = row_block(0, 0, k)
        rt[own, side * 2 + xj // 2] = ls[side * 4 + xj, c, z]
        gr.begin(k)

    def load_pair():
        for h in range(2):
            ref = xq.at[1 - c, pl.ds(h * HALF, HALF)]
            remote(ref, ref, xq_send.at[h], xq_recv.at[h], core).wait_recv()
            passed[h][1].wait()
        for k in range(COLS // 128):
            cols = slice(k * 128, (k + 1) * 128)
            xt[1, cols, :] = xq[:, :, cols].reshape(CHIP, 128).T

    def square(j, rows):
        left = rt[j, rows].reshape(-1, CHIP)
        right = ls[j].reshape(CHIP, CHIP)
        return jnp.dot(left, right, preferred_element_type=jnp.float32)

    def squares(ns, rows):
        return sum(square(chip_at(parts[n][1], parts[n][0]), rows) for n in ns)

    def square_add(n, first=False):
        for dz in (0, -1, 1, 2):
            from_core(n, dz)
        total = squares((n,), slice(None)).reshape(4, PIECE, CHIP)
        sq[...] = total if first else sq[...] + total

    passed = []
    gram(0, 0, 1)
    gx.arrive(1, 0, 1)
    gx.arrive(-1, 0, 0)
    gram(0, -1, 0)
    gx.arrive(0, 1, 0)
    passed.append(pass_pair(0))
    gram(0, 1, 1)
    gram(0, 0, 0)
    gx.arrive(0, 1, 1)
    passed.append(pass_pair(1))
    gx.arrive(-1, 0, 1)
    gram(0, -1, 1)
    gx.spread(1)
    gx.arrive(1, 0, 0)
    gram(0, 1, 0)
    load_pair()
    reduce(0, 0)
    gram(1, -1, 0)
    gram(1, 1, 1)
    gram(1, 0, 1)
    gram(1, -1, 1)
    reduce(0, -1)
    gx.arrive(2, 0, 1)
    gram(1, 1, 0)
    gx.pass_far(1)
    gram(1, 0, 0)
    relay(1, -1)
    reduce(0, 1)
    gx.arrive(2, 0, 0)
    gram(1, 2, 0)
    finish_sum(1)
    relay(1, 0)
    gram(0, 2, 1)
    relay(1, 1)
    gram(1, 2, 1)
    finish_sum(0)
    r_begin(0)
    gram(0, 2, 0)
    reduce(1, -1)
    gr.arrive(-1, 0, 0)
    gx.spread(0)
    relay(1, 2)
    finish_sum(2)
    reduce(1, 0)
    gr.arrive(0, 1, 0)
    reduce(1, 1)
    relay(0, 2)
    reduce(1, 2)
    finish_sum(4)
    finish_sum(3)
    r_begin(2)
    l_arrive(1, -1)
    finish_sum(6)
    l_arrive(2, -1)
    reduce(0, 2)
    l_arrive(4, -1)
    l_arrive(0, -1)
    gr.arrive(-1, 0, 2)
    finish_sum(7)
    r_begin(3)
    l_arrive(0, 1)
    gr.arrive(1, 0, 0)
    finish_sum(5)
    r_begin(1)
    l_arrive(3, 1)
    l_arrive(1, 1)
    l_arrive(2, 1)
    gr.arrive(0, 1, 2)
    l_arrive(3, -1)
    gr.arrive(-1, 1, 0)
    gr.arrive(1, 0, 3)
    l_arrive(6, -1)
    l_arrive(5, 1)
    gr.arrive(0, 1, 1)
    gr.arrive(1, 0, 1)
    l_arrive(7, 1)
    gr.arrive(2, 0, 2)
    gr.arrive(-1, 0, 1)
    gr.arrive(1, 1, 2)
    gr.arrive(-1, 0, 3)
    gx.pass_far(0)
    l_arrive(3, 2)
    l_arrive(4, 2)
    l_arrive(0, 2)
    gr.arrive(1, 1, 3)
    gr.arrive(-1, 1, 2)
    l_arrive(2, 2)
    l_arrive(4, 1)
    l_arrive(1, 2)
    gr.arrive(0, 1, 3)
    gr.arrive(1, 1, 1)
    gr.arrive(2, 0, 0)
    square_add(0, True)
    l_arrive(5, -1)
    square_add(3)
    square_add(1)
    l_arrive(5, 2)
    gr.arrive(2, 1, 0)
    l_arrive(6, 1)
    l_arrive(6, 2)
    gr.arrive(1, 0, 2)
    gr.arrive(1, 1, 0)
    gr.arrive(2, 0, 1)
    gr.arrive(2, 1, 2)
    square_add(2)
    l_arrive(7, 2)
    gr.arrive(2, 1, 3)
    gr.arrive(2, 0, 3)
    l_arrive(7, -1)
    square_add(5)
    gr.arrive(-1, 1, 1)
    gr.arrive(-1, 1, 3)
    square_add(6)
    gr.arrive(2, 1, 1)
    for h in range(2):
        gx.arrive(-1, 1, h)
        gx.arrive(1, 1, h)

    done = (4, 7)
    for n in done:
        for dz in (0, -1, 1, 2):
            from_core(n, dz)

    def mix_slot(dr, dp, h):
        return ms.at[h, :, (yh + dp) % 2, (z + dr + 4) % 4]

    gm = Gather(mix_slot, zp, zm, yq, m_send, m_recv, "cross")
    for h in range(2):
        rows = slice(2 * h, 2 * h + 2)
        total = sq[rows].reshape(HALF, CHIP) + squares(done, rows)
        gram_rows = jnp.concatenate([gf[h * 4 + yh], gf[h * 4 + 2 + yh]], axis=0)
        mixing = (COEF_B * gram_rows + COEF_C * total).astype(jnp.bfloat16)
        ms[h, 0, yh, z] = mixing[:PIECE]
        ms[h, 1, yh, z] = mixing[PIECE:]
        gm.begin(h)

    def turn(dr, dp):
        mt[...] = ms[:, :, (yh + dp) % 2, (z + dr + 4) % 4].reshape(ROWS, CHIP).T

    def product(dr, dp, rows, n, first=False):
        side, at = (yh + dp) % 2, (z + dr + 4) % 4
        cols = pl.ds(n * 384, 384)
        at_rows = pl.ds(pl.multiple_of(at * PIECE, 16), PIECE)
        right = jnp.concatenate([xs[2 * k + side, at_rows, cols] for k in range(4)], axis=0)
        part = jnp.dot(mt[rows, :], right, preferred_element_type=jnp.float32)
        zs[rows, cols] = part if first else zs[rows, cols] + part

    def unit(dr, dp, first=False):
        turn(dr, dp)
        for n in range(3):
            product(dr, dp, every, n, first)

    every = slice(None)
    for h in range(2):
        gm.arrive(-1, 0, h)
        gm.arrive(1, 0, 1 - h)
        gm.arrive(0, 1, h)
    for h in range(2):
        gx.arrive(2, 1, h)
    unit(0, 0, True)
    unit(-1, 0)
    unit(1, 0)
    gm.arrive(-1, 1, 0)
    gm.arrive(1, 1, 1)
    unit(0, 1)
    for h in range(2):
        gm.arrive(2, 0, h)
    unit(2, 0)
    gm.arrive(-1, 1, 1)
    gm.arrive(1, 1, 0)
    unit(-1, 1)
    unit(1, 1)
    for h in range(2):
        gm.arrive(2, 1, h)
    turn(2, 1)
    last = []
    for n in range(3):
        product(2, 1, theirs, n)
        zb[n] = zs[theirs, pl.ds(n * 384, 384)].astype(jnp.bfloat16)
        last.append(remote(zb.at[n], zr.at[n], z_send.at[n], z_recv.at[n], core))
        last[n].start()
    for n in range(3):
        product(2, 1, mine, n)
    for n in range(3):
        last[n].wait_recv()
        cols = pl.ds(n * 384, 384)
        out_ref[:, cols] = zs[mine, cols] + zr[n].astype(jnp.float32)

    for copy in lanes + l_sent + [swap] + last + [over for over, _ in passed]:
        copy.wait_send()
    for gather in (gx, gr, gm):
        gather.finish()
    for place in parts:
        for _, copy in pieces_of(*place):
            copy.wait_send()
        if place in RELAY:
            onward(*place).wait_send()
    for xj in range(4):
        for slot in range(3):
            sum_copy(min(slot, 1), xj, slot).wait_send()


def local(gradient, momentum):
    half, full = jnp.bfloat16, jnp.float32
    dma = pltpu.SemaphoreType.DMA
    product = pl.pallas_call(
        kernel,
        out_shape=jax.ShapeDtypeStruct((ROWS, COLS), full),
        in_specs=[pl.BlockSpec(memory_space=pl.ANY)] * 2,
        out_specs=pl.BlockSpec(memory_space=pltpu.VMEM),
        scratch_shapes=[
            pltpu.VMEM((ROWS, COLS), full),
            pltpu.VMEM((ROWS, COLS), full),
            pltpu.VMEM((8, ROWS, COLS), half),
            pltpu.VMEM((CHIP, COLS), half),
            pltpu.VMEM((2, ROWS, COLS), half),
            pltpu.VMEM((2, COLS, CHIP), half),
            pltpu.VMEM((8, 4, PIECE, CHIP), half),
            pltpu.VMEM((8, PIECE, CHIP), half),
            pltpu.VMEM((8, PIECE, CHIP), half),
            pltpu.VMEM((8, 3, PIECE, CHIP), half),
            pltpu.VMEM((4, PIECE, CHIP), full),
            pltpu.VMEM((2, 4, PIECE, CHIP), half),
            pltpu.VMEM((3, 4, PIECE, CHIP), half),
            pltpu.VMEM((8, PIECE, CHIP), full),
            pltpu.VMEM((4, PIECE, CHIP), full),
            pltpu.VMEM((8, 4, PIECE, CHIP), half),
            pltpu.VMEM((8, 2, 4, PIECE, CHIP), half),
            pltpu.VMEM((2, 2, 2, 4, PIECE, CHIP), half),
            pltpu.VMEM((CHIP, ROWS), half),
            pltpu.VMEM((CHIP, COLS), full),
            pltpu.VMEM((3, ROWS, 384), half),
            pltpu.VMEM((3, ROWS, 384), half),
            dma((4,)), dma((14,)), dma((16,)), dma(()), dma(()), dma((2,)), dma((2,)), dma((2,)),
            dma((8,)), dma((8,)), dma((8, 3)), dma((8, 3)), dma((3, 4)), dma((3, 4)),
            dma((28,)), dma((32,)), dma((28,)), dma((32,)),
            dma((32,)), dma((32,)), dma((14,)), dma((16,)),
            dma((3,)), dma((3,)),
        ],
        name="muon",
        compiler_params=pltpu.CompilerParams(
            collective_id=0, has_side_effects=True, vmem_limit_bytes=52 * 2**20
        ),
    )(gradient, momentum)
    new_momentum = MOMENTUM_RATE * momentum + gradient
    nesterov = gradient + MOMENTUM_RATE * new_momentum
    return new_momentum, SCALE * (COEF_A * nesterov + product)


def solution(mesh):
    specs = (P("row", "col"), P("row", "col"))
    return jax.shard_map(local, mesh=mesh, in_specs=specs, out_specs=specs, check_vma=False)
```
